32 devices in a mesh: dp: 16 (over z, y, core), tensor: 2 (over x).
Axes of the slice: x: 2, y: 2, z: 4, core: 2. Of those that a mesh axis runs over, the one named last changes fastest.
Arguments:
- tokens: bfloat16 [12800, 512], P('dp'), may hold values from -6 to 6
- memory: bfloat16 [131072, 512], P('dp'), may hold values from -6 to 6
- mem_lengths: int32 [32, 4], P('dp'), may hold values from 1 to 1200, 4096 in all within a row
- key_pad: int32 [32, 4096], P('dp'), may hold values 0 or 1
- query_embed: float32 [100, 512], replicated, may hold values from -5 to 5
- self_wq: bfloat16 [512, 512], P(None, 'tensor'), may hold values from -0.25 to 0.25
- self_bq: float32 [512], P('tensor'), may hold values from -3 to 3
- self_wk: bfloat16 [512, 512], P(None, 'tensor'), may hold values from -0.25 to 0.25
- self_wv: bfloat16 [512, 512], P(None, 'tensor'), may hold values from -0.25 to 0.25
- self_bv: float32 [512], P('tensor'), may hold values from -3 to 3
- self_wo: bfloat16 [512, 512], P('tensor'), may hold values from -0.5 to 0.5
- self_bo: float32 [512], replicated, may hold values from -3 to 3
- norm1_gain: float32 [512], replicated, may hold values from 0.5 to 1.5
- norm1_bias: float32 [512], replicated, may hold values from -2 to 2
- cross_wq: bfloat16 [512, 512], P(None, 'tensor'), may hold values from -0.25 to 0.25
- cross_bq: float32 [512], P('tensor'), may hold values from -3 to 3
- cross_wk: bfloat16 [512, 512], P(None, 'tensor'), may hold values from -0.25 to 0.25
- cross_wv: bfloat16 [512, 512], P(None, 'tensor'), may hold values from -0.25 to 0.25
- cross_bv: float32 [512], P('tensor'), may hold values from -3 to 3
- cross_wo: bfloat16 [512, 512], P('tensor'), may hold values from -1 to 1
- cross_bo: float32 [512], replicated, may hold values from -3 to 3
- norm2_gain: float32 [512], replicated, may hold values from 0.5 to 1.5
- norm2_bias: float32 [512], replicated, may hold values from -2 to 2
- ffn_w1: bfloat16 [512, 3200], P(None, 'tensor'), may hold values from -0.25 to 0.25
- ffn_b1: float32 [3200], P('tensor'), may hold values from -3 to 3
- ffn_w2: bfloat16 [3200, 512], P('tensor'), may hold values from -0.109375 to 0.109375
- ffn_b2: float32 [512], replicated, may hold values from -3 to 3
- norm3_gain: float32 [512], replicated, may hold values from 0.5 to 1.5
- norm3_bias: float32 [512], replicated, may hold values from -2 to 2
- cotangent: bfloat16 [12800, 512], P('dp'), may hold values from -6 to 6
Outputs:
- layer_out: bfloat16 [12800, 512], P('dp')
- grad_tokens: float32 [12800, 512], P('dp')
- grad_memory: float32 [131072, 512], P('dp')
- grad_query_embed: float32 [100, 512], replicated
- grad_self_wq: float32 [512, 512], P(None, 'tensor')
- grad_self_bq: float32 [512], P('tensor')
- grad_self_wk: float32 [512, 512], P(None, 'tensor')
- grad_self_wv: float32 [512, 512], P(None, 'tensor')
- grad_self_bv: float32 [512], P('tensor')
- grad_self_wo: float32 [512, 512], P('tensor')
- grad_self_bo: float32 [512], replicated
- grad_norm1_gain: float32 [512], replicated
- grad_norm1_bias: float32 [512], replicated
- grad_cross_wq: float32 [512, 512], P(None, 'tensor')
- grad_cross_bq: float32 [512], P('tensor')
- grad_cross_wk: float32 [512, 512], P(None, 'tensor')
- grad_cross_wv: float32 [512, 512], P(None, 'tensor')
- grad_cross_bv: float32 [512], P('tensor')
- grad_cross_wo: float32 [512, 512], P('tensor')
- grad_cross_bo: float32 [512], replicated
- grad_norm2_gain: float32 [512], replicated
- grad_norm2_bias: float32 [512], replicated
- grad_ffn_w1: float32 [512, 3200], P(None, 'tensor')
- grad_ffn_b1: float32 [3200], P('tensor')
- grad_ffn_w2: float32 [3200, 512], P('tensor')
- grad_ffn_b2: float32 [512], replicated
- grad_norm3_gain: float32 [512], replicated
- grad_norm3_bias: float32 [512], replicated
The draws below stay inside these ranges and needn't reach their ends.
Inputs may be any that keep to these rules, and one draw needn't show every extreme that they name: `mem_lengths`: the 4 lengths of a row sum to 4096.
All inputs are finite; a program needn't handle non-finite values. No bound on the sum of `key_pad` on one device may be relied on, other than what follows from the above.
Results may differ from the reference program's by a relative error of at most 0.028.
The reference program's roundings to bfloat16 on the way (of `shared_in`, `self_probs`, `self_mix`, `cross_mix` and `hidden`) count: a program that leaves them out, or rounds other values in their place, can miss the bound.
Values may be sent and summed in bfloat16 or wider, within the bound.
No kernel may reach another device: no remote copies, remote signals or barrier semaphores. Data moves between devices by JAX's collectives and lax.ppermute only.
A program may use at most 256 MiB of HBM per device.

```python
import math
import jax
import jax.numpy as jnp
import numpy as np
from jax import lax

D = 512
H = 8
HEAD = 64
FF = 3200
SPAN = 100
MEM_MOST = 1200
ITEMS_ROW = 4
MEM_ROW = 4096
Q_ROW = 400
ROWS = 32
TOKENS = 12800
MEMTOK = 131072


def place_ends(drawn, key, smallest, high):
    longest = drawn.shape.index(max(drawn.shape))
    spots = []
    for shift in (0, 1):
        where = [jax.random.randint(jax.random.fold_in(key, axis), (), 0, length) for axis, length in enumerate(drawn.shape)]
        where[longest] = (where[longest] + shift) % drawn.shape[longest]
        spots.append(tuple(where))
    return drawn.at[spots[0]].set(smallest).at[spots[1]].set(high)


def steps_of(own_key, extent, cuts, low, high):
    level = 1.0
    for position, blocks in cuts:
        heights = jax.random.uniform(jax.random.fold_in(jax.random.fold_in(own_key, 6), position), (blocks,), jnp.float32, low / len(cuts), high / len(cuts))
        level = level * jnp.repeat(jnp.exp(heights), extent[position] // blocks).reshape((-1,) + (1,) * (len(extent) - 1 - position))
    return level


def profile(amount, total, most, skew):
    loads = [(1 << 20) // math.isqrt(grade ** skew) + 1 for grade in range(2, amount + 1)]
    rest, counts = total - most - (amount - 1), [1] * (amount - 1)
    while rest > 0:
        movable = [i for i in range(amount - 1) if counts[i] < most]
        pool, budget = sum([loads[i] for i in movable]), rest
        for i in movable:
            more = min(most - counts[i], max(1, budget * loads[i] // pool), rest)
            counts[i] = counts[i] + more
            rest = rest - more
    return np.array([most] + counts)


def ragged(rng, amount, total, limit, lean):
    if amount == 2:
        one = jax.random.randint(rng, (), max(1, total - limit), min(limit, total - 1) + 1)
        return jnp.stack([one, total - one])
    sizes = jnp.asarray(profile(amount, total, limit, lean), jnp.int32)
    twos = (amount - 1) // 2
    source_of, receiver = sizes[1:1 + 2 * twos:2], sizes[2:2 + 2 * twos:2]
    slack = jnp.minimum(source_of - 1, limit - receiver)
    moved = jax.random.randint(jax.random.fold_in(rng, 1), (twos,), 0, 1 << 20) % (slack + 1)
    sizes = sizes.at[1:1 + 2 * twos:2].set(source_of - moved).at[2:2 + 2 * twos:2].set(receiver + moved)
    return sizes[jax.random.permutation(jax.random.fold_in(rng, 2), amount)]


def scatter_about(own_key, extent, scale, reach, cuts=(), held_as=jnp.bfloat16):
    result = scale * jax.random.normal(own_key, extent, jnp.float32)
    if cuts:
        result = result * steps_of(own_key, extent, cuts, -0.22, 0.18)
    return jnp.clip(result, -reach, reach).astype(held_as)


def setup_inputs(seed: int = 0) -> dict:
    key_list = jax.random.split(jax.random.key(seed), 31)
    tokens = scatter_about(key_list[0], (TOKENS, D), 1.0, 6.0, ((0, 16),))
    memory = scatter_about(key_list[1], (MEMTOK, D), 1.0, 6.0, ((0, 16),))
    mem_lengths = jax.vmap(lambda own: ragged(own, ITEMS_ROW, MEM_ROW, MEM_MOST, 1))(jax.random.split(key_list[2], ROWS)).reshape((ROWS, ITEMS_ROW)).astype(jnp.int32)
    key_pad = place_ends((jax.random.randint(key_list[3], (ROWS, MEM_ROW), 0, 8) < 7).astype(jnp.int32), jax.random.fold_in(key_list[3], 1), 0, 1)
    query_embed = scatter_about(key_list[4], (SPAN, D), 1.0, 5.0, (), jnp.float32)
    self_wq = scatter_about(key_list[5], (D, D), D ** -0.5, 0.25, ((1, 2),))
    self_bq = scatter_about(key_list[6], (D,), 0.5, 3.0, ((0, 2),), jnp.float32)
    self_wk = scatter_about(key_list[7], (D, D), D ** -0.5, 0.25, ((1, 2),))
    self_wv = scatter_about(key_list[8], (D, D), D ** -0.5, 0.25, ((1, 2),))
    self_bv = scatter_about(key_list[9], (D,), 0.5, 3.0, ((0, 2),), jnp.float32)
    self_wo = scatter_about(key_list[10], (D, D), (D // 4) ** -0.5, 0.5, ((0, 2),))
    self_bo = scatter_about(key_list[11], (D,), 0.5, 3.0, (), jnp.float32)
    norm1_gain = jnp.clip(1.0 + 0.1 * jax.random.normal(key_list[12], (D,), jnp.float32), 0.5, 1.5)
    norm1_bias = scatter_about(key_list[13], (D,), 0.3, 2.0, (), jnp.float32)
    cross_wq = scatter_about(key_list[14], (D, D), D ** -0.5, 0.25, ((1, 2),))
    cross_bq = scatter_about(key_list[15], (D,), 0.5, 3.0, ((0, 2),), jnp.float32)
    cross_wk = scatter_about(key_list[16], (D, D), D ** -0.5, 0.25, ((1, 2),))
    cross_wv = scatter_about(key_list[17], (D, D), D ** -0.5, 0.25, ((1, 2),))
    cross_bv = scatter_about(key_list[18], (D,), 0.5, 3.0, ((0, 2),), jnp.float32)
    cross_wo = scatter_about(key_list[19], (D, D), (D // 16) ** -0.5, 1.0, ((0, 2),))
    cross_bo = scatter_about(key_list[20], (D,), 0.5, 3.0, (), jnp.float32)
    norm2_gain = jnp.clip(1.0 + 0.1 * jax.random.normal(key_list[21], (D,), jnp.float32), 0.5, 1.5)
    norm2_bias = scatter_about(key_list[22], (D,), 0.3, 2.0, (), jnp.float32)
    ffn_w1 = scatter_about(key_list[23], (D, FF), D ** -0.5, 0.25, ((1, 2),))
    ffn_b1 = scatter_about(key_list[24], (FF,), 0.5, 3.0, ((0, 2),), jnp.float32)
    ffn_w2 = scatter_about(key_list[25], (FF, D), FF ** -0.5, 0.109375, ((0, 2),))
    ffn_b2 = scatter_about(key_list[26], (D,), 0.5, 3.0, (), jnp.float32)
    norm3_gain = jnp.clip(1.0 + 0.1 * jax.random.normal(key_list[27], (D,), jnp.float32), 0.5, 1.5)
    norm3_bias = scatter_about(key_list[28], (D,), 0.3, 2.0, (), jnp.float32)
    cotangent = scatter_about(key_list[29], (TOKENS, D), 1.0, 6.0, ((0, 16),))
    return dict(tokens=tokens, memory=memory, mem_lengths=mem_lengths, key_pad=key_pad, query_embed=query_embed, self_wq=self_wq, self_bq=self_bq, self_wk=self_wk, self_wv=self_wv, self_bv=self_bv, self_wo=self_wo, self_bo=self_bo, norm1_gain=norm1_gain, norm1_bias=norm1_bias, cross_wq=cross_wq, cross_bq=cross_bq, cross_wk=cross_wk, cross_wv=cross_wv, cross_bv=cross_bv, cross_wo=cross_wo, cross_bo=cross_bo, norm2_gain=norm2_gain, norm2_bias=norm2_bias, ffn_w1=ffn_w1, ffn_b1=ffn_b1, ffn_w2=ffn_w2, ffn_b2=ffn_b2, norm3_gain=norm3_gain, norm3_bias=norm3_bias, cotangent=cotangent)


@jax.custom_vjp
def low(v):
    return lax.optimization_barrier(v.astype(jnp.bfloat16)).astype(jnp.float32)

@jax.custom_vjp
def low_back(v):
    return v

def low_keep(v):
    return (low(v), None)

def low_pass(kept, grad):
    return (grad,)

def back_keep(v):
    return (v, None)

def back_low(kept, grad):
    return (low(grad),)
low.defvjp(low_keep, low_pass)
low_back.defvjp(back_keep, back_low)

def round_both(value_in):
    return low(low_back(value_in))

def highest_dot(left, right):
    return jnp.dot(left, right, precision=lax.Precision.HIGHEST)

def layer_norm(value_in, norm_gain, norm_shift):
    center = value_in - lax.optimization_barrier(jnp.mean(value_in, axis=-1, keepdims=True))
    spread = lax.optimization_barrier(jnp.mean(center * center, axis=-1, keepdims=True))
    return center * lax.rsqrt(spread + 1e-05) * norm_gain + norm_shift

def smooth_act(pre_act):
    return 0.5 * pre_act * (1.0 + jnp.tanh(math.sqrt(2.0 / math.pi) * (pre_act + 0.044715 * pre_act * pre_act * pre_act)))

def softmax_rows(scores):
    largest = lax.optimization_barrier(jnp.max(scores, axis=-1, keepdims=True))
    expo_terms = jnp.exp(scores - largest)
    return expo_terms / lax.optimization_barrier(jnp.sum(expo_terms, axis=-1, keepdims=True))

def memory_layout(lengths_row, slot_count):
    item_ends = jnp.cumsum(lengths_row).astype(jnp.int32)
    starts = (item_ends - lengths_row).astype(jnp.int32)
    slot_index = jnp.arange(slot_count, dtype=jnp.int32)
    slot_owner = lax.optimization_barrier(jnp.sum((slot_index[:, None] >= item_ends[None, :]).astype(jnp.int32), axis=1)).astype(jnp.int32)
    chosen = slot_owner[:, None] == jnp.arange(lengths_row.shape[0], dtype=jnp.int32)[None, :]
    start_of = lax.optimization_barrier(jnp.sum(jnp.where(chosen, starts[None, :], 0), axis=1)).astype(jnp.int32)
    return (slot_owner, slot_index - start_of)

def cross_allowed(lengths_row, pad_row, query_count):
    slot_owner, slot_place = memory_layout(lengths_row, pad_row.shape[0])
    is_valid = (pad_row > 0) | (slot_place == 0)
    query_item = jnp.arange(query_count, dtype=jnp.int32) // SPAN
    return (query_item[:, None] == slot_owner[None, :]) & is_valid[None, :]

def sinusoid(places, feature_dim):
    freq_index = jnp.arange(feature_dim // 2, dtype=jnp.float32)
    freq_rates = jnp.exp(freq_index * (-2.0 * math.log(10000.0) / feature_dim))
    angles = places.astype(jnp.float32)[:, None] * freq_rates[None, :]
    return jnp.stack([jnp.sin(angles), jnp.cos(angles)], axis=-1).reshape(places.shape[0], feature_dim)

def decoder_row(params, row_data):
    query_embed, self_wq, self_bq, self_wk, self_wv, self_bv, self_wo, self_bo, norm1_gain, norm1_bias, cross_wq, cross_bq, cross_wk, cross_wv, cross_bv, cross_wo, cross_bo, norm2_gain, norm2_bias, ffn_w1, ffn_b1, ffn_w2, ffn_b2, norm3_gain, norm3_bias = params
    tokens_row, memory_row, lengths_row, pad_row = row_data
    query_pos = jnp.tile(query_embed, (ITEMS_ROW, 1))
    shared_in = low(tokens_row + query_pos)
    self_query = round_both(highest_dot(shared_in, self_wq) + self_bq).reshape(ITEMS_ROW, SPAN, H, HEAD)
    self_keys = round_both(highest_dot(shared_in, self_wk)).reshape(ITEMS_ROW, SPAN, H, HEAD)
    self_values = round_both(highest_dot(tokens_row, self_wv) + self_bv).reshape(ITEMS_ROW, SPAN, H, HEAD)
    self_scores = low_back(jnp.einsum('iqhe,ikhe->ihqk', self_query, self_keys, precision=lax.Precision.HIGHEST) / math.sqrt(HEAD))
    self_probs = low(softmax_rows(self_scores))
    self_mix = round_both(jnp.einsum('ihqk,ikhe->iqhe', self_probs, self_values, precision=lax.Precision.HIGHEST)).reshape(Q_ROW, D)
    normed_one = layer_norm(tokens_row + low_back(highest_dot(self_mix, self_wo) + self_bo), norm1_gain, norm1_bias)
    slot_owner, slot_place = memory_layout(lengths_row, MEM_ROW)
    memory_pos = sinusoid(slot_place, D)
    allowed = cross_allowed(lengths_row, pad_row, Q_ROW)
    cross_in = low(normed_one + query_pos)
    memory_in = low(memory_row + memory_pos)
    cross_query = round_both(highest_dot(cross_in, cross_wq) + cross_bq).reshape(Q_ROW, H, HEAD)
    cross_keys = round_both(highest_dot(memory_in, cross_wk)).reshape(MEM_ROW, H, HEAD)
    cross_values = round_both(highest_dot(memory_row, cross_wv) + cross_bv).reshape(MEM_ROW, H, HEAD)
    cross_scores = low_back(jnp.einsum('qhe,khe->hqk', cross_query, cross_keys, precision=lax.Precision.HIGHEST) / math.sqrt(HEAD))
    cross_scores = jnp.where(allowed[None], cross_scores, -1000000000.0)
    cross_probs = low(softmax_rows(cross_scores))
    cross_mix = round_both(jnp.einsum('hqk,khe->qhe', cross_probs, cross_values, precision=lax.Precision.HIGHEST)).reshape(Q_ROW, D)
    normed_two = layer_norm(normed_one + low_back(highest_dot(cross_mix, cross_wo) + cross_bo), norm2_gain, norm2_bias)
    hidden = low(smooth_act(low_back(highest_dot(low(normed_two), ffn_w1) + ffn_b1)))
    return layer_norm(normed_two + low_back(highest_dot(hidden, ffn_w2) + ffn_b2), norm3_gain, norm3_bias)

def reference(tokens, memory, mem_lengths, key_pad, query_embed, self_wq, self_bq, self_wk, self_wv, self_bv, self_wo, self_bo, norm1_gain, norm1_bias, cross_wq, cross_bq, cross_wk, cross_wv, cross_bv, cross_wo, cross_bo, norm2_gain, norm2_bias, ffn_w1, ffn_b1, ffn_w2, ffn_b2, norm3_gain, norm3_bias, cotangent):
    params = tuple((weight.astype(jnp.float32) for weight in (query_embed, self_wq, self_bq, self_wk, self_wv, self_bv, self_wo, self_bo, norm1_gain, norm1_bias, cross_wq, cross_bq, cross_wk, cross_wv, cross_bv, cross_wo, cross_bo, norm2_gain, norm2_bias, ffn_w1, ffn_b1, ffn_w2, ffn_b2, norm3_gain, norm3_bias)))
    tokens_rows = tokens.astype(jnp.float32).reshape(ROWS, Q_ROW, D)
    memory_rows = memory.astype(jnp.float32).reshape(ROWS, MEM_ROW, D)

    def forward(params_in, tokens_in, memory_in):

        def one_row(row_data):
            return decoder_row(params_in, row_data)
        return lax.map(jax.checkpoint(one_row), (tokens_in, memory_in, mem_lengths, key_pad))
    layer_rows, pull_back = jax.vjp(forward, params, tokens_rows, memory_rows)
    grad_params, grad_tokens, grad_memory = pull_back(cotangent.astype(jnp.float32).reshape(ROWS, Q_ROW, D))
    grad_query_embed, grad_self_wq, grad_self_bq, grad_self_wk, grad_self_wv, grad_self_bv, grad_self_wo, grad_self_bo, grad_norm1_gain, grad_norm1_bias, grad_cross_wq, grad_cross_bq, grad_cross_wk, grad_cross_wv, grad_cross_bv, grad_cross_wo, grad_cross_bo, grad_norm2_gain, grad_norm2_bias, grad_ffn_w1, grad_ffn_b1, grad_ffn_w2, grad_ffn_b2, grad_norm3_gain, grad_norm3_bias = grad_params
    return (layer_rows.reshape(TOKENS, D).astype(jnp.bfloat16), grad_tokens.reshape(TOKENS, D), grad_memory.reshape(MEMTOK, D), grad_query_embed, grad_self_wq, grad_self_bq, grad_self_wk, grad_self_wv, grad_self_bv, grad_self_wo, grad_self_bo, grad_norm1_gain, grad_norm1_bias, grad_cross_wq, grad_cross_bq, grad_cross_wk, grad_cross_wv, grad_cross_bv, grad_cross_wo, grad_cross_bo, grad_norm2_gain, grad_norm2_bias, grad_ffn_w1, grad_ffn_b1, grad_ffn_w2, grad_ffn_b2, grad_norm3_gain, grad_norm3_bias)
```

```python
import functools
import math

import jax
import jax.numpy as jnp
import numpy as np
from jax import lax
from jax.experimental import pallas as pl
from jax.experimental.pallas import tpu as pltpu
from jax.sharding import PartitionSpec as P

HEAD = 64
SPAN = 100
LANES = 128
PAIR = 2 * HEAD
TILE = 256
FAR = -1.0e9
BF = jnp.bfloat16
F32 = jnp.float32


def mm(left, right):
    return jnp.dot(left, right, preferred_element_type=F32)


def mm_tn(left, right):
    return lax.dot_general(left, right, (((0,), (0,)), ((), ())), preferred_element_type=F32)


def mm_nt(left, right):
    return lax.dot_general(left, right, (((1,), (1,)), ((), ())), preferred_element_type=F32)


def split3(value):
    top = value.astype(BF)
    rest = value - top.astype(F32)
    middle = rest.astype(BF)
    return top, middle, (rest - middle.astype(F32)).astype(BF)


def iota(shape, dim):
    return lax.broadcasted_iota(jnp.int32, shape, dim)


def keys_values_kernel(
    first_ref, last_ref, starts_ref, ends_ref,
    memory_ref, pad_ref, bounds_ref, sin_ref, cos_ref, local_sin_ref, local_cos_ref, wk_ref, wv_ref, bv_ref,
    memory_in_ref, keys_ref, values_ref, gate_ref,
):
    tiles = pl.num_programs(1)
    row, tile = pl.program_id(0), pl.program_id(1)
    step = row * tiles + tile
    base = tile * TILE
    memory = memory_ref[...]
    local_sin, local_cos = local_sin_ref[...], local_cos_ref[...]
    slots = iota((TILE, 1), 0) + base

    def place(item):
        return sin_ref[0, pl.ds(item, 1), :] * local_cos + cos_ref[0, pl.ds(item, 1), :] * local_sin

    def later(item, held):
        return jnp.where(slots >= starts_ref[row, item], place(item), held)

    first = first_ref[step]
    where_at = lax.fori_loop(first + 1, last_ref[step] + 1, later, place(first))
    memory_in = (memory.astype(F32) + where_at).astype(BF)
    memory_in_ref[...] = memory_in
    keys_ref[...] = mm(memory_in, wk_ref[...]).astype(BF)
    values_ref[...] = (mm(memory, wv_ref[...]) + bv_ref[...]).astype(BF)
    pad = jnp.transpose(jnp.broadcast_to(pad_ref[0].astype(F32), (LANES, TILE)))
    lane_starts, lane_ends = bounds_ref[0, 0:1, :], bounds_ref[0, 1:2, :]
    slot_grid = iota((TILE, LANES), 0) + base
    lane = iota((TILE, LANES), 1)
    mine = (slot_grid >= lane_starts) & (slot_grid < lane_ends)
    is_open = mine & ((pad > 0.0) | (slot_grid == lane_starts))
    items = starts_ref.shape[1]
    gate = jnp.where(lane < items, jnp.where(is_open, 0.0, 1.0), jnp.where(lane < items + 3, 1.0, 0.0))
    gate_ref[...] = gate.astype(BF)


def keys_values(memory, layout, tables, wk, wv, bv):
    rows, tiles = layout["rows"], layout["tiles"]
    feature = memory.shape[1]
    width = wk.shape[1]
    total = memory.shape[0]
    slab = lambda columns: pl.BlockSpec((TILE, columns), lambda r, t, *_: (r * tiles + t, 0))
    whole = lambda array: pl.BlockSpec(array.shape, lambda r, t, *_: (0,) * array.ndim)
    per_tile = lambda array: pl.BlockSpec((1,) + array.shape[1:], lambda r, t, *_: (r * tiles + t, 0, 0))
    return pl.pallas_call(
        keys_values_kernel,
        grid_spec=pltpu.PrefetchScalarGridSpec(
            num_scalar_prefetch=4,
            grid=(rows, tiles),
            in_specs=[
                slab(feature),
                per_tile(layout["pad"]),
                pl.BlockSpec((1,) + layout["bounds"].shape[1:], lambda r, t, *_: (r, 0, 0)),
                per_tile(tables["tile_sin"]),
                per_tile(tables["tile_cos"]),
                whole(tables["local_sin"]),
                whole(tables["local_cos"]),
                whole(wk), whole(wv), whole(bv),
            ],
            out_specs=[slab(feature), slab(width), slab(width), slab(LANES)],
        ),
        out_shape=[
            jax.ShapeDtypeStruct((total, feature), BF),
            jax.ShapeDtypeStruct((total, width), BF),
            jax.ShapeDtypeStruct((total, width), BF),
            jax.ShapeDtypeStruct((total, LANES), BF),
        ],
        compiler_params=pltpu.CompilerParams(vmem_limit_bytes=40 << 20),
        cost_estimate=pl.CostEstimate(flops=4 * total * feature * width, bytes_accessed=total * 4096, transcendentals=0),
        name="keys_values",
    )(
        layout["first"], layout["last"], layout["starts"], layout["ends"],
        memory, layout["pad"], layout["bounds"], tables["tile_sin"], tables["tile_cos"],
        tables["local_sin"], tables["local_cos"], wk, wv, bv,
    )


def block_rows(pair_transposed):
    blank = jnp.zeros((HEAD, pair_transposed.shape[1]), BF)
    upper = jnp.concatenate([pair_transposed[:HEAD], blank], axis=1)
    lower = jnp.concatenate([blank, pair_transposed[HEAD:]], axis=1)
    return jnp.concatenate([upper, lower], axis=0)


def block_columns(pair):
    twice = jnp.concatenate([pair, pair], axis=0)
    same = (iota(twice.shape, 0) < pair.shape[0]) == (iota(twice.shape, 1) < HEAD)
    return jnp.where(same, twice, jnp.zeros_like(twice))


def gate_rows(item, items, closed, added):
    row = iota((LANES, 2 * LANES), 0)
    value = jnp.where(row == item, closed, 0.0)
    if added is not None:
        for place, part in enumerate(split3(added)):
            value = jnp.where(row == items + place, part.astype(F32), value)
    return value.astype(BF)


def cross_forward_kernel(starts_ref, ends_ref, keys_ref, values_ref, gate_ref, qt_ref, mix_ref, lse_ref, right_ref, scores_ref, acc_ref):
    row = pl.program_id(0)
    items = starts_ref.shape[1]
    width = keys_ref.shape[1]
    pairs = width // PAIR

    def one_item(item, carry):
        start, end = starts_ref[row, item], ends_ref[row, item]
        tile_from = start // TILE
        tile_to = (end + (TILE - 1)) // TILE
        closed = gate_rows(item, items, FAR, None)
        for pair in range(pairs):
            right_ref[pair, :PAIR, :] = block_rows(qt_ref[item, pl.ds(pair * PAIR, PAIR), :])
            right_ref[pair, PAIR:, :] = closed
            acc_ref[pair] = jnp.zeros((PAIR, 2 * LANES), F32)

        def score_tile(tile, largest):
            where_at = pl.ds(pl.multiple_of(tile * TILE, TILE), TILE)
            gate = gate_ref[where_at, :]
            out = []
            for pair in range(pairs):
                left = jnp.concatenate([keys_ref[where_at, pair * PAIR : (pair + 1) * PAIR], gate], axis=1)
                scores = mm(left, right_ref[pair])
                scores_ref[tile - tile_from, :, pair * 2 * LANES : (pair + 1) * 2 * LANES] = scores
                out.append(jnp.maximum(largest[pair], jnp.max(scores.reshape(TILE // 8, 8, 2 * LANES), axis=0)))
            return tuple(out)

        lowest = jnp.full((8, 2 * LANES), -3.0e38, F32)
        largest = lax.fori_loop(tile_from, tile_to, score_tile, (lowest,) * pairs)
        largest = [jnp.max(one, axis=0, keepdims=True) for one in largest]

        def mix_tile(tile, sums):
            where_at = pl.ds(pl.multiple_of(tile * TILE, TILE), TILE)
            out = []
            for pair in range(pairs):
                scores = scores_ref[tile - tile_from, :, pair * 2 * LANES : (pair + 1) * 2 * LANES]
                expo = jnp.exp(scores - largest[pair])
                out.append(sums[pair] + jnp.sum(expo.reshape(TILE // 8, 8, 2 * LANES), axis=0))
                values = values_ref[where_at, pair * PAIR : (pair + 1) * PAIR]
                acc_ref[pair] += mm_tn(values, expo.astype(BF))
            return tuple(out)

        sums = lax.fori_loop(tile_from, tile_to, mix_tile, (jnp.zeros((8, 2 * LANES), F32),) * pairs)
        mixed = []
        for pair in range(pairs):
            total = jnp.sum(sums[pair], axis=0, keepdims=True)
            both = acc_ref[pair] / total
            mixed += [both[:HEAD, :LANES], both[HEAD:, LANES:]]
            lse = largest[pair] + jnp.log(total)
            lse_ref[item, 2 * pair : 2 * pair + 1, :] = lse[:, :LANES]
            lse_ref[item, 2 * pair + 1 : 2 * pair + 2, :] = lse[:, LANES:]
        mix_ref[item] = jnp.transpose(jnp.concatenate(mixed, axis=0))
        return carry

    lax.fori_loop(0, items, one_item, 0)


def cross_forward(keys, values, gate, qt, layout):
    rows, items = layout["rows"], layout["items"]
    slots = layout["slots"]
    width = keys.shape[1]
    heads = width // HEAD
    tiles_most = min(slots, -(-layout["longest"] // TILE) * TILE + TILE) // TILE
    by_row = lambda columns: pl.BlockSpec((slots, columns), lambda r, *_: (r, 0))
    by_items = lambda one, two: pl.BlockSpec((items, one, two), lambda r, *_: (r, 0, 0))
    return pl.pallas_call(
        cross_forward_kernel,
        grid_spec=pltpu.PrefetchScalarGridSpec(
            num_scalar_prefetch=2,
            grid=(rows,),
            in_specs=[by_row(width), by_row(width), by_row(LANES), by_items(width, LANES)],
            out_specs=[by_items(LANES, width), by_items(heads, LANES)],
            scratch_shapes=[
                pltpu.VMEM((width // PAIR, 2 * LANES, 2 * LANES), BF),
                pltpu.VMEM((tiles_most, TILE, heads * LANES), F32),
                pltpu.VMEM((width // PAIR, PAIR, 2 * LANES), F32),
            ],
        ),
        out_shape=[
            jax.ShapeDtypeStruct((rows * items, LANES, width), F32),
            jax.ShapeDtypeStruct((rows * items, heads, LANES), F32),
        ],
        compiler_params=pltpu.CompilerParams(vmem_limit_bytes=48 << 20),
        cost_estimate=pl.CostEstimate(flops=rows * 19 * 4 * 512 * TILE * 1024, bytes_accessed=keys.shape[0] * 2304, transcendentals=0),
        name="cross_forward",
    )(layout["starts"], layout["ends"], keys, values, gate, qt)


def cross_backward_kernel(
    own_columns, first_ref, last_ref, mine_ref,
    memory_ref, memory_in_ref, keys_ref, values_ref, gate_ref,
    q_ref, qt_ref, g_ref, gt_ref, lse_ref, inner_ref, wk_ref, wv_ref,
    gmem_ref, dq_ref, dwk_ref, dwv_ref, dbv_ref,
    score_right, prob_right, key_right, value_right, dq_acc, dk_acc, dv_acc, low_k, low_v, wk_acc, wv_acc, bv_acc,
):
    row, tile = pl.program_id(0), pl.program_id(1)
    rows, tiles = pl.num_programs(0), pl.num_programs(1)
    step = row * tiles + tile
    width = keys_ref.shape[1]
    pairs = width // PAIR
    items = q_ref.shape[0]

    @pl.when(step == 0)
    def _():
        wk_acc[...] = jnp.zeros_like(wk_acc)
        wv_acc[...] = jnp.zeros_like(wv_acc)
        bv_acc[...] = jnp.zeros_like(bv_acc)

    @pl.when(tile == 0)
    def _():
        def lay_out(item, carry):
            for pair in range(pairs):
                columns = slice(pair * PAIR, (pair + 1) * PAIR)
                score_right[item, pair, :PAIR, :] = block_rows(qt_ref[item, columns, :])
                prob_right[item, pair, :PAIR, :] = block_rows(gt_ref[item, columns, :])
                lse = jnp.concatenate([lse_ref[item, 2 * pair : 2 * pair + 1, :], lse_ref[item, 2 * pair + 1 : 2 * pair + 2, :]], axis=1)
                inner = jnp.concatenate([inner_ref[item, 2 * pair : 2 * pair + 1, :], inner_ref[item, 2 * pair + 1 : 2 * pair + 2, :]], axis=1)
                score_right[item, pair, PAIR:, :] = gate_rows(item, items, FAR, -lse)
                prob_right[item, pair, PAIR:, :] = gate_rows(item, items, 0.0, -inner)
                key_right[item, pair] = block_columns(q_ref[item, :, columns])
                value_right[item, pair] = block_columns(g_ref[item, :, columns])
            return carry

        lax.fori_loop(0, items, lay_out, 0)
        dq_acc[...] = jnp.zeros_like(dq_acc)

    dk_acc[...] = jnp.zeros_like(dk_acc)
    dv_acc[...] = jnp.zeros_like(dv_acc)
    gate = gate_ref[...]

    def one_item(item, carry):
        for pair in range(pairs):
            columns = slice(pair * PAIR, (pair + 1) * PAIR)
            keys, values = keys_ref[:, columns], values_ref[:, columns]
            probs = jnp.exp(mm(jnp.concatenate([keys, gate], axis=1), score_right[item, pair]))
            slopes = mm(jnp.concatenate([values, gate], axis=1), prob_right[item, pair])
            low_probs = probs.astype(BF)
            low_scores = (probs * slopes).astype(BF)
            dv_acc[:, columns] += mm(low_probs, value_right[item, pair])
            dk_acc[:, columns] += mm(low_scores, key_right[item, pair])
            dq_acc[item, pair] += mm_tn(keys, low_scores)
        return carry

    lax.fori_loop(first_ref[step], last_ref[step] + 1, one_item, 0)
    grad_keys = dk_acc[...].astype(BF)
    grad_values = dv_acc[...].astype(BF)
    low_k[...] = grad_keys
    low_v[...] = grad_values
    gmem_ref[...] = mm_nt(grad_keys, wk_ref[...]) + mm_nt(grad_values, wv_ref[...])
    if own_columns == width:
        own = slice(None)
    else:
        own = pl.ds(pl.multiple_of(mine_ref[0] * own_columns, own_columns), own_columns)
    own_keys, own_values = low_k[:, own], low_v[:, own]
    wk_acc[...] += mm_tn(own_keys, memory_in_ref[...])
    wv_acc[...] += mm_tn(own_values, memory_ref[...])
    bv_acc[...] += jnp.sum(own_values.astype(F32).reshape(TILE // 8, 8, own_columns), axis=0)

    @pl.when(tile == tiles - 1)
    def _():
        def give(item, carry):
            parts = []
            for pair in range(pairs):
                both = dq_acc[item, pair]
                parts += [both[:HEAD, :LANES], both[HEAD:, LANES:]]
            dq_ref[item] = jnp.transpose(jnp.concatenate(parts, axis=0) * (1.0 / math.sqrt(HEAD))).astype(BF)
            return carry

        lax.fori_loop(0, items, give, 0)

    @pl.when(step == rows * tiles - 1)
    def _():
        dwk_ref[...] = jnp.transpose(wk_acc[...])
        dwv_ref[...] = jnp.transpose(wv_acc[...])
        dbv_ref[...] = jnp.sum(bv_acc[...], axis=0, keepdims=True)


def cross_backward(memory, memory_in, keys, values, gate, q, qt, g, gt, lse, inner, wk, wv, layout, own_columns, mine):
    rows, items, tiles = layout["rows"], layout["items"], layout["tiles"]
    total, feature = memory.shape
    width = keys.shape[1]
    heads, pairs = width // HEAD, width // PAIR
    slab = lambda columns: pl.BlockSpec((TILE, columns), lambda r, t, *_: (r * tiles + t, 0))
    whole = lambda shape: pl.BlockSpec(shape, lambda r, t, *_: (0,) * len(shape))
    by_items = lambda one, two: pl.BlockSpec((items, one, two), lambda r, t, *_: (r, 0, 0))
    return pl.pallas_call(
        functools.partial(cross_backward_kernel, own_columns),
        grid_spec=pltpu.PrefetchScalarGridSpec(
            num_scalar_prefetch=3,
            grid=(rows, tiles),
            in_specs=[
                slab(feature), slab(feature), slab(width), slab(width), slab(LANES),
                by_items(LANES, width), by_items(width, LANES), by_items(LANES, width), by_items(width, LANES),
                by_items(heads, LANES), by_items(heads, LANES),
                whole(wk.shape), whole(wv.shape),
            ],
            out_specs=[
                slab(feature), by_items(LANES, width),
                whole((feature, own_columns)), whole((feature, own_columns)), whole((1, own_columns)),
            ],
            scratch_shapes=[
                pltpu.VMEM((items, pairs, 2 * LANES, 2 * LANES), BF),
                pltpu.VMEM((items, pairs, 2 * LANES, 2 * LANES), BF),
                pltpu.VMEM((items, pairs, 2 * LANES, PAIR), BF),
                pltpu.VMEM((items, pairs, 2 * LANES, PAIR), BF),
                pltpu.VMEM((items, pairs, PAIR, 2 * LANES), F32),
                pltpu.VMEM((TILE, width), F32),
                pltpu.VMEM((TILE, width), F32),
                pltpu.VMEM((TILE, width), BF),
                pltpu.VMEM((TILE, width), BF),
                pltpu.VMEM((own_columns, feature), F32),
                pltpu.VMEM((own_columns, feature), F32),
                pltpu.VMEM((8, own_columns), F32),
            ],
        ),
        out_shape=[
            jax.ShapeDtypeStruct((total, feature), F32),
            jax.ShapeDtypeStruct((rows * items, LANES, width), BF),
            jax.ShapeDtypeStruct((feature, own_columns), F32),
            jax.ShapeDtypeStruct((feature, own_columns), F32),
            jax.ShapeDtypeStruct((1, own_columns), F32),
        ],
        compiler_params=pltpu.CompilerParams(vmem_limit_bytes=48 << 20),
        cost_estimate=pl.CostEstimate(flops=60 * total * feature * width // 4, bytes_accessed=total * 6144, transcendentals=0),
        name="cross_backward",
    )(
        layout["first"], layout["last"], mine, memory, memory_in, keys, values, gate,
        q, qt, g, gt, lse, inner, wk, wv,
    )


def position_tables(starts, tiles, feature):
    lane = jnp.arange(feature, dtype=jnp.int32)
    rates = jnp.exp((lane // 2).astype(F32) * (-2.0 * math.log(10000.0) / feature))
    turn = jnp.where(lane % 2 == 1, 0.5 * math.pi, 0.0).astype(F32)
    local = jnp.arange(TILE, dtype=F32)[:, None] * rates[None, :]
    begin = TILE * jnp.arange(tiles, dtype=jnp.int32)[None, :, None] - starts[:, None, :]
    angle = begin.astype(F32).reshape(-1, starts.shape[1])[:, :, None] * rates + turn
    return {"tile_sin": jnp.sin(angle), "tile_cos": jnp.cos(angle), "local_sin": jnp.sin(local), "local_cos": jnp.cos(local)}


def memory_layout(lengths, key_pad):
    rows, items = lengths.shape
    slots = key_pad.shape[1]
    tiles = slots // TILE
    ends = jnp.cumsum(lengths, axis=1).astype(jnp.int32)
    starts = (ends - lengths).astype(jnp.int32)
    base = TILE * jnp.arange(tiles, dtype=jnp.int32)
    first = jnp.sum((ends[:, None, :] <= base[None, :, None]).astype(jnp.int32), axis=2)
    last = jnp.sum((starts[:, None, :] < base[None, :, None] + TILE).astype(jnp.int32), axis=2) - 1
    bounds = jnp.pad(jnp.stack([starts, ends], axis=1), ((0, 0), (0, 0), (0, LANES - items)))
    return {
        "rows": rows, "items": items, "slots": slots, "tiles": tiles, "longest": 1200,
        "starts": starts, "ends": ends, "first": first.reshape(-1), "last": last.reshape(-1),
        "bounds": bounds, "pad": key_pad.reshape(rows * tiles, 1, TILE),
    }


def layer_norm(value_in, norm_gain, norm_shift):
    center = value_in - jnp.mean(value_in, axis=-1, keepdims=True)
    spread = jnp.mean(center * center, axis=-1, keepdims=True)
    return center * lax.rsqrt(spread + 1e-05) * norm_gain + norm_shift


def smooth_act(pre_act):
    return 0.5 * pre_act * (1.0 + jnp.tanh(math.sqrt(2.0 / math.pi) * (pre_act + 0.044715 * pre_act * pre_act * pre_act)))


def column_sums(matrix):
    return jnp.sum(matrix.astype(F32), axis=0)


def self_forward(queries, keys_in, values_in):
    scores = jnp.einsum("iqhe,ikhe->ihqk", queries, keys_in, preferred_element_type=F32) / math.sqrt(HEAD)
    largest = jnp.max(scores, axis=-1, keepdims=True)
    expo = jnp.exp(scores - largest)
    probs = expo / jnp.sum(expo, axis=-1, keepdims=True)
    mix = jnp.einsum("ihqk,ikhe->iqhe", probs.astype(BF), values_in, preferred_element_type=F32)
    return mix.astype(BF), probs


def self_backward(queries, keys_in, values_in, probs, grad_mixed):
    grad_values = jnp.einsum("ihqk,iqhe->ikhe", probs.astype(BF), grad_mixed, preferred_element_type=F32)
    grad_probs = jnp.einsum("iqhe,ikhe->ihqk", grad_mixed, values_in, preferred_element_type=F32)
    inner = jnp.sum(grad_probs * probs, axis=-1, keepdims=True)
    grad_scores = (probs * (grad_probs - inner)).astype(BF)
    grad_queries = jnp.einsum("ihqk,ikhe->iqhe", grad_scores, keys_in, preferred_element_type=F32) / math.sqrt(HEAD)
    grad_keys = jnp.einsum("ihqk,iqhe->ikhe", grad_scores, queries, preferred_element_type=F32) / math.sqrt(HEAD)
    return grad_queries.astype(BF), grad_keys.astype(BF), grad_values.astype(BF)


def solution(mesh):
    tensor = mesh.shape["tensor"]

    def body(
        tokens, memory, mem_lengths, key_pad, query_embed,
        self_wq, self_bq, self_wk, self_wv, self_bv, self_wo, self_bo, norm1_gain, norm1_bias,
        cross_wq, cross_bq, cross_wk, cross_wv, cross_bv, cross_wo, cross_bo, norm2_gain, norm2_bias,
        ffn_w1, ffn_b1, ffn_w2, ffn_b2, norm3_gain, norm3_bias, cotangent,
    ):
        mine = lax.axis_index("tensor")
        own_columns = self_wq.shape[1]
        own_hidden = ffn_w1.shape[1]

        def whole(part, dim):
            if tensor == 1:
                return part
            if tensor != 2:
                return lax.all_gather(part, "tensor", axis=dim, tiled=True)
            other = lax.ppermute(part, "tensor", [(0, 1), (1, 0)])
            low, high = jnp.where(mine == 0, part, other), jnp.where(mine == 0, other, part)
            return jnp.concatenate([low, high], axis=dim)

        def own(full, dim, size):
            return lax.dynamic_slice_in_dim(full, mine * size, size, axis=dim)

        token_count, feature = tokens.shape
        row_count = mem_lengths.shape[0]
        items = token_count // SPAN
        width = own_columns * tensor
        heads = width // HEAD
        to_items = lambda matrix: matrix.reshape(items, SPAN, heads, HEAD)
        padded = lambda matrix: jnp.pad(matrix.reshape(items, SPAN, -1), ((0, 0), (0, LANES - SPAN), (0, 0)))

        swq, swk, swv, swo = whole(self_wq, 1), whole(self_wk, 1), whole(self_wv, 1), whole(self_wo, 0)
        sbq, sbv = whole(self_bq, 0), whole(self_bv, 0)
        cwk, cwv, cbv = whole(cross_wk, 1), whole(cross_wv, 1), whole(cross_bv, 0)
        cwq, cwo, cbq = whole(cross_wq, 1), whole(cross_wo, 0), whole(cross_bq, 0)
        w1, w2, b1 = whole(ffn_w1, 1), whole(ffn_w2, 0), whole(ffn_b1, 0)

        layout = memory_layout(mem_lengths, key_pad)
        tables = position_tables(layout["starts"], layout["tiles"], feature)
        memory_in, cross_keys, cross_values, gate = keys_values(memory, layout, tables, cwk, cwv, cbv[None, :])

        query_pos = jnp.tile(query_embed, (items, 1))
        tokens_wide = tokens.astype(F32)
        shared_in = (tokens_wide + query_pos).astype(BF)
        self_query = (mm(shared_in, swq) + sbq).astype(BF)
        self_keys = mm(shared_in, swk).astype(BF)
        self_values = (mm(tokens, swv) + sbv).astype(BF)
        self_mix, self_probs = self_forward(to_items(self_query), to_items(self_keys), to_items(self_values))
        self_mix = self_mix.reshape(token_count, width)
        resid_one = tokens_wide + (mm(self_mix, swo) + self_bo)
        normed_one, pull_one = jax.vjp(layer_norm, resid_one, norm1_gain, norm1_bias)
        cross_in = (normed_one + query_pos).astype(BF)
        cross_query = (mm(cross_in, cwq) + cbq).astype(BF)
        q = padded(cross_query * jnp.asarray(1.0 / math.sqrt(HEAD), BF))
        qt = jnp.swapaxes(q, 1, 2)
        mix, lse = cross_forward(cross_keys, cross_values, gate, qt, layout)
        mix_wide = mix[:, :SPAN].reshape(token_count, width)
        cross_mix = mix_wide.astype(BF)
        resid_two = normed_one + (mm(cross_mix, cwo) + cross_bo)
        normed_two, pull_two = jax.vjp(layer_norm, resid_two, norm2_gain, norm2_bias)
        ffn_input = normed_two.astype(BF)
        pre_act = mm(ffn_input, w1) + b1
        hidden_wide, pull_act = jax.vjp(smooth_act, pre_act)
        hidden = hidden_wide.astype(BF)
        resid_three = normed_two + (mm(hidden, w2) + ffn_b2)
        normed_three, pull_three = jax.vjp(layer_norm, resid_three, norm3_gain, norm3_bias)
        layer_out = normed_three.astype(BF)
        grad_three, grad_norm3_gain, grad_norm3_bias = pull_three(cotangent.astype(F32))
        low_three = grad_three.astype(BF)
        grad_ffn_b2 = column_sums(low_three)
        grad_ffn_w2 = mm_tn(own(hidden, 1, own_hidden), low_three)
        (grad_pre,) = pull_act(mm_nt(low_three, w2))
        low_pre = grad_pre.astype(BF)
        own_pre = own(low_pre, 1, own_hidden)
        grad_ffn_b1 = column_sums(own_pre)
        grad_ffn_w1 = mm_tn(ffn_input, own_pre)
        grad_two, grad_norm2_gain, grad_norm2_bias = pull_two(grad_three + mm_nt(low_pre, w1))
        low_two = grad_two.astype(BF)
        grad_cross_bo = column_sums(low_two)
        grad_cross_wo = mm_tn(own(cross_mix, 1, own_columns), low_two)
        grad_cross_mix = mm_nt(low_two, cwo).astype(BF)
        inner = jnp.sum((grad_cross_mix.astype(F32) * mix_wide).reshape(items, SPAN, heads, HEAD), axis=-1)
        inner = jnp.pad(jnp.swapaxes(inner, 1, 2), ((0, 0), (0, 0), (0, LANES - SPAN)))
        g = padded(grad_cross_mix)
        gt = jnp.swapaxes(g, 1, 2)
        kernel_columns = own_columns if own_columns % LANES == 0 else width
        grad_memory, dq, grad_cross_wk, grad_cross_wv, grad_cross_bv = cross_backward(
            memory, memory_in, cross_keys, cross_values, gate, q, qt, g, gt, lse, inner, cwk, cwv,
            layout, kernel_columns, mine[None].astype(jnp.int32),
        )
        grad_cross_bv = grad_cross_bv[0]
        if kernel_columns != own_columns:
            grad_cross_wk, grad_cross_wv = own(grad_cross_wk, 1, own_columns), own(grad_cross_wv, 1, own_columns)
            grad_cross_bv = own(grad_cross_bv, 0, own_columns)
        grad_cross_query = dq[:, :SPAN].reshape(token_count, width)
        own_query = own(grad_cross_query, 1, own_columns)
        grad_cross_bq = column_sums(own_query)
        grad_cross_wq = mm_tn(cross_in, own_query)
        grad_cross_in = mm_nt(grad_cross_query, cwq)
        grad_one, grad_norm1_gain, grad_norm1_bias = pull_one(grad_two + grad_cross_in)
        low_one = grad_one.astype(BF)
        grad_self_bo = column_sums(low_one)
        grad_self_wo = mm_tn(own(self_mix, 1, own_columns), low_one)
        grad_self_mix = mm_nt(low_one, swo).astype(BF)
        grad_self_query, grad_self_keys, grad_self_values = self_backward(
            to_items(self_query), to_items(self_keys), to_items(self_values), self_probs, to_items(grad_self_mix)
        )
        grad_self_query = grad_self_query.reshape(token_count, width)
        grad_self_keys = grad_self_keys.reshape(token_count, width)
        grad_self_values = grad_self_values.reshape(token_count, width)
        own_sq, own_sk, own_sv = (own(one, 1, own_columns) for one in (grad_self_query, grad_self_keys, grad_self_values))
        grad_self_bq = column_sums(own_sq)
        grad_self_wq = mm_tn(shared_in, own_sq)
        grad_self_wk = mm_tn(shared_in, own_sk)
        grad_self_wv = mm_tn(tokens, own_sv)
        grad_self_bv = column_sums(own_sv)
        grad_shared = mm_nt(grad_self_query, swq) + mm_nt(grad_self_keys, swk)
        grad_tokens = grad_one + grad_shared + mm_nt(grad_self_values, swv)
        grad_query_embed = jnp.sum((grad_shared + grad_cross_in).reshape(items, SPAN, feature), axis=0)
        partial = [
            grad_query_embed, grad_self_wq, grad_self_bq, grad_self_wk, grad_self_wv, grad_self_bv, grad_self_wo, grad_self_bo,
            grad_norm1_gain, grad_norm1_bias, grad_cross_wq, grad_cross_bq, grad_cross_wk, grad_cross_wv, grad_cross_bv,
            grad_cross_wo, grad_cross_bo, grad_norm2_gain, grad_norm2_bias, grad_ffn_w1, grad_ffn_b1, grad_ffn_w2, grad_ffn_b2,
            grad_norm3_gain, grad_norm3_bias,
        ]
        out = [lax.psum(one.astype(BF), "dp").astype(F32) for one in partial]
        return (layer_out, grad_tokens, grad_memory, *out)

    rep, by_row, by_col, by_first = P(), P("dp", None), P(None, "tensor"), P("tensor", None)
    one_dim = P("tensor")
    return jax.shard_map(
        body,
        mesh=mesh,
        in_specs=(
            by_row, by_row, by_row, by_row, rep,
            by_col, one_dim, by_col, by_col, one_dim, by_first, rep, rep, rep,
            by_col, one_dim, by_col, by_col, one_dim, by_first, rep, rep, rep,
            by_col, one_dim, by_first, rep, rep, rep, by_row,
        ),
        out_specs=(
            by_row, by_row, by_row, rep,
            by_col, one_dim, by_col, by_col, one_dim, by_first, rep, rep, rep,
            by_col, one_dim, by_col, by_col, one_dim, by_first, rep, rep, rep,
            by_col, one_dim, by_first, rep, rep, rep,
        ),
        check_vma=False,
    )
```

```python
import functools
import math

import jax
import jax.numpy as jnp
import numpy as np
from jax import lax
from jax.experimental import pallas as pl
from jax.experimental.pallas import tpu as pltpu
from jax.sharding import PartitionSpec as P

HEAD = 64
SPAN = 100
MEM_MOST = 1200
LANES = 128
PAIR = 2 * HEAD
TILE = 512
BLOCK = 1024
WINDOW = -(-(MEM_MOST + 15) // 32) * 32
FAR = -1.0e9
FEED_LINES = 16
SCALE = 1.0 / math.sqrt(HEAD)
VMEM = 60 << 20
BF = jnp.bfloat16
F32 = jnp.float32


def mm(left, right):
    return jnp.dot(left, right, preferred_element_type=F32)


def mm_tn(left, right):
    return lax.dot_general(left, right, (((0,), (0,)), ((), ())), preferred_element_type=F32)


def mm_nt(left, right):
    return lax.dot_general(left, right, (((1,), (1,)), ((), ())), preferred_element_type=F32)


def split3(value):
    top = value.astype(BF)
    rest = value - top.astype(F32)
    middle = rest.astype(BF)
    return top, middle, (rest - middle.astype(F32)).astype(BF)


def iota(shape, dim):
    return lax.broadcasted_iota(jnp.int32, shape, dim)


def whole_spec(array):
    return pl.BlockSpec(array.shape, lambda *_: (0,) * array.ndim)


def rates_of(feature):
    lane = np.arange(feature)
    rates = np.exp((lane // 2).astype(np.float32) * np.float32(-2.0 * math.log(10000.0) / feature)).astype(np.float32)
    return rates, np.where(lane % 2 == 1, 0.5 * math.pi, 0.0)


def position_tables(starts, slots, feature):
    rates, turn = rates_of(feature)
    wide = rates.astype(np.float64)
    local = np.arange(TILE)[:, None] * wide
    base = TILE * np.arange(slots // TILE)[:, None, None] * wide + turn
    angle = starts.astype(F32)[:, :, None] * jnp.asarray(rates)
    fixed = lambda array: jnp.asarray(array.astype(np.float32))
    return {
        "local_sin": fixed(np.sin(local)), "local_cos": fixed(np.cos(local)),
        "base_sin": fixed(np.sin(base)), "base_cos": fixed(np.cos(base)),
        "start_sin": jnp.sin(angle), "start_cos": jnp.cos(angle),
    }


def memory_layout(lengths, key_pad):
    rows, items = lengths.shape
    slots = key_pad.shape[1]
    tiles = slots // TILE
    ends = jnp.cumsum(lengths, axis=1).astype(jnp.int32)
    starts = (ends - lengths).astype(jnp.int32)
    base = TILE * jnp.arange(tiles, dtype=jnp.int32)
    first = jnp.sum((ends[:, None, :] <= base[None, :, None]).astype(jnp.int32), axis=2)
    last = jnp.sum((starts[:, None, :] < base[None, :, None] + TILE).astype(jnp.int32), axis=2) - 1
    bounds = jnp.pad(jnp.stack([starts, ends], axis=1), ((0, 0), (0, 0), (0, LANES - items)))
    return {
        "rows": rows, "items": items, "slots": slots, "starts": starts, "ends": ends,
        "first": first.reshape(-1), "last": last.reshape(-1),
        "bounds": bounds, "pad": key_pad.reshape(rows * tiles, 1, TILE),
    }


def keys_values_kernel(
    first_ref, last_ref, starts_ref, place_ref,
    memory_ref, pad_ref, bounds_ref, start_sin_ref, start_cos_ref, base_sin_ref, base_cos_ref, local_sin_ref, local_cos_ref,
    wk_own, wv_own, part_ref, rest_ref, bias_own, bias_other,
    memory_in_ref, keys_ref, values_ref, gate_ref, wk_ref, wv_ref,
):
    row = pl.program_id(0)
    parts = memory_ref.shape[0] // TILE
    items = starts_ref.shape[1]
    columns = wk_own.shape[1]

    @pl.when((row == 0) & (pl.program_id(1) == 0))
    def _():
        assemble(wk_ref, wk_own, part_ref, rest_ref, (0, 0), place_ref, 1)
        assemble(wv_ref, wv_own, part_ref, rest_ref, (0, columns), place_ref, 1)

    lane = iota((TILE, LANES), 1)
    lane_starts, lane_ends = bounds_ref[0, 0:1, :], bounds_ref[0, 1:2, :]
    bias = jnp.concatenate(bias_of(place_ref, bias_own, bias_other, 1, columns, columns), axis=1)
    places = []
    for part in range(parts):
        tile = pl.program_id(1) * parts + part
        step = row * pl.num_programs(1) * parts + tile
        here = slice(part * TILE, (part + 1) * TILE)
        base_sin, base_cos = base_sin_ref[part], base_cos_ref[part]

        def place(item, here=here, base_sin=base_sin, base_cos=base_cos):
            start_sin, start_cos = start_sin_ref[0, pl.ds(item, 1), :], start_cos_ref[0, pl.ds(item, 1), :]
            angle_sin = base_sin * start_cos - base_cos * start_sin
            angle_cos = base_cos * start_cos + base_sin * start_sin
            position = angle_sin * local_cos_ref[...] + angle_cos * local_sin_ref[...]
            return (memory_ref[here, :].astype(F32) + position).astype(BF)

        first = first_ref[step]
        memory_in_ref[here, :] = place(first)
        places.append((here, tile, step, first, place))
    values_ref[...] = (mm(memory_ref[...], wv_ref[...]) + bias).astype(BF)
    for here, tile, step, first, place in places:

        def later(item, carry, here=here, tile=tile, place=place):
            slots = iota((TILE, 1), 0) + tile * TILE
            memory_in_ref[here, :] = jnp.where(slots >= starts_ref[row, item], place(item), memory_in_ref[here, :])
            return carry

        lax.fori_loop(first + 1, last_ref[step] + 1, later, 0)
    keys_ref[...] = mm(memory_in_ref[...], wk_ref[...]).astype(BF)
    for part, (here, tile, *_) in enumerate(places):
        pad = jnp.transpose(jnp.broadcast_to(pad_ref[part].astype(F32), (LANES, TILE)))
        slot_grid = iota((TILE, LANES), 0) + tile * TILE
        mine = (slot_grid >= lane_starts) & (slot_grid < lane_ends)
        is_open = mine & ((pad > 0.0) | (slot_grid == lane_starts))
        gate = jnp.where(lane < items, jnp.where(is_open, 0.0, 1.0), jnp.where(lane < items + 3, 1.0, 0.0))
        gate_ref[here, :] = gate.astype(BF)


def keys_values(place, memory, layout, tables, wk_own, wv_own, part, rest, bias_own, bias_other):
    rows, slots = layout["rows"], layout["slots"]
    total, feature = memory.shape
    width = 2 * wk_own.shape[1]
    steps, parts = slots // BLOCK, BLOCK // TILE
    slab = lambda columns: pl.BlockSpec((BLOCK, columns), lambda r, t, *_: (r * steps + t, 0))
    by_row = lambda array: pl.BlockSpec((1,) + array.shape[1:], lambda r, t, *_: (r, 0, 0))
    by_block = lambda array: pl.BlockSpec((parts,) + array.shape[1:], lambda r, t, *_: (t, 0, 0))
    full = pl.BlockSpec((feature, width), lambda *_: (0, 0))
    fixed = [tables["local_sin"], tables["local_cos"], wk_own, wv_own, part, rest, bias_own, bias_other]
    return pl.pallas_call(
        keys_values_kernel,
        grid_spec=pltpu.PrefetchScalarGridSpec(
            num_scalar_prefetch=4,
            grid=(rows, steps),
            in_specs=[
                slab(feature),
                pl.BlockSpec((parts, 1, TILE), lambda r, t, *_: (r * steps + t, 0, 0)),
                by_row(layout["bounds"]), by_row(tables["start_sin"]), by_row(tables["start_cos"]),
                by_block(tables["base_sin"]), by_block(tables["base_cos"]),
            ] + [whole_spec(one) for one in fixed],
            out_specs=[slab(feature), slab(width), slab(width), slab(LANES), full, full],
        ),
        out_shape=[
            jax.ShapeDtypeStruct((total, feature), BF),
            jax.ShapeDtypeStruct((total, width), BF),
            jax.ShapeDtypeStruct((total, width), BF),
            jax.ShapeDtypeStruct((total, LANES), BF),
            jax.ShapeDtypeStruct((feature, width), BF),
            jax.ShapeDtypeStruct((feature, width), BF),
        ],
        compiler_params=pltpu.CompilerParams(vmem_limit_bytes=VMEM),
        cost_estimate=pl.CostEstimate(flops=4 * total * feature * width, bytes_accessed=total * 4096, transcendentals=0),
        name="keys_values",
    )(
        layout["first"], layout["last"], layout["starts"], place,
        memory, layout["pad"], layout["bounds"], tables["start_sin"], tables["start_cos"], tables["base_sin"], tables["base_cos"], *fixed,
    )


def block_rows(pair_transposed):
    blank = jnp.zeros((HEAD, pair_transposed.shape[1]), BF)
    upper = jnp.concatenate([pair_transposed[:HEAD], blank], axis=1)
    lower = jnp.concatenate([blank, pair_transposed[HEAD:]], axis=1)
    return jnp.concatenate([upper, lower], axis=0)


def block_columns(pair):
    twice = jnp.concatenate([pair, pair], axis=0)
    same = (iota(twice.shape, 0) < pair.shape[0]) == (iota(twice.shape, 1) < HEAD)
    return jnp.where(same, twice, jnp.zeros_like(twice))


def gate_rows(item, items, closed, added):
    row = iota((LANES, 2 * LANES), 0)
    value = jnp.where(row == item, closed, 0.0)
    if added is not None:
        for place, part in enumerate(split3(added)):
            value = jnp.where(row == items + place, part.astype(F32), value)
    return value.astype(BF)


def window_of(starts_ref, row, item, slots):
    start = starts_ref[row, item]
    return pl.multiple_of(jnp.minimum((start // 16) * 16, slots - WINDOW), 16)


def cross_forward_kernel(starts_ref, keys_ref, values_ref, gate_ref, qt_ref, mix_ref, mixt_ref, lse_ref):
    row = pl.program_id(0)
    slots = keys_ref.shape[0]
    items = starts_ref.shape[1]

    def one_item(item, carry):
        rows = pl.ds(window_of(starts_ref, row, item, slots), WINDOW)
        right = jnp.concatenate([block_rows(qt_ref[item]), gate_rows(item, items, FAR, None)], axis=0)
        scores = mm(jnp.concatenate([keys_ref[rows, :], gate_ref[rows, :]], axis=1), right)
        largest = jnp.max(scores, axis=0, keepdims=True)
        expo = jnp.exp(scores - largest)
        total = jnp.sum(expo, axis=0, keepdims=True)
        both = mm_tn(values_ref[rows, :], expo.astype(BF)) / total
        mixed = jnp.concatenate([both[:HEAD, :LANES], both[HEAD:, LANES:]], axis=0)
        mixt_ref[item] = mixed
        mix_ref[item] = jnp.transpose(mixed).astype(BF)
        lse_ref[0, pl.ds(item, 1), :] = largest + jnp.log(total)
        return carry

    lax.fori_loop(0, items, one_item, 0, unroll=True)


def cross_forward(keys, values, gate, qt, layout):
    rows, items, slots = layout["rows"], layout["items"], layout["slots"]
    width = keys.shape[1]
    pairs = width // PAIR
    by_pair = pl.BlockSpec((slots, PAIR), lambda r, p, *_: (r, p))
    return pl.pallas_call(
        cross_forward_kernel,
        grid_spec=pltpu.PrefetchScalarGridSpec(
            num_scalar_prefetch=1,
            grid=(rows, pairs),
            in_specs=[
                by_pair, by_pair,
                pl.BlockSpec((slots, LANES), lambda r, p, *_: (r, 0)),
                pl.BlockSpec((items, PAIR, LANES), lambda r, p, *_: (r, p, 0)),
            ],
            out_specs=[
                pl.BlockSpec((items, LANES, PAIR), lambda r, p, *_: (r, 0, p)),
                pl.BlockSpec((items, PAIR, LANES), lambda r, p, *_: (r, p, 0)),
                pl.BlockSpec((1, items, 2 * LANES), lambda r, p, *_: (r * pairs + p, 0, 0)),
            ],
        ),
        out_shape=[
            jax.ShapeDtypeStruct((rows * items, LANES, width), BF),
            jax.ShapeDtypeStruct((rows * items, width, LANES), F32),
            jax.ShapeDtypeStruct((rows * pairs, items, 2 * LANES), F32),
        ],
        compiler_params=pltpu.CompilerParams(vmem_limit_bytes=VMEM),
        cost_estimate=pl.CostEstimate(flops=rows * items * pairs * 512 * WINDOW * 512, bytes_accessed=keys.shape[0] * 2304, transcendentals=0),
        name="cross_forward",
    )(layout["starts"], keys, values, gate, qt)


def cross_backward_kernel(starts_ref, ends_ref, keys_ref, values_ref, gate_ref, qt_ref, gt_ref, mixt_ref, lse_ref, dk_ref, dv_ref, dq_ref):
    row = pl.program_id(0)
    slots = keys_ref.shape[0]
    items = starts_ref.shape[1]

    def one_item(item, carry):
        at = window_of(starts_ref, row, item, slots)
        rows = pl.ds(at, WINDOW)
        qt, gt = qt_ref[item], gt_ref[item]
        products = gt.astype(F32) * mixt_ref[item]
        inner = jnp.concatenate([jnp.sum(products[:HEAD], axis=0, keepdims=True), jnp.sum(products[HEAD:], axis=0, keepdims=True)], axis=1)
        score_right = jnp.concatenate([block_rows(qt), gate_rows(item, items, FAR, -lse_ref[0, pl.ds(item, 1), :])], axis=0)
        slope_right = jnp.concatenate([block_rows(gt), gate_rows(item, items, 0.0, -inner)], axis=0)
        keys, gate = keys_ref[rows, :], gate_ref[rows, :]
        probs = jnp.exp(mm(jnp.concatenate([keys, gate], axis=1), score_right))
        slopes = mm(jnp.concatenate([values_ref[rows, :], gate], axis=1), slope_right)
        low_scores = (probs * slopes).astype(BF)
        slot = iota((WINDOW, 1), 0) + at
        mine = (slot >= starts_ref[row, item]) & (slot < ends_ref[row, item])
        grad_values = mm(probs.astype(BF), block_columns(jnp.transpose(gt))).astype(BF)
        dv_ref[rows, :] = jnp.where(mine, grad_values, dv_ref[rows, :])
        grad_keys = mm(low_scores, block_columns(jnp.transpose(qt))).astype(BF)
        dk_ref[rows, :] = jnp.where(mine, grad_keys, dk_ref[rows, :])
        both = mm_tn(keys, low_scores)
        dq_ref[item] = jnp.transpose(jnp.concatenate([both[:HEAD, :LANES], both[HEAD:, LANES:]], axis=0) * SCALE).astype(BF)
        return carry

    lax.fori_loop(0, items, one_item, 0, unroll=True)


def cross_backward(keys, values, gate, qt, gt, mixt, lse, layout):
    rows, items, slots = layout["rows"], layout["items"], layout["slots"]
    total, width = keys.shape
    pairs = width // PAIR
    by_pair = pl.BlockSpec((slots, PAIR), lambda r, p, *_: (r, p))
    turned = pl.BlockSpec((items, PAIR, LANES), lambda r, p, *_: (r, p, 0))
    return pl.pallas_call(
        cross_backward_kernel,
        grid_spec=pltpu.PrefetchScalarGridSpec(
            num_scalar_prefetch=2,
            grid=(rows, pairs),
            in_specs=[
                by_pair, by_pair,
                pl.BlockSpec((slots, LANES), lambda r, p, *_: (r, 0)),
                turned, turned, turned,
                pl.BlockSpec((1, items, 2 * LANES), lambda r, p, *_: (r * pairs + p, 0, 0)),
            ],
            out_specs=[by_pair, by_pair, pl.BlockSpec((items, LANES, PAIR), lambda r, p, *_: (r, 0, p))],
        ),
        out_shape=[
            jax.ShapeDtypeStruct((total, width), BF),
            jax.ShapeDtypeStruct((total, width), BF),
            jax.ShapeDtypeStruct((rows * items, LANES, width), BF),
        ],
        compiler_params=pltpu.CompilerParams(vmem_limit_bytes=VMEM),
        name="cross_backward",
    )(layout["starts"], layout["ends"], keys, values, gate, qt, gt, mixt, lse)


def memory_weights_kernel(mine_ref, dk_ref, dv_ref, memory_ref, memory_in_ref, out_ref, vec_ref, wk_acc, wv_acc, bv_acc):
    step = pl.program_id(0)
    block, columns = dk_ref.shape

    @pl.when(step == 0)
    def _():
        wk_acc[...] = jnp.zeros_like(wk_acc)
        wv_acc[...] = jnp.zeros_like(wv_acc)
        bv_acc[...] = jnp.zeros_like(bv_acc)

    wk_acc[...] += mm_tn(dk_ref[...], memory_in_ref[...])
    wv_acc[...] += mm_tn(dv_ref[...], memory_ref[...])
    bv_acc[...] += jnp.sum(dv_ref[...].astype(F32).reshape(block // 8, 8, columns), axis=0)

    @pl.when(step == pl.num_programs(0) - 1)
    def _():
        out_ref[...] = jnp.concatenate([jnp.transpose(wk_acc[...]), jnp.transpose(wv_acc[...])], axis=1).astype(BF)
        vec_ref[...] = jnp.concatenate([jnp.sum(bv_acc[...], axis=0, keepdims=True), jnp.zeros((1, columns), F32)], axis=1)


def memory_weights(place, dk, dv, memory, memory_in, columns):
    total, feature = memory.shape
    own = pl.BlockSpec((BLOCK, columns), lambda t, place: (t, place[0]))
    slab = pl.BlockSpec((BLOCK, feature), lambda t, *_: (t, 0))
    whole = lambda shape: pl.BlockSpec(shape, lambda t, *_: (0,) * len(shape))
    return pl.pallas_call(
        memory_weights_kernel,
        grid_spec=pltpu.PrefetchScalarGridSpec(
            num_scalar_prefetch=1,
            grid=(total // BLOCK,),
            in_specs=[own, own, slab, slab],
            out_specs=[whole((feature, 2 * columns)), whole((1, 2 * columns))],
            scratch_shapes=[pltpu.VMEM((columns, feature), F32), pltpu.VMEM((columns, feature), F32), pltpu.VMEM((8, columns), F32)],
        ),
        out_shape=[jax.ShapeDtypeStruct((feature, 2 * columns), BF), jax.ShapeDtypeStruct((1, 2 * columns), F32)],
        compiler_params=pltpu.CompilerParams(vmem_limit_bytes=VMEM),
        name="memory_weights",
    )(place, dk, dv, memory, memory_in)


def memory_gradient_kernel(dk_ref, dv_ref, wk_ref, wv_ref, *rest):
    rest[-1][...] = mm_nt(dk_ref[...], wk_ref[...]) + mm_nt(dv_ref[...], wv_ref[...])


def memory_gradient(dk, dv, wk, wv, piece, pieces, held):
    total, width = dk.shape
    feature = wk.shape[0]
    steps = total // BLOCK // pieces
    slab = lambda columns: pl.BlockSpec((BLOCK, columns), lambda t: (piece * steps + t, 0))
    operands, specs = [dk, dv, wk, wv], [slab(width), slab(width), whole_spec(wk), whole_spec(wv)]
    if held is not None:
        operands, specs = operands + [held], specs + [pl.BlockSpec(memory_space=pl.ANY)]
    return pl.pallas_call(
        memory_gradient_kernel,
        grid=(steps,),
        in_specs=specs,
        out_specs=slab(feature),
        out_shape=jax.ShapeDtypeStruct((total, feature), F32),
        input_output_aliases={} if held is None else {4: 0},
        compiler_params=pltpu.CompilerParams(vmem_limit_bytes=VMEM),
        name="memory_gradient",
    )(*operands)


def assemble(full_ref, own_ref, part_ref, rest_ref, corner, place_ref, dim):
    mine, bit = place_ref[0], place_ref[1]
    rows, columns = own_ref.shape
    half = rows // 2
    line, lane = corner
    for source, offset in ((part_ref, bit * half), (rest_ref, (1 - bit) * half)):
        if dim == 1:
            at = (pl.ds(pl.multiple_of(offset, half), half), pl.ds(pl.multiple_of((1 - mine) * columns, columns), columns))
        elif dim == 0:
            at = (pl.ds(pl.multiple_of((1 - mine) * rows + offset, half), half), slice(None))
        else:
            at = (1 - mine, pl.ds(pl.multiple_of(offset, half), half), slice(None))
        full_ref[at] = source[line : line + half, lane : lane + columns]
    if dim == 1:
        full_ref[:, pl.ds(pl.multiple_of(mine * columns, columns), columns)] = own_ref[...]
    elif dim == 0:
        full_ref[pl.ds(pl.multiple_of(mine * rows, rows), rows), :] = own_ref[...]
    else:
        full_ref[mine] = own_ref[...]


def bias_of(place_ref, own_ref, other_ref, line, lane, size):
    if size <= own_ref.shape[1] - lane:
        own, other = own_ref[line : line + 1, lane : lane + size], other_ref[line : line + 1, lane : lane + size]
    else:
        lines = -(-size // own_ref.shape[1])
        own, other = (jnp.concatenate([ref[line + one : line + one + 1, :] for one in range(lines)], axis=1)[:, :size] for ref in (own_ref, other_ref))
    first = place_ref[0] == 0
    return jnp.where(first, own, other), jnp.where(first, other, own)


def assemble_token(wq, wk, wv, cwq, wo, wq_own, wk_own, wv_own, cwq_own, wo_own, part_ref, rest_ref, place_ref):
    rows, columns = wq_own.shape
    assemble(wq, wq_own, part_ref, rest_ref, (0, 0), place_ref, 1)
    assemble(wk, wk_own, part_ref, rest_ref, (0, columns), place_ref, 1)
    assemble(wv, wv_own, part_ref, rest_ref, (rows // 2, 0), place_ref, 1)
    assemble(cwq, cwq_own, part_ref, rest_ref, (rows // 2, columns), place_ref, 1)
    assemble(wo, wo_own, part_ref, rest_ref, (rows, 0), place_ref, 0)


def normalize(value):
    center = value - jnp.mean(value, axis=-1, keepdims=True)
    spread = lax.rsqrt(jnp.mean(center * center, axis=-1, keepdims=True) + 1e-05)
    return center * spread, spread


def normalize_back(grad, normed, spread, gain):
    scaled = grad * gain
    inner = jnp.mean(scaled * normed, axis=-1, keepdims=True)
    return (scaled - jnp.mean(scaled, axis=-1, keepdims=True) - normed * inner) * spread


def total_rows(value):
    return jnp.sum(value, axis=0, keepdims=True)


def cut_items(value):
    blank = jnp.zeros((LANES - SPAN, value.shape[1]), value.dtype)
    return [jnp.concatenate([value[at : at + SPAN], blank], axis=0) for at in range(0, value.shape[0], SPAN)]


def join_items(pieces):
    return jnp.concatenate([one[:SPAN] for one in pieces], axis=0)


def self_probs(keys, qt_block):
    scores = mm(keys, qt_block)
    scores = jnp.where(iota(scores.shape, 0) < SPAN, scores, FAR)
    expo = jnp.exp(scores - jnp.max(scores, axis=0, keepdims=True))
    return expo / jnp.sum(expo, axis=0, keepdims=True)


def own_blocks(both):
    return jnp.concatenate([both[:HEAD, :LANES], both[HEAD:, LANES:]], axis=0)


def token_forward_kernel(
    place_ref, tokens_ref, embed_ref,
    wq_own, wk_own, wv_own, cwq_own, wo_own, part_ref, rest_ref, bias_own, bias_other, so_bias, gain_ref, shift_ref,
    q_ref, k_ref, v_ref, mix_ref, resid_ref, normed_ref, qt_ref,
    wq, wk, wv, wo, cwq,
):
    @pl.when(pl.program_id(0) == 0)
    def _():
        assemble_token(wq, wk, wv, cwq, wo, wq_own, wk_own, wv_own, cwq_own, wo_own, part_ref, rest_ref, place_ref)

    width = wq.shape[1]
    half = width // 2
    bias = lambda line, lane: jnp.concatenate(bias_of(place_ref, bias_own, bias_other, line, lane, half), axis=1)
    tokens = tokens_ref[...]
    items = tokens.shape[0] // SPAN
    query_pos = jnp.concatenate([embed_ref[...]] * items, axis=0)
    tokens_wide = tokens.astype(F32)
    shared_in = (tokens_wide + query_pos).astype(BF)
    q = (mm(shared_in, wq[...]) + bias(0, 0)).astype(BF)
    k = mm(shared_in, wk[...]).astype(BF)
    v = (mm(tokens, wv[...]) + bias(0, half)).astype(BF)
    q_ref[...], k_ref[...], v_ref[...] = q, k, v
    q_items, k_items, v_items = (cut_items(one.astype(F32)) for one in (q, k, v))
    mixes = []
    for item in range(items):
        qt = jnp.transpose(q_items[item] * SCALE).astype(BF)
        keys, values = k_items[item].astype(BF), v_items[item].astype(BF)
        mixed = []
        for at in range(0, width, PAIR):
            probs = self_probs(keys[:, at : at + PAIR], block_rows(qt[at : at + PAIR]))
            mixed.append(own_blocks(mm_tn(values[:, at : at + PAIR], probs.astype(BF))))
        mixes.append(jnp.transpose(jnp.concatenate(mixed, axis=0)))
    mix = join_items(mixes).astype(BF)
    mix_ref[...] = mix
    resid = tokens_wide + (mm(mix, wo[...]) + so_bias[...])
    resid_ref[...] = resid
    normed, _ = normalize(resid)
    normed = normed * gain_ref[...] + shift_ref[...]
    normed_ref[...] = normed
    cross_in = (normed + query_pos).astype(BF)
    cross_q = (mm(cross_in, cwq[...]) + bias(1, 0)).astype(BF).astype(F32) * SCALE
    for item, one in enumerate(cut_items(cross_q)):
        qt_ref[item] = jnp.transpose(one).astype(BF)


def token_forward(place, tokens, embed, weights, part, rest, bias_own, bias_other, so_bias, gain, shift, rows):
    token_count, feature = tokens.shape
    width = 2 * weights[0].shape[1]
    size = token_count // rows
    items = size // SPAN
    slab = lambda columns: pl.BlockSpec((size, columns), lambda r, *_: (r, 0))
    flat = [*weights, part, rest]
    fixed = [bias_own, bias_other, so_bias, gain, shift]
    return pl.pallas_call(
        token_forward_kernel,
        grid_spec=pltpu.PrefetchScalarGridSpec(
            num_scalar_prefetch=1,
            grid=(rows,),
            in_specs=[slab(feature), whole_spec(embed)] + [whole_spec(one) for one in flat + fixed],
            out_specs=[slab(width)] * 4 + [slab(feature)] * 2 + [pl.BlockSpec((items, width, LANES), lambda r, *_: (r, 0, 0))],
            scratch_shapes=[pltpu.VMEM((feature, width), BF)] * 3 + [pltpu.VMEM((width, feature), BF), pltpu.VMEM((feature, width), BF)],
        ),
        out_shape=[jax.ShapeDtypeStruct((token_count, width), BF)] * 4
        + [jax.ShapeDtypeStruct((token_count, feature), F32)] * 2
        + [jax.ShapeDtypeStruct((rows * items, width, LANES), BF)],
        compiler_params=pltpu.CompilerParams(vmem_limit_bytes=VMEM),
        cost_estimate=pl.CostEstimate(flops=14 * token_count * feature * width, bytes_accessed=16 * token_count * feature, transcendentals=0),
        name="token_forward",
    )(place, tokens, embed, *flat, *fixed)


def gelu_both(pre):
    inner = math.sqrt(2.0 / math.pi)
    square = pre * pre
    bend = jnp.tanh(pre * (inner + (inner * 0.044715) * square))
    lift = 0.5 + 0.5 * bend
    slope = lift + (0.5 * pre) * (1.0 - bend * bend) * (inner + (3.0 * inner * 0.044715) * square)
    return pre * lift, slope


def feed_kernel(
    place_ref, mix_in_ref, normed_one_ref, cotangent_ref,
    wo_own, w1_own, w2_own, token_part, token_rest, part_ref, rest_ref, bias_own, bias_other,
    co_bias, gain2_ref, shift2_ref, f_bias, gain3_ref, shift3_ref,
    out_ref, grad_two_ref, gt_ref, sums_ref,
    wo, w1, w2, hidden, slope, low_pre, mix_scr, w1_acc, w2_acc, wo_acc, b1_acc, vec_acc,
):
    row = pl.program_id(0)
    mine = place_ref[0]
    columns = wo_acc.shape[0]
    width = wo.shape[0]
    size = out_ref.shape[0]
    hidden_half = w1.shape[1]

    @pl.when(row == 0)
    def _():
        assemble(wo, wo_own, token_part, token_rest, (wo.shape[1] + columns // 2, 0), place_ref, 0)
        assemble(w1, w1_own, part_ref, rest_ref, (0, 0), place_ref, 2)
        assemble(w2, w2_own, part_ref, rest_ref, (hidden_half // 2, 0), place_ref, 2)
        for acc in (w1_acc, w2_acc, wo_acc, b1_acc, vec_acc):
            acc[...] = jnp.zeros_like(acc)

    mix = join_items([mix_in_ref[item].astype(F32) for item in range(mix_in_ref.shape[0])]).astype(BF)
    mix_scr[...] = mix
    normed2, spread2 = normalize(normed_one_ref[...] + (mm(mix, wo[...]) + co_bias[...]))
    normed_two = normed2 * gain2_ref[...] + shift2_ref[...]
    feed_in = normed_two.astype(BF)
    b1 = bias_of(place_ref, bias_own, bias_other, 2, 0, hidden_half)
    total = normed_two + f_bias[...]
    for part in range(2):
        one, rise = gelu_both(mm_nt(feed_in, w1[part]) + b1[part])
        hidden[part] = one.astype(BF)
        slope[part] = rise
        total = total + mm(hidden[part], w2[part])
    normed3, spread3 = normalize(total)
    out_ref[...] = (normed3 * gain3_ref[...] + shift3_ref[...]).astype(BF)
    cotangent = cotangent_ref[...].astype(F32)
    grad_three = normalize_back(cotangent, normed3, spread3, gain3_ref[...])
    low_three = grad_three.astype(BF)
    back = grad_three
    for part in range(2):
        low = (mm_nt(low_three, w2[part]) * slope[part]).astype(BF)
        low_pre[part] = low
        back = back + mm(low, w1[part])
    grad_two = normalize_back(back, normed2, spread2, gain2_ref[...])
    grad_two_ref[...] = grad_two
    low_two = grad_two.astype(BF)
    own_pre = low_pre[mine]
    w2_acc[...] += mm_tn(hidden[mine], low_three)
    w1_acc[...] += mm_tn(own_pre, feed_in)
    b1_acc[...] += total_rows(own_pre.astype(F32))
    if columns == width:
        own = slice(None)
    else:
        own = pl.ds(pl.multiple_of(mine * columns, columns), columns)
    wo_acc[...] += mm_tn(mix_scr[:, own], low_two)
    vec_acc[...] += jnp.concatenate(
        [
            total_rows(cotangent * normed3), total_rows(cotangent), total_rows(low_three.astype(F32)),
            total_rows(back * normed2), total_rows(back), total_rows(low_two.astype(F32)),
            jnp.zeros((2, vec_acc.shape[1]), F32),
        ],
        axis=0,
    )
    grad_mix = mm_nt(low_two, wo[...]).astype(BF).astype(F32)
    for item, one in enumerate(cut_items(grad_mix)):
        gt_ref[item] = jnp.transpose(one).astype(BF)

    @pl.when(row == pl.num_programs(0) - 1)
    def _():
        sums_ref[:hidden_half, :] = w1_acc[...].astype(BF)
        sums_ref[hidden_half : 2 * hidden_half, :] = w2_acc[...].astype(BF)
        sums_ref[2 * hidden_half : 2 * hidden_half + columns, :] = wo_acc[...].astype(BF)
        feature = vec_acc.shape[1]
        lines = [b1_acc[:, at : at + feature] for at in range(0, hidden_half, feature)]
        lines[-1] = jnp.concatenate([lines[-1], jnp.zeros((1, feature - lines[-1].shape[1]), F32)], axis=1)
        lines.append(jnp.zeros((FEED_LINES - 8 - len(lines), feature), F32))
        sums_ref[2 * hidden_half + columns :, :] = jnp.concatenate([vec_acc[...], *lines], axis=0).astype(BF)


def feed(place, mix, normed_one, cotangent, weights, parts, bias_own, bias_other, vectors, rows, columns):
    token_count, feature = normed_one.shape
    width = mix.shape[2]
    size = token_count // rows
    items = size // SPAN
    hidden_half = weights[1].shape[0]
    lines = 2 * hidden_half + columns + FEED_LINES
    slab = lambda columns: pl.BlockSpec((size, columns), lambda r, *_: (r, 0))
    whole = lambda shape: pl.BlockSpec(shape, lambda r, *_: (0,) * len(shape))
    flat = [*weights, *parts]
    fixed = [bias_own, bias_other, *vectors]
    return pl.pallas_call(
        feed_kernel,
        grid_spec=pltpu.PrefetchScalarGridSpec(
            num_scalar_prefetch=1,
            grid=(rows,),
            in_specs=[pl.BlockSpec((items, LANES, width), lambda r, *_: (r, 0, 0)), slab(feature), slab(feature)]
            + [whole_spec(one) for one in flat + fixed],
            out_specs=[
                slab(feature), slab(feature), pl.BlockSpec((items, width, LANES), lambda r, *_: (r, 0, 0)),
                whole((lines, feature)),
            ],
            scratch_shapes=[
                pltpu.VMEM((width, feature), BF),
                pltpu.VMEM((2, hidden_half, feature), BF),
                pltpu.VMEM((2, hidden_half, feature), BF),
                pltpu.VMEM((2, size, hidden_half), BF),
                pltpu.VMEM((2, size, hidden_half), F32),
                pltpu.VMEM((2, size, hidden_half), BF),
                pltpu.VMEM((size, width), BF),
                pltpu.VMEM((hidden_half, feature), F32),
                pltpu.VMEM((hidden_half, feature), F32),
                pltpu.VMEM((columns, feature), F32),
                pltpu.VMEM((1, hidden_half), F32),
                pltpu.VMEM((8, feature), F32),
            ],
        ),
        out_shape=[
            jax.ShapeDtypeStruct((token_count, feature), BF),
            jax.ShapeDtypeStruct((token_count, feature), F32),
            jax.ShapeDtypeStruct((rows * items, width, LANES), BF),
            jax.ShapeDtypeStruct((lines, feature), BF),
        ],
        compiler_params=pltpu.CompilerParams(vmem_limit_bytes=VMEM),
        name="feed",
    )(place, mix, normed_one, cotangent, *flat, *fixed)


def token_backward_kernel(
    place_ref, dq_in_ref, grad_two_ref, resid_ref, normed_ref, tokens_ref, embed_ref, q_ref, k_ref, v_ref, mix_ref,
    memory_sums_ref, memory_vec_ref,
    wq_own, wk_own, wv_own, cwq_own, wo_own, part_ref, rest_ref, gain_ref,
    grad_tokens_ref, sums_ref,
    wq, wk, wv, wo, cwq, cross_dq, low_q, low_k, low_v, cwq_acc, wq_acc, wk_acc, wv_acc, wo_acc, embed_acc, vec_acc,
):
    row = pl.program_id(0)
    mine = place_ref[0]
    width = wq.shape[1]
    columns = wo_acc.shape[0]

    @pl.when(row == 0)
    def _():
        assemble_token(wq, wk, wv, cwq, wo, wq_own, wk_own, wv_own, cwq_own, wo_own, part_ref, rest_ref, place_ref)
        for acc in (cwq_acc, wq_acc, wk_acc, wv_acc, wo_acc, embed_acc, vec_acc):
            acc[...] = jnp.zeros_like(acc)

    if columns == width:
        own = slice(None)
    else:
        own = pl.ds(pl.multiple_of(mine * columns, columns), columns)
    tokens = tokens_ref[...]
    items = tokens.shape[0] // SPAN
    query_pos = jnp.concatenate([embed_ref[...]] * items, axis=0)
    shared_in = (tokens.astype(F32) + query_pos).astype(BF)
    cross_in = (normed_ref[...] + query_pos).astype(BF)
    cross_dq[...] = join_items([dq_in_ref[item].astype(F32) for item in range(items)]).astype(BF)
    cwq_acc[...] += mm_tn(cross_in, cross_dq[:, own])
    grad_cross_in = mm_nt(cross_dq[...], cwq[...])
    back = grad_two_ref[...] + grad_cross_in
    normed, spread = normalize(resid_ref[...])
    grad_one = normalize_back(back, normed, spread, gain_ref[...])
    low_one = grad_one.astype(BF)
    wo_acc[...] += mm_tn(mix_ref[:, own], low_one)
    g_items = cut_items(mm_nt(low_one, wo[...]).astype(BF).astype(F32))
    q_items = cut_items(q_ref[...].astype(F32) * SCALE)
    k_items, v_items = cut_items(k_ref[...].astype(F32)), cut_items(v_ref[...].astype(F32))
    all_dq, all_dk, all_dv = [], [], []
    for item in range(items):
        qt, gt = jnp.transpose(q_items[item]).astype(BF), jnp.transpose(g_items[item]).astype(BF)
        qn, gn, keys, values = (one[item].astype(BF) for one in (q_items, g_items, k_items, v_items))
        one_dq, one_dk, one_dv = [], [], []
        for at in range(0, width, PAIR):
            here = slice(at, at + PAIR)
            probs = self_probs(keys[:, here], block_rows(qt[here]))
            slopes = mm(values[:, here], block_rows(gt[here]))
            inner = jnp.sum(probs * slopes, axis=0, keepdims=True)
            low = (probs * (slopes - inner)).astype(BF)
            one_dv.append(mm(probs.astype(BF), block_columns(gn[:, here])))
            one_dk.append(mm(low, block_columns(qn[:, here])))
            one_dq.append(own_blocks(mm_tn(keys[:, here], low)))
        all_dq.append(jnp.transpose(jnp.concatenate(one_dq, axis=0) * SCALE))
        all_dk.append(jnp.concatenate(one_dk, axis=1))
        all_dv.append(jnp.concatenate(one_dv, axis=1))
    low_q[...] = join_items(all_dq).astype(BF)
    low_k[...] = join_items(all_dk).astype(BF)
    low_v[...] = join_items(all_dv).astype(BF)
    wq_acc[...] += mm_tn(shared_in, low_q[:, own])
    wk_acc[...] += mm_tn(shared_in, low_k[:, own])
    wv_acc[...] += mm_tn(tokens, low_v[:, own])
    grad_shared = mm_nt(low_q[...], wq[...]) + mm_nt(low_k[...], wk[...])
    grad_tokens_ref[...] = grad_one + grad_shared + mm_nt(low_v[...], wv[...])
    position = grad_shared + grad_cross_in
    embed_acc[...] += sum(position[at : at + SPAN] for at in range(0, position.shape[0], SPAN))
    vec_acc[...] += jnp.concatenate(
        [
            total_rows(back * normed), total_rows(back), total_rows(low_one.astype(F32)),
            total_rows(cross_dq[...].astype(F32)), total_rows(low_q[...].astype(F32)), total_rows(low_v[...].astype(F32)),
            jnp.zeros((2, width), F32),
        ],
        axis=0,
    )

    @pl.when(row == pl.num_programs(0) - 1)
    def _():
        feature = wq_acc.shape[0]
        for at, (one, two) in enumerate(((wq_acc, wk_acc), (wv_acc, cwq_acc))):
            sums_ref[at * feature : (at + 1) * feature, :columns] = one[...].astype(BF)
            sums_ref[at * feature : (at + 1) * feature, columns:] = two[...].astype(BF)
        sums_ref[2 * feature : 3 * feature, :] = memory_sums_ref[...]
        sums_ref[3 * feature : 3 * feature + columns, :] = wo_acc[...].astype(BF)
        at = 3 * feature + columns
        sums_ref[at : at + LANES, :] = jnp.concatenate([embed_acc[...], jnp.zeros((LANES - SPAN, width), F32)], axis=0).astype(BF)
        vectors = jnp.concatenate([vec_acc[...], memory_vec_ref[...], jnp.zeros((7, width), F32)], axis=0)
        sums_ref[at + LANES : at + LANES + 16, :] = vectors.astype(BF)
        sums_ref[at + LANES + 16 :, :] = jnp.zeros((sums_ref.shape[0] - at - LANES - 16, width), BF)


def token_backward(place, dq, grad_two, resid, normed, tokens, embed, q, k, v, mix, memory_sums, memory_vec, weights, part, rest, gain, rows, columns, lines):
    token_count, feature = tokens.shape
    width = q.shape[1]
    size = token_count // rows
    items = size // SPAN
    slab = lambda columns: pl.BlockSpec((size, columns), lambda r, *_: (r, 0))
    whole = lambda shape: pl.BlockSpec(shape, lambda r, *_: (0,) * len(shape))
    flat = [memory_sums, memory_vec, *weights, part, rest]
    grads = [(feature, columns)] * 4 + [(columns, feature)]
    return pl.pallas_call(
        token_backward_kernel,
        grid_spec=pltpu.PrefetchScalarGridSpec(
            num_scalar_prefetch=1,
            grid=(rows,),
            in_specs=[pl.BlockSpec((items, LANES, width), lambda r, *_: (r, 0, 0))]
            + [slab(feature)] * 4 + [whole_spec(embed)] + [slab(width)] * 4
            + [whole_spec(one) for one in flat] + [whole_spec(gain)],
            out_specs=[slab(feature), whole((lines, feature))],
            scratch_shapes=[pltpu.VMEM((feature, width), BF)] * 3 + [pltpu.VMEM((width, feature), BF), pltpu.VMEM((feature, width), BF)]
            + [pltpu.VMEM((size, width), BF)] * 4
            + [pltpu.VMEM(one, F32) for one in grads] + [pltpu.VMEM((SPAN, feature), F32), pltpu.VMEM((8, feature), F32)],
        ),
        out_shape=[jax.ShapeDtypeStruct((token_count, feature), F32), jax.ShapeDtypeStruct((lines, feature), BF)],
        compiler_params=pltpu.CompilerParams(vmem_limit_bytes=VMEM),
        name="token_backward",
    )(place, dq, grad_two, resid, normed, tokens, embed, q, k, v, mix, *flat, gain)


def pack_columns_kernel(place_ref, wk_ref, wv_ref, out_ref):
    columns = wk_ref.shape[1]
    out_ref[:, :columns] = wk_ref[...]
    out_ref[:, columns:] = wv_ref[...]


def pack_token_kernel(place_ref, wq_ref, wk_ref, wv_ref, cwq_ref, wo_ref, cwo_ref, out_ref):
    half, columns = wq_ref.shape
    out_ref[:half, :columns] = wq_ref[...]
    out_ref[:half, columns:] = wk_ref[...]
    out_ref[half : 2 * half, :columns] = wv_ref[...]
    out_ref[half : 2 * half, columns:] = cwq_ref[...]
    lines = wo_ref.shape[0]
    out_ref[2 * half : 2 * half + lines, :] = wo_ref[...]
    out_ref[2 * half + lines :, :] = cwo_ref[...]


def pack_lines_kernel(place_ref, w1_ref, w2_ref, out_ref):
    lines = w1_ref.shape[0]
    out_ref[:lines, :] = w1_ref[...]
    out_ref[lines:, :] = w2_ref[...]


def pack_half(kernel, bit, arrays, lines, columns):
    return pl.pallas_call(
        kernel,
        grid_spec=pltpu.PrefetchScalarGridSpec(
            num_scalar_prefetch=1, grid=(1,),
            in_specs=[pl.BlockSpec((one.shape[0] // 2, one.shape[1]), lambda _, place: (place[0], 0)) for one in arrays],
            out_specs=pl.BlockSpec((lines, columns), lambda *_: (0, 0)),
        ),
        out_shape=jax.ShapeDtypeStruct((lines, columns), BF),
        compiler_params=pltpu.CompilerParams(vmem_limit_bytes=VMEM),
        name=kernel.__name__.replace("_kernel", ""),
    )(bit[None], *arrays)


def pack_bias_kernel(sbq_ref, sbv_ref, cbq_ref, cbv_ref, b1_ref, out_ref):
    columns = out_ref.shape[1]
    out_ref[...] = jnp.zeros_like(out_ref)
    size = sbq_ref.shape[1]
    out_ref[0:1, :size], out_ref[0:1, size : 2 * size] = sbq_ref[...], sbv_ref[...]
    out_ref[1:2, :size], out_ref[1:2, size : 2 * size] = cbq_ref[...], cbv_ref[...]
    for line, at in enumerate(range(0, b1_ref.shape[1], columns)):
        part = b1_ref[:, at : min(at + columns, b1_ref.shape[1])]
        out_ref[2 + line : 3 + line, : part.shape[1]] = part


def pack_bias(biases, columns):
    lines = -(-(2 + -(-biases[-1].shape[1] // columns)) // 8) * 8
    return pl.pallas_call(pack_bias_kernel, out_shape=jax.ShapeDtypeStruct((lines, columns), F32), name="pack_bias")(*biases)


def feed_unpack_kernel(hidden_half, columns, sums_ref, w1_ref, w2_ref, wo_ref, b1_ref, *vec_refs):
    w1_ref[...] = sums_ref[:hidden_half, :].astype(F32)
    w2_ref[...] = sums_ref[hidden_half : 2 * hidden_half, :].astype(F32)
    wo_ref[...] = sums_ref[2 * hidden_half : 2 * hidden_half + columns, :].astype(F32)
    vectors = sums_ref[2 * hidden_half + columns :, :].astype(F32)
    for line, one in enumerate(vec_refs):
        one[...] = vectors[line : line + 1]
    lines = -(-hidden_half // vectors.shape[1])
    b1_ref[...] = jnp.concatenate([vectors[8 + one : 9 + one] for one in range(lines)], axis=1)[:, :hidden_half]


def feed_unpack(sums, hidden_half, columns):
    feature = sums.shape[1]
    shapes = [(hidden_half, feature), (hidden_half, feature), (columns, feature), (1, hidden_half)] + [(1, feature)] * 6
    return pl.pallas_call(
        functools.partial(feed_unpack_kernel, hidden_half, columns),
        out_shape=[jax.ShapeDtypeStruct(one, F32) for one in shapes],
        compiler_params=pltpu.CompilerParams(vmem_limit_bytes=VMEM),
        name="feed_unpack",
    )(sums)


def token_unpack_kernel(
    place_ref, kept_ref, other_ref, wq_ref, wk_ref, wv_ref, cwq_ref, cwk_ref, cwv_ref, wo_ref, embed_ref,
    gain_ref, shift_ref, so_ref, cq_ref, sq_ref, sv_ref, cv_ref, sums, vectors,
):
    half = kept_ref.shape[0]
    sums[pl.ds(pl.multiple_of(place_ref[1] * half, half), half), :] = kept_ref[...]
    sums[pl.ds(pl.multiple_of((1 - place_ref[1]) * half, half), half), :] = other_ref[...]
    feature, columns = wq_ref.shape
    for at, (one, two) in enumerate(((wq_ref, wk_ref), (wv_ref, cwq_ref), (cwk_ref, cwv_ref))):
        one[...] = sums[at * feature : (at + 1) * feature, :columns].astype(F32)
        two[...] = sums[at * feature : (at + 1) * feature, columns:].astype(F32)
    wo_ref[...] = sums[3 * feature : 3 * feature + columns, :].astype(F32)
    at = 3 * feature + columns
    embed_ref[...] = sums[at : at + LANES, :].astype(F32)[:SPAN]
    vectors[...] = sums[at + LANES : at + LANES + 16, :].astype(F32)
    gain_ref[...], shift_ref[...], so_ref[...] = vectors[0:1, :], vectors[1:2, :], vectors[2:3, :]
    own = pl.ds(pl.multiple_of(place_ref[0] * columns, columns), columns)
    cq_ref[...], sq_ref[...], sv_ref[...] = vectors[3:4, own], vectors[4:5, own], vectors[5:6, own]
    cv_ref[...] = vectors[8:9, :columns]


def token_unpack(place, kept, other, feature, columns):
    half, width = kept.shape
    shapes = [(feature, columns)] * 6 + [(columns, feature), (SPAN, feature)] + [(1, feature)] * 3 + [(1, columns)] * 4
    whole = lambda shape: pl.BlockSpec(shape, lambda *_: (0, 0))
    return pl.pallas_call(
        token_unpack_kernel,
        grid_spec=pltpu.PrefetchScalarGridSpec(
            num_scalar_prefetch=1, grid=(1,),
            in_specs=[whole((half, width))] * 2,
            out_specs=[whole(one) for one in shapes],
            scratch_shapes=[pltpu.VMEM((2 * half, width), BF), pltpu.VMEM((16, width), F32)],
        ),
        out_shape=[jax.ShapeDtypeStruct(one, F32) for one in shapes],
        compiler_params=pltpu.CompilerParams(vmem_limit_bytes=VMEM),
        name="token_unpack",
    )(place, kept, other)


def after(value, *others):
    return lax.optimization_barrier((value, *others))[0]


def sum_over_dp(packed, at, count, work):
    swap = lambda array, by: lax.ppermute(array, "dp", [(one, one ^ by) for one in range(count)])
    bit_of = lambda by: (at // by) % 2

    def give(array, by):
        half = array.shape[0] // 2
        bit = bit_of(by)
        return lax.dynamic_slice_in_dim(array, (1 - bit) * half, half), lax.dynamic_slice_in_dim(array, bit * half, half)

    def add(kept, got):
        return (kept.astype(F32) + got.astype(F32)).astype(BF)

    def join(array, got, by):
        first = bit_of(by) == 0
        return jnp.concatenate([jnp.where(first, array, got), jnp.where(first, got, array)])

    def exchange(sent, bys):
        got = [swap(one, by) for one, by in zip(sent, bys)]
        done = work(sent)
        return got if done is None else list(lax.optimization_barrier((*got, done)))[: len(got)]

    sent, kept = give(packed, 1)
    held = add(kept, swap(sent, 1))
    middle = held.shape[0] // 2
    two = [held[:middle], held[middle:]]
    hops = [1 << one for one in range(1, count.bit_length() - 1)]
    orders = (hops, hops[1:] + hops[:1])
    for bys in zip(*orders):
        given = [give(one, by) for one, by in zip(two, bys)]
        got = exchange([one for one, _ in given], bys)
        two = [add(one, other) for (_, one), other in zip(given, got)]
    for bys in zip(*(order[::-1] for order in orders)):
        got = exchange(two, bys)
        two = [join(one, other, by) for one, other, by in zip(two, got, bys)]
    mine = jnp.concatenate(two)
    return mine, swap(mine, 1)


def solution(mesh):
    tensor, count = mesh.shape["tensor"], mesh.shape["dp"]

    def body(
        tokens, memory, mem_lengths, key_pad, query_embed,
        self_wq, self_bq, self_wk, self_wv, self_bv, self_wo, self_bo, norm1_gain, norm1_bias,
        cross_wq, cross_bq, cross_wk, cross_wv, cross_bv, cross_wo, cross_bo, norm2_gain, norm2_bias,
        ffn_w1, ffn_b1, ffn_w2, ffn_b2, norm3_gain, norm3_bias, cotangent,
    ):
        rank, at = lax.axis_index("tensor"), lax.axis_index("dp")
        side = (rank * 2 // tensor).astype(jnp.int32)
        bit = (at % 2).astype(jnp.int32)
        place = jnp.stack([side, bit])
        own_columns, own_hidden = self_wq.shape[1], ffn_w1.shape[1]
        feature = tokens.shape[1]
        columns, hidden_half = own_columns * tensor // 2, own_hidden * tensor // 2
        rows = mem_lengths.shape[0]
        direct = tensor == 2 and count > 1
        as_row = lambda one: one.reshape(1, -1)

        def two_halves(part, dim):
            if direct:
                return part, part
            full = lax.all_gather(part, "tensor", axis=dim, tiled=True)
            size = full.shape[dim] // 2
            cut = lambda which: lax.dynamic_slice_in_dim(full, which * size, size, axis=dim)
            return cut(side), cut(1 - side)

        def crossing(kernel, others, lines, first, then):
            sent = pack_half(kernel, bit, others, lines, 2 * columns)
            if not direct:
                return sent, pack_half(kernel, 1 - bit, others, lines, 2 * columns)
            crossed = lax.ppermute(after(sent, *first), "tensor", [(0, 1), (1, 0)])
            return crossed, lax.ppermute(after(crossed, *then), "dp", [(one, one ^ 1) for one in range(count)])

        biases = [two_halves(one, 0) for one in (self_bq, self_bv, cross_bq, cross_bv, ffn_b1)]
        bias_own = pack_bias([as_row(own) for own, _ in biases], 2 * columns)
        if direct:
            bias_other = lax.ppermute(bias_own, "tensor", [(0, 1), (1, 0)])
        else:
            bias_other = pack_bias([as_row(other) for _, other in biases], 2 * columns)
        cwk, cwv = two_halves(cross_wk, 1), two_halves(cross_wv, 1)
        memory_part, memory_rest = crossing(pack_columns_kernel, [cwk[1], cwv[1]], feature // 2, [], [])
        swq, swk, swv, cwq = (two_halves(one, 1) for one in (self_wq, self_wk, self_wv, cross_wq))
        swo, cwo = two_halves(self_wo, 0), two_halves(cross_wo, 0)
        token_weights = [one[0] for one in (swq, swk, swv, cwq, swo)]

        layout = memory_layout(mem_lengths, key_pad)
        tables = position_tables(layout["starts"], layout["slots"], feature)
        memory_in, cross_keys, cross_values, gate, cwk_full, cwv_full = keys_values(
            place, memory, layout, tables, cwk[0], cwv[0], memory_part, memory_rest, bias_own, bias_other
        )
        token_part, token_rest = crossing(
            pack_token_kernel, [one[1] for one in (swq, swk, swv, cwq, swo, cwo)], feature + columns, [memory_part], [gate]
        )
        q, k, v, self_mix, resid_one, normed_one, qt = token_forward(
            place, tokens, query_embed, token_weights, token_part, token_rest, bias_own, bias_other,
            as_row(self_bo), as_row(norm1_gain), as_row(norm1_bias), rows,
        )
        mix, mixt, lse = cross_forward(cross_keys, cross_values, gate, qt, layout)
        w1, w2 = two_halves(jnp.transpose(ffn_w1), 0), two_halves(ffn_w2, 0)
        feed_part, feed_rest = crossing(pack_lines_kernel, [w1[1], w2[1]], hidden_half, [token_rest], [lse])
        layer_out, grad_two, gt, feed_sums = feed(
            place, mix, normed_one, cotangent, [cwo[0], w1[0], w2[0]], [token_part, token_rest, feed_part, feed_rest],
            bias_own, bias_other,
            [as_row(one) for one in (cross_bo, norm2_gain, norm2_bias, ffn_b2, norm3_gain, norm3_bias)], rows, columns,
        )
        multiple = 32 * count
        lines = -(-(3 * feature + columns + LANES + 16) // multiple) * multiple

        def backward():
            dk, dv, dq = cross_backward(cross_keys, cross_values, gate, qt, gt, mixt, lse, layout)
            memory_sums, memory_vec = memory_weights(place, dk, dv, memory, memory_in, columns)
            grad_tokens, token_sums = token_backward(
                place, dq, grad_two, resid_one, normed_one, tokens, query_embed, q, k, v, self_mix, memory_sums, memory_vec,
                token_weights, token_part, token_rest, as_row(norm1_gain), rows, columns, lines,
            )
            pieces, given = 4, []

            def piece(sent):
                if len(given) == pieces:
                    return None
                held = given[-1] if given else None
                given.append(memory_gradient(after(dk, *sent), dv, cwk_full, cwv_full, len(given), pieces, held))
                return given[-1]

            if count > 1:
                kept, other = sum_over_dp(token_sums, at, count, piece)
            else:
                kept, other = token_sums[: lines // 2], token_sums[lines // 2 :]
            while len(given) < pieces:
                piece([])
            return grad_tokens, given[-1], kept, other

        feed_total = lax.psum(feed_sums, "dp")
        shapes = jax.eval_shape(backward)
        grad_tokens, grad_memory, kept, other = lax.cond(
            at < count * rows, backward, lambda: tuple(jnp.zeros(one.shape, one.dtype) for one in shapes)
        )
        g_sq, g_sk, g_sv, g_cq, g_ck, g_cv, g_so, g_embed, g_n1g, g_n1b, g_sbo, g_cbq, g_sbq, g_sbv, g_cbv = token_unpack(
            place, kept, other, feature, columns
        )
        g_w1t, g_w2, g_co, g_b1, g_n3g, g_n3b, g_b2, g_n2g, g_n2b, g_cbo = feed_unpack(feed_total, hidden_half, columns)

        def share(array, dim, size):
            if array.shape[dim] == size:
                return array
            return lax.dynamic_slice_in_dim(array, rank % (tensor // 2) * size, size, axis=dim)

        lanes = lambda array: share(array, 1, own_columns)
        bias = lambda array: share(array, 1, own_columns).reshape(-1)
        vector = lambda array: array.reshape(-1)
        return (
            layer_out, grad_tokens, grad_memory, g_embed,
            lanes(g_sq), bias(g_sbq), lanes(g_sk), lanes(g_sv), bias(g_sbv), share(g_so, 0, own_columns),
            vector(g_sbo), vector(g_n1g), vector(g_n1b),
            lanes(g_cq), bias(g_cbq), lanes(g_ck), lanes(g_cv), bias(g_cbv), share(g_co, 0, own_columns),
            vector(g_cbo), vector(g_n2g), vector(g_n2b),
            jnp.transpose(share(g_w1t, 0, own_hidden)), share(g_b1, 1, own_hidden).reshape(-1), share(g_w2, 0, own_hidden),
            vector(g_b2), vector(g_n3g), vector(g_n3b),
        )

    rep, by_row, by_col, by_first = P(), P("dp", None), P(None, "tensor"), P("tensor", None)
    one_dim = P("tensor")
    return jax.shard_map(
        body,
        mesh=mesh,
        in_specs=(
            by_row, by_row, by_row, by_row, rep,
            by_col, one_dim, by_col, by_col, one_dim, by_first, rep, rep, rep,
            by_col, one_dim, by_col, by_col, one_dim, by_first, rep, rep, rep,
            by_col, one_dim, by_first, rep, rep, rep, by_row,
        ),
        out_specs=(
            by_row, by_row, by_row, rep,
            by_col, one_dim, by_col, by_col, one_dim, by_first, rep, rep, rep,
            by_col, one_dim, by_col, by_col, one_dim, by_first, rep, rep, rep,
            by_col, one_dim, by_first, rep, rep, rep,
        ),
        check_vma=False,
    )
```

```python
import functools
import math

import jax
import jax.numpy as jnp
import numpy as np
from jax import lax
from jax.experimental import pallas as pl
from jax.experimental.pallas import tpu as pltpu
from jax.sharding import PartitionSpec as P

HEAD = 64
SPAN = 100
MEM_MOST = 1200
LANES = 128
PAIR = 2 * HEAD
TILE = 256
BLOCK = 1024
SUMS_BLOCK = 2048
GRAD_BLOCK = 1024
WINDOW = -(-(MEM_MOST + 15) // 32) * 32
FAR = -1.0e9
CHUNKS = 4
LUMP = 256
BIAS_LINES = 16
FEED_LINES = 16
SCALE = 1.0 / math.sqrt(HEAD)
VMEM = 60 << 20
BF = jnp.bfloat16
F32 = jnp.float32


def mm(left, right):
    return jnp.dot(left, right, preferred_element_type=F32)


def mm_tn(left, right):
    return lax.dot_general(left, right, (((0,), (0,)), ((), ())), preferred_element_type=F32)


def mm_nt(left, right):
    return lax.dot_general(left, right, (((1,), (1,)), ((), ())), preferred_element_type=F32)


def split3(value):
    top = value.astype(BF)
    rest = value - top.astype(F32)
    middle = rest.astype(BF)
    return top, middle, (rest - middle.astype(F32)).astype(BF)


def iota(shape, dim):
    return lax.broadcasted_iota(jnp.int32, shape, dim)


def whole_spec(array):
    return pl.BlockSpec(array.shape, lambda *_: (0,) * array.ndim)


def rates_of(feature):
    lane = np.arange(feature)
    rates = np.exp((lane // 2).astype(np.float32) * np.float32(-2.0 * math.log(10000.0) / feature)).astype(np.float32)
    return rates, np.where(lane % 2 == 1, 0.5 * math.pi, 0.0).astype(np.float32)


def bounds_of(lengths_ref, row):
    starts, ends, at = [], [], jnp.int32(0)
    for item in range(lengths_ref.shape[1]):
        starts.append(at)
        at = at + lengths_ref[row, item]
        ends.append(at)
    return starts, ends


def keys_values_kernel(
    row, lengths_ref, place_ref,
    memory_ref, pad_ref, angles_ref, local_sin_ref, local_cos_ref, wk_own, wv_own, part_ref, rest_ref, bias_ref, *refs,
):
    memory_in_ref, gate_ref, keys_ref, values_ref, wk_ref, wv_ref = refs[-6:]
    parts = memory_ref.shape[0] // TILE
    items = lengths_ref.shape[1]
    columns = wk_own.shape[1]

    @pl.when(pl.program_id(0) == 0)
    def _():
        assemble(wk_ref, wk_own, part_ref, rest_ref, (0, 0), place_ref, 1)
        assemble(wv_ref, wv_own, part_ref, rest_ref, (0, columns), place_ref, 1)

    starts, ends = bounds_of(lengths_ref, row)
    lane = iota((TILE, LANES), 1)
    lane_starts, lane_ends = (
        sum(jnp.where(iota((1, LANES), 1) == item, one, 0) for item, one in enumerate(ones)) for ones in (starts, ends)
    )
    tiles, crowded = [], jnp.bool_(False)
    for part in range(parts):
        base = (pl.program_id(0) * parts + part) * TILE
        here = slice(part * TILE, (part + 1) * TILE)
        first = sum((one <= base).astype(jnp.int32) for one in ends)
        last = sum((one < base + TILE).astype(jnp.int32) for one in starts) - 1

        def start_of(item):
            return sum(jnp.where(item == index, one, 0) for index, one in enumerate(starts))

        def place(item, base=base):
            shift = (base - start_of(item)).astype(F32)
            angle = shift * angles_ref[0:1, :] + angles_ref[1:2, :]
            return jnp.sin(angle) * local_cos_ref[...] + jnp.cos(angle) * local_sin_ref[...]

        def later(item, held, base=base, place=place):
            return jnp.where(iota((TILE, 1), 0) + base >= start_of(item), place(item), held)

        position = later(jnp.minimum(first + 1, items - 1), place(first))
        memory_in_ref[here, :] = (memory_ref[here, :].astype(F32) + position).astype(BF)
        tiles.append((here, base, first, last, place, start_of))
        crowded = crowded | (last > first + 1)
    own_bias, line = bias_ref[...], part_ref.shape[0] - BIAS_LINES
    lines = part_ref[line : line + BIAS_LINES, :columns].astype(F32)
    other_bias = lines[0:1] + lines[1:2] + lines[2:3]
    low = place_ref[0] == 0
    biases = jnp.where(low, own_bias, other_bias), jnp.where(low, other_bias, own_bias)
    for half in range(2):
        here = slice(half * columns, (half + 1) * columns)
        values_ref[half] = (mm(memory_ref[...], wv_ref[:, here]) + biases[half]).astype(BF)
    for half in range(2):
        here = slice(half * columns, (half + 1) * columns)
        keys_ref[half] = mm(memory_in_ref[...], wk_ref[:, here]).astype(BF)
    for here, base, *_ in tiles:
        pad = jnp.transpose(jnp.broadcast_to(pad_ref[row : row + 1, here].astype(F32), (LANES, TILE)))
        slot_grid = iota((TILE, LANES), 0) + base
        mine = (slot_grid >= lane_starts) & (slot_grid < lane_ends)
        is_open = mine & ((pad > 0.0) | (slot_grid == lane_starts))
        gate = jnp.where(lane < items, jnp.where(is_open, 0.0, 1.0), jnp.where(lane < items + 3, 1.0, 0.0))
        gate_ref[here, :] = gate.astype(BF)

    @pl.when(crowded)
    def _():
        for here, base, first, last, place, start_of in tiles:

            def patch(item, carry, here=here, base=base, place=place, start_of=start_of):
                with_place = (memory_ref[here, :].astype(F32) + place(item)).astype(BF)
                slots = iota((TILE, 1), 0) + base
                memory_in_ref[here, :] = jnp.where(slots >= start_of(item), with_place, memory_in_ref[here, :])
                return carry

            lax.fori_loop(first + 2, last + 1, patch, 0)
        for half in range(2):
            keys_ref[half] = mm(memory_in_ref[...], wk_ref[:, half * columns : (half + 1) * columns]).astype(BF)


def keys_values(lengths, place, memory, key_pad, wk_own, wv_own, part, rest, bias, row, held):
    rows, slots = key_pad.shape
    total, feature = memory.shape
    columns = wk_own.shape[1]
    steps = slots // BLOCK
    rates, turn = rates_of(feature)
    local = np.arange(TILE)[:, None] * rates.astype(np.float64)
    fixed = [jnp.asarray(np.stack([rates, turn])), jnp.asarray(np.sin(local).astype(np.float32)), jnp.asarray(np.cos(local).astype(np.float32))]
    fixed += [wk_own, wv_own, part, rest, bias]
    slab = lambda columns: pl.BlockSpec((BLOCK, columns), lambda t, *_: (row * steps + t, 0))
    halves = pl.BlockSpec((2, BLOCK, columns), lambda t, *_: (0, row * steps + t, 0))
    full = pl.BlockSpec((feature, 2 * columns), lambda *_: (0, 0))
    held = [] if held is None else list(held)
    return pl.pallas_call(
        functools.partial(keys_values_kernel, row),
        grid_spec=pltpu.PrefetchScalarGridSpec(
            num_scalar_prefetch=2,
            grid=(steps,),
            in_specs=[slab(feature), pl.BlockSpec((rows, BLOCK), lambda t, *_: (0, t))] + [whole_spec(one) for one in fixed]
            + [pl.BlockSpec(memory_space=pl.ANY)] * len(held),
            out_specs=[slab(feature), slab(LANES), halves, halves, full, full],
        ),
        out_shape=[
            jax.ShapeDtypeStruct((total, feature), BF),
            jax.ShapeDtypeStruct((total, LANES), BF),
            jax.ShapeDtypeStruct((2, total, columns), BF),
            jax.ShapeDtypeStruct((2, total, columns), BF),
            jax.ShapeDtypeStruct((feature, 2 * columns), BF),
            jax.ShapeDtypeStruct((feature, 2 * columns), BF),
        ],
        input_output_aliases={4 + len(fixed) + one: one for one in range(len(held))},
        compiler_params=pltpu.CompilerParams(vmem_limit_bytes=VMEM),
        name="keys_values",
    )(lengths, place, memory, key_pad, *fixed, *held)


def block_rows(pair_transposed):
    blank = jnp.zeros((HEAD, pair_transposed.shape[1]), BF)
    upper = jnp.concatenate([pair_transposed[:HEAD], blank], axis=1)
    lower = jnp.concatenate([blank, pair_transposed[HEAD:]], axis=1)
    return jnp.concatenate([upper, lower], axis=0)


def block_columns(pair):
    twice = jnp.concatenate([pair, pair], axis=0)
    same = (iota(twice.shape, 0) < pair.shape[0]) == (iota(twice.shape, 1) < HEAD)
    return jnp.where(same, twice, jnp.zeros_like(twice))


def gate_rows(item, items, closed, added):
    row = iota((LANES, 2 * LANES), 0)
    value = jnp.where(row == item, closed, 0.0)
    if added is not None:
        for place, part in enumerate(split3(added)):
            value = jnp.where(row == items + place, part.astype(F32), value)
    return value.astype(BF)


def window_of(start, slots):
    return pl.multiple_of(jnp.minimum((start // 16) * 16, slots - WINDOW), 16)


def cross_forward_kernel(lengths_ref, keys_ref, values_ref, gate_ref, qt_ref, mix_ref, mixt_ref, lse_ref, scores_a, scores_b, probs_a, probs_b):
    row = pl.program_id(0)
    slots = keys_ref.shape[0]
    items = lengths_ref.shape[1]
    starts, ends = bounds_of(lengths_ref, row)
    works = [(item, pair) for pair in range(keys_ref.shape[1] // PAIR) for item in range(items)]
    scores_of, probs_of = (scores_a, scores_b), (probs_a, probs_b)
    largest, total = {}, {}
    size = WINDOW // CHUNKS

    def lanes(pair):
        return slice(pair * PAIR, (pair + 1) * PAIR)

    def prepare(work):
        item, pair = works[work]
        return jnp.concatenate([block_rows(qt_ref[item, lanes(pair), :]), gate_rows(item, items, FAR, None)], axis=0)

    def score(work, right, chunk):
        item, pair = works[work]
        rows = pl.ds(pl.multiple_of(window_of(starts[item], slots) + chunk * size, 16), size)
        part = mm(jnp.concatenate([keys_ref[rows, lanes(pair)], gate_ref[rows, :]], axis=1), right)
        scores_of[work % 2][chunk * size : (chunk + 1) * size, :] = part
        top = jnp.max(part.reshape(size // 8, 8, 2 * LANES), axis=0)
        largest[work] = top if chunk == 0 else jnp.maximum(largest[work], top)

    def soften(work, chunk):
        if chunk == 0:
            largest[work] = jnp.max(largest[work], axis=0, keepdims=True)
        here = slice(chunk * size, (chunk + 1) * size)
        expo = jnp.exp(scores_of[work % 2][here, :] - largest[work])
        probs_of[work % 2][here, :] = expo.astype(BF)
        add = jnp.sum(expo.reshape(size // 8, 8, 2 * LANES), axis=0)
        total[work] = add if chunk == 0 else total[work] + add

    def finish(work):
        item, pair = works[work]
        rows = pl.ds(window_of(starts[item], slots), WINDOW)
        sums = jnp.sum(total[work], axis=0, keepdims=True)
        both = mm_tn(values_ref[rows, lanes(pair)], probs_of[work % 2][...]) / sums
        mixed = own_blocks(both)
        mixt_ref[item, lanes(pair), :] = mixed
        mix_ref[item, :, lanes(pair)] = jnp.transpose(mixed).astype(BF)
        lse_ref[pair, item : item + 1, :] = largest[work] + jnp.log(sums)

    for step in range(len(works) + 2):
        right = prepare(step) if step < len(works) else None
        if step >= 2:
            finish(step - 2)
        for chunk in range(CHUNKS):
            if step < len(works):
                score(step, right, chunk)
            if 1 <= step <= len(works):
                soften(step - 1, chunk)


def cross_forward(lengths, keys, values, gate, qt):
    rows, items = lengths.shape
    slots, columns = keys.shape[1] // rows, keys.shape[2]
    width = 2 * columns
    pairs = width // PAIR
    by_half = pl.BlockSpec((None, slots, columns), lambda r, p, *_: (p, r, 0))
    turned = pl.BlockSpec((items, columns, LANES), lambda r, p, *_: (r, p, 0))
    return pl.pallas_call(
        cross_forward_kernel,
        grid_spec=pltpu.PrefetchScalarGridSpec(
            num_scalar_prefetch=1,
            grid=(rows, 2),
            in_specs=[by_half, by_half, pl.BlockSpec((slots, LANES), lambda r, p, *_: (r, 0)), turned],
            out_specs=[
                pl.BlockSpec((items, LANES, columns), lambda r, p, *_: (r, 0, p)),
                turned,
                pl.BlockSpec((pairs // 2, items, 2 * LANES), lambda r, p, *_: (r * 2 + p, 0, 0)),
            ],
            scratch_shapes=[pltpu.VMEM((WINDOW, 2 * LANES), F32)] * 2 + [pltpu.VMEM((WINDOW, 2 * LANES), BF)] * 2,
        ),
        out_shape=[
            jax.ShapeDtypeStruct((rows * items, LANES, width), BF),
            jax.ShapeDtypeStruct((rows * items, width, LANES), F32),
            jax.ShapeDtypeStruct((rows * pairs, items, 2 * LANES), F32),
        ],
        compiler_params=pltpu.CompilerParams(vmem_limit_bytes=VMEM),
        name="cross_forward",
    )(lengths, keys, values, gate, qt)


def cross_backward_kernel(lengths_ref, keys_ref, values_ref, gate_ref, qt_ref, gt_ref, mixt_ref, lse_ref, dk_ref, dv_ref, dq_ref):
    row = pl.program_id(0)
    slots = keys_ref.shape[0]
    items = lengths_ref.shape[1]
    starts, ends = bounds_of(lengths_ref, row)

    def one_item(item):
        at = window_of(starts[item], slots)
        rows = pl.ds(at, WINDOW)
        qt, gt = qt_ref[item], gt_ref[item]
        products = gt.astype(F32) * mixt_ref[item]
        inner = jnp.concatenate([jnp.sum(products[:HEAD], axis=0, keepdims=True), jnp.sum(products[HEAD:], axis=0, keepdims=True)], axis=1)
        score_right = jnp.concatenate([block_rows(qt), gate_rows(item, items, FAR, -lse_ref[0, item : item + 1, :])], axis=0)
        slope_right = jnp.concatenate([block_rows(gt), gate_rows(item, items, 0.0, -inner)], axis=0)
        keys, gate = keys_ref[rows, :], gate_ref[rows, :]
        probs = jnp.exp(mm(jnp.concatenate([keys, gate], axis=1), score_right))
        slopes = mm(jnp.concatenate([values_ref[rows, :], gate], axis=1), slope_right)
        low_scores = (probs * slopes).astype(BF)
        slot = iota((WINDOW, 1), 0) + at
        mine = (slot >= starts[item]) & (slot < ends[item])
        grad_values = mm(probs.astype(BF), block_columns(jnp.transpose(gt))).astype(BF)
        dv_ref[rows, :] = jnp.where(mine, grad_values, dv_ref[rows, :])
        grad_keys = mm(low_scores, block_columns(jnp.transpose(qt))).astype(BF)
        dk_ref[rows, :] = jnp.where(mine, grad_keys, dk_ref[rows, :])
        both = mm_tn(keys, low_scores)
        dq_ref[item] = jnp.transpose(jnp.concatenate([both[:HEAD, :LANES], both[HEAD:, LANES:]], axis=0) * SCALE).astype(BF)

    for item in range(items):
        one_item(item)


def cross_backward(lengths, keys, values, gate, qt, gt, mixt, lse):
    rows, items = lengths.shape
    _, total, columns = keys.shape
    slots, width = total // rows, 2 * columns
    pairs, inside = width // PAIR, columns // PAIR
    by_pair = pl.BlockSpec((None, slots, PAIR), lambda r, p, *_: (p // inside, r, p % inside))
    turned = pl.BlockSpec((items, PAIR, LANES), lambda r, p, *_: (r, p, 0))
    return pl.pallas_call(
        cross_backward_kernel,
        grid_spec=pltpu.PrefetchScalarGridSpec(
            num_scalar_prefetch=1,
            grid=(rows, pairs),
            in_specs=[
                by_pair, by_pair,
                pl.BlockSpec((slots, LANES), lambda r, p, *_: (r, 0)),
                turned, turned, turned,
                pl.BlockSpec((1, items, 2 * LANES), lambda r, p, *_: (r * pairs + p, 0, 0)),
            ],
            out_specs=[by_pair, by_pair, pl.BlockSpec((items, LANES, PAIR), lambda r, p, *_: (r, 0, p))],
        ),
        out_shape=[
            jax.ShapeDtypeStruct((2, total, columns), BF),
            jax.ShapeDtypeStruct((2, total, columns), BF),
            jax.ShapeDtypeStruct((rows * items, LANES, width), BF),
        ],
        compiler_params=pltpu.CompilerParams(vmem_limit_bytes=VMEM),
        name="cross_backward",
    )(lengths, keys, values, gate, qt, gt, mixt, lse)


def memory_weights_kernel(mine_ref, dk_ref, dv_ref, memory_ref, memory_in_ref, out_ref, vec_ref, wk_acc, wv_acc, bv_acc):
    step = pl.program_id(0)
    block, columns = dk_ref.shape

    @pl.when(step == 0)
    def _():
        wk_acc[...] = jnp.zeros_like(wk_acc)
        wv_acc[...] = jnp.zeros_like(wv_acc)
        bv_acc[...] = jnp.zeros_like(bv_acc)

    wk_acc[...] += mm_tn(dk_ref[...], memory_in_ref[...])
    wv_acc[...] += mm_tn(dv_ref[...], memory_ref[...])
    bv_acc[...] += jnp.sum(dv_ref[...].astype(F32).reshape(block // 8, 8, columns), axis=0)

    @pl.when(step == pl.num_programs(0) - 1)
    def _():
        out_ref[...] = jnp.concatenate([jnp.transpose(wk_acc[...]), jnp.transpose(wv_acc[...])], axis=1).astype(BF)
        vec_ref[...] = jnp.concatenate([jnp.sum(bv_acc[...], axis=0, keepdims=True), jnp.zeros((1, columns), F32)], axis=1)


def memory_weights(place, dk, dv, memory, memory_in, columns):
    total, feature = memory.shape
    own = pl.BlockSpec((None, SUMS_BLOCK, columns), lambda t, place: (place[0], t, 0))
    slab = pl.BlockSpec((SUMS_BLOCK, feature), lambda t, *_: (t, 0))
    whole = lambda shape: pl.BlockSpec(shape, lambda t, *_: (0,) * len(shape))
    return pl.pallas_call(
        memory_weights_kernel,
        grid_spec=pltpu.PrefetchScalarGridSpec(
            num_scalar_prefetch=1,
            grid=(total // SUMS_BLOCK,),
            in_specs=[own, own, slab, slab],
            out_specs=[whole((feature, 2 * columns)), whole((1, 2 * columns))],
            scratch_shapes=[pltpu.VMEM((columns, feature), F32), pltpu.VMEM((columns, feature), F32), pltpu.VMEM((8, columns), F32)],
        ),
        out_shape=[jax.ShapeDtypeStruct((feature, 2 * columns), BF), jax.ShapeDtypeStruct((1, 2 * columns), F32)],
        compiler_params=pltpu.CompilerParams(vmem_limit_bytes=VMEM),
        name="memory_weights",
    )(place, dk, dv, memory, memory_in)


def memory_gradient_kernel(dk_low, dk_high, dv_low, dv_high, wk_ref, wv_ref, *rest):
    dk = jnp.concatenate([dk_low[...], dk_high[...]], axis=1)
    dv = jnp.concatenate([dv_low[...], dv_high[...]], axis=1)
    rest[-1][...] = mm_nt(dk, wk_ref[...]) + mm_nt(dv, wv_ref[...])


def memory_gradient(dk, dv, wk, wv, piece, pieces, held):
    _, total, columns = dk.shape
    feature = wk.shape[0]
    steps = total // GRAD_BLOCK // pieces
    half = lambda which: pl.BlockSpec((None, GRAD_BLOCK, columns), lambda t: (which, piece * steps + t, 0))
    operands, specs = [dk, dk, dv, dv, wk, wv], [half(0), half(1), half(0), half(1), whole_spec(wk), whole_spec(wv)]
    if held is not None:
        operands, specs = operands + [held], specs + [pl.BlockSpec(memory_space=pl.ANY)]
    return pl.pallas_call(
        memory_gradient_kernel,
        grid=(steps,),
        in_specs=specs,
        out_specs=pl.BlockSpec((GRAD_BLOCK, feature), lambda t: (piece * steps + t, 0)),
        out_shape=jax.ShapeDtypeStruct((total, feature), F32),
        input_output_aliases={} if held is None else {6: 0},
        compiler_params=pltpu.CompilerParams(vmem_limit_bytes=VMEM),
        name="memory_gradient",
    )(*operands)


def assemble(full_ref, own_ref, part_ref, rest_ref, corner, place_ref, dim):
    mine, bit = place_ref[0], place_ref[1]
    rows, columns = own_ref.shape
    half = rows // 2
    line, lane = corner
    for source, offset in ((part_ref, bit * half), (rest_ref, (1 - bit) * half)):
        if dim == 1:
            at = (pl.ds(pl.multiple_of(offset, half), half), pl.ds(pl.multiple_of((1 - mine) * columns, columns), columns))
        elif dim == 0:
            at = (pl.ds(pl.multiple_of((1 - mine) * rows + offset, half), half), slice(None))
        else:
            at = (1 - mine, pl.ds(pl.multiple_of(offset, half), half), slice(None))
        full_ref[at] = source[line : line + half, lane : lane + columns]
    if dim == 1:
        full_ref[:, pl.ds(pl.multiple_of(mine * columns, columns), columns)] = own_ref[...]
    elif dim == 0:
        full_ref[pl.ds(pl.multiple_of(mine * rows, rows), rows), :] = own_ref[...]
    else:
        full_ref[mine] = own_ref[...]


def bias_of(place_ref, own_ref, other_ref, line, lane, size):
    if size <= own_ref.shape[1] - lane:
        own, other = own_ref[line : line + 1, lane : lane + size], other_ref[line : line + 1, lane : lane + size]
    else:
        lines = -(-size // own_ref.shape[1])
        own, other = (jnp.concatenate([ref[line + one : line + one + 1, :] for one in range(lines)], axis=1)[:, :size] for ref in (own_ref, other_ref))
    first = place_ref[0] == 0
    return jnp.where(first, own, other), jnp.where(first, other, own)


def assemble_token(wq, wk, wv, cwq, wo, wq_own, wk_own, wv_own, cwq_own, wo_own, part_ref, rest_ref, place_ref):
    rows, columns = wq_own.shape
    assemble(wq, wq_own, part_ref, rest_ref, (0, 0), place_ref, 1)
    assemble(wk, wk_own, part_ref, rest_ref, (0, columns), place_ref, 1)
    assemble(wv, wv_own, part_ref, rest_ref, (rows // 2, 0), place_ref, 1)
    assemble(cwq, cwq_own, part_ref, rest_ref, (rows // 2, columns), place_ref, 1)
    assemble(wo, wo_own, part_ref, rest_ref, (rows, 0), place_ref, 0)


def give_halves(place_ref, sums, sent_ref, kept_ref):
    half = sent_ref.shape[0]
    sent_ref[...] = sums[pl.ds(pl.multiple_of((1 - place_ref[1]) * half, half), half), :]
    kept_ref[...] = sums[pl.ds(pl.multiple_of(place_ref[1] * half, half), half), :]


def normalize(value):
    center = value - jnp.mean(value, axis=-1, keepdims=True)
    spread = lax.rsqrt(jnp.mean(center * center, axis=-1, keepdims=True) + 1e-05)
    return center * spread, spread


def normalize_back(grad, normed, spread, gain):
    scaled = grad * gain
    inner = jnp.mean(scaled * normed, axis=-1, keepdims=True)
    return (scaled - jnp.mean(scaled, axis=-1, keepdims=True) - normed * inner) * spread


def total_rows(value):
    return jnp.sum(value, axis=0, keepdims=True)


def cut_items(value):
    blank = jnp.zeros((LANES - SPAN, value.shape[1]), value.dtype)
    return [jnp.concatenate([value[at : at + SPAN], blank], axis=0) for at in range(0, value.shape[0], SPAN)]


def join_items(pieces):
    return jnp.concatenate([one[:SPAN] for one in pieces], axis=0)


def self_probs(keys, qt_block):
    scores = mm(keys, qt_block)
    scores = jnp.where(iota(scores.shape, 0) < SPAN, scores, FAR)
    expo = jnp.exp(scores - jnp.max(scores, axis=0, keepdims=True))
    return expo / jnp.sum(expo, axis=0, keepdims=True)


def own_blocks(both):
    return jnp.concatenate([both[:HEAD, :LANES], both[HEAD:, LANES:]], axis=0)


def token_forward_kernel(
    place_ref, tokens_ref, embed_ref,
    wq_own, wk_own, wv_own, cwq_own, wo_own, part_ref, rest_ref, bias_own, bias_other, so_bias, gain_ref, shift_ref,
    q_ref, k_ref, v_ref, mix_ref, resid_ref, normed_ref, qt_ref,
    wq, wk, wv, wo, cwq,
):
    @pl.when(pl.program_id(0) == 0)
    def _():
        assemble_token(wq, wk, wv, cwq, wo, wq_own, wk_own, wv_own, cwq_own, wo_own, part_ref, rest_ref, place_ref)

    width = wq.shape[1]
    half = width // 2
    bias = lambda line, lane: jnp.concatenate(bias_of(place_ref, bias_own, bias_other, line, lane, half), axis=1)
    tokens = tokens_ref[...]
    items = tokens.shape[0] // SPAN
    query_pos = jnp.concatenate([embed_ref[...]] * items, axis=0)
    tokens_wide = tokens.astype(F32)
    shared_in = (tokens_wide + query_pos).astype(BF)
    q = (mm(shared_in, wq[...]) + bias(0, 0)).astype(BF)
    k = mm(shared_in, wk[...]).astype(BF)
    v = (mm(tokens, wv[...]) + bias(0, half)).astype(BF)
    q_ref[...], k_ref[...], v_ref[...] = q, k, v
    q_items, k_items, v_items = (cut_items(one.astype(F32)) for one in (q, k, v))
    mixes = []
    for item in range(items):
        qt = jnp.transpose(q_items[item] * SCALE).astype(BF)
        keys, values = k_items[item].astype(BF), v_items[item].astype(BF)
        mixed = []
        for at in range(0, width, PAIR):
            probs = self_probs(keys[:, at : at + PAIR], block_rows(qt[at : at + PAIR]))
            mixed.append(own_blocks(mm_tn(values[:, at : at + PAIR], probs.astype(BF))))
        mixes.append(jnp.transpose(jnp.concatenate(mixed, axis=0)))
    mix = join_items(mixes).astype(BF)
    mix_ref[...] = mix
    resid = tokens_wide + (mm(mix, wo[...]) + so_bias[...])
    resid_ref[...] = resid
    normed, _ = normalize(resid)
    normed = normed * gain_ref[...] + shift_ref[...]
    normed_ref[...] = normed
    cross_in = (normed + query_pos).astype(BF)
    cross_q = (mm(cross_in, cwq[...]) + bias(1, 0)).astype(BF).astype(F32) * SCALE
    for item, one in enumerate(cut_items(cross_q)):
        qt_ref[item] = jnp.transpose(one).astype(BF)


def token_forward(place, tokens, embed, weights, part, rest, bias_own, bias_other, so_bias, gain, shift, rows):
    token_count, feature = tokens.shape
    width = 2 * weights[0].shape[1]
    size = token_count // rows
    items = size // SPAN
    slab = lambda columns: pl.BlockSpec((size, columns), lambda r, *_: (r, 0))
    flat = [*weights, part, rest]
    fixed = [bias_own, bias_other, so_bias, gain, shift]
    return pl.pallas_call(
        token_forward_kernel,
        grid_spec=pltpu.PrefetchScalarGridSpec(
            num_scalar_prefetch=1,
            grid=(rows,),
            in_specs=[slab(feature), whole_spec(embed)] + [whole_spec(one) for one in flat + fixed],
            out_specs=[slab(width)] * 4 + [slab(feature)] * 2 + [pl.BlockSpec((items, width, LANES), lambda r, *_: (r, 0, 0))],
            scratch_shapes=[pltpu.VMEM((feature, width), BF)] * 3 + [pltpu.VMEM((width, feature), BF), pltpu.VMEM((feature, width), BF)],
        ),
        out_shape=[jax.ShapeDtypeStruct((token_count, width), BF)] * 4
        + [jax.ShapeDtypeStruct((token_count, feature), F32)] * 2
        + [jax.ShapeDtypeStruct((rows * items, width, LANES), BF)],
        compiler_params=pltpu.CompilerParams(vmem_limit_bytes=VMEM),
        name="token_forward",
    )(place, tokens, embed, *flat, *fixed)


def gelu_both(pre):
    inner = math.sqrt(2.0 / math.pi)
    square = pre * pre
    bend = jnp.tanh(pre * (inner + (inner * 0.044715) * square))
    lift = 0.5 + 0.5 * bend
    slope = lift + (0.5 * pre) * (1.0 - bend * bend) * (inner + (3.0 * inner * 0.044715) * square)
    return pre * lift, slope


def feed_kernel(
    place_ref, mix_in_ref, normed_one_ref, cotangent_ref,
    wo_own, w1_own, w2_own, token_part, token_rest, part_ref, rest_ref, bias_own, bias_other,
    co_bias, gain2_ref, shift2_ref, f_bias, gain3_ref, shift3_ref,
    out_ref, grad_two_ref, gt_ref, sums_ref,
    wo, w1, w2, hidden, slope, low_pre, mix_scr, w1_acc, w2_acc, wo_acc, b1_acc, vec_acc,
):
    row = pl.program_id(0)
    mine = place_ref[0]
    columns = wo_acc.shape[0]
    width = wo.shape[0]
    size = out_ref.shape[0]
    hidden_half = w1.shape[1]

    @pl.when(row == 0)
    def _():
        assemble(wo, wo_own, token_part, token_rest, (wo.shape[1] + columns // 2, 0), place_ref, 0)
        assemble(w1, w1_own, part_ref, rest_ref, (0, 0), place_ref, 2)
        assemble(w2, w2_own, part_ref, rest_ref, (hidden_half // 2, 0), place_ref, 2)
        for acc in (w1_acc, w2_acc, wo_acc, b1_acc, vec_acc):
            acc[...] = jnp.zeros_like(acc)

    mix = join_items([mix_in_ref[item].astype(F32) for item in range(mix_in_ref.shape[0])]).astype(BF)
    mix_scr[...] = mix
    normed2, spread2 = normalize(normed_one_ref[...] + (mm(mix, wo[...]) + co_bias[...]))
    normed_two = normed2 * gain2_ref[...] + shift2_ref[...]
    feed_in = normed_two.astype(BF)
    b1 = bias_of(place_ref, bias_own, bias_other, 2, 0, hidden_half)
    total = normed_two + f_bias[...]
    for part in range(2):
        one, rise = gelu_both(mm_nt(feed_in, w1[part]) + b1[part])
        hidden[part] = one.astype(BF)
        slope[part] = rise
        total = total + mm(hidden[part], w2[part])
    normed3, spread3 = normalize(total)
    out_ref[...] = (normed3 * gain3_ref[...] + shift3_ref[...]).astype(BF)
    cotangent = cotangent_ref[...].astype(F32)
    grad_three = normalize_back(cotangent, normed3, spread3, gain3_ref[...])
    low_three = grad_three.astype(BF)
    back = grad_three
    for part in range(2):
        low = (mm_nt(low_three, w2[part]) * slope[part]).astype(BF)
        low_pre[part] = low
        back = back + mm(low, w1[part])
    grad_two = normalize_back(back, normed2, spread2, gain2_ref[...])
    grad_two_ref[...] = grad_two
    low_two = grad_two.astype(BF)
    own_pre = low_pre[mine]
    w2_acc[...] += mm_tn(hidden[mine], low_three)
    w1_acc[...] += mm_tn(own_pre, feed_in)
    b1_acc[...] += total_rows(own_pre.astype(F32))
    if columns == width:
        own = slice(None)
    else:
        own = pl.ds(pl.multiple_of(mine * columns, columns), columns)
    wo_acc[...] += mm_tn(mix_scr[:, own], low_two)
    vec_acc[...] += jnp.concatenate(
        [
            total_rows(cotangent * normed3), total_rows(cotangent), total_rows(low_three.astype(F32)),
            total_rows(back * normed2), total_rows(back), total_rows(low_two.astype(F32)),
            jnp.zeros((2, vec_acc.shape[1]), F32),
        ],
        axis=0,
    )
    grad_mix = mm_nt(low_two, wo[...]).astype(BF).astype(F32)
    for item, one in enumerate(cut_items(grad_mix)):
        gt_ref[item] = jnp.transpose(one).astype(BF)

    @pl.when(row == pl.num_programs(0) - 1)
    def _():
        sums_ref[:hidden_half, :] = w1_acc[...].astype(BF)
        sums_ref[hidden_half : 2 * hidden_half, :] = w2_acc[...].astype(BF)
        sums_ref[2 * hidden_half : 2 * hidden_half + columns, :] = wo_acc[...].astype(BF)
        feature = vec_acc.shape[1]
        lines = [b1_acc[:, at : at + feature] for at in range(0, hidden_half, feature)]
        lines[-1] = jnp.concatenate([lines[-1], jnp.zeros((1, feature - lines[-1].shape[1]), F32)], axis=1)
        lines.append(jnp.zeros((FEED_LINES - 8 - len(lines), feature), F32))
        sums_ref[2 * hidden_half + columns :, :] = jnp.concatenate([vec_acc[...], *lines], axis=0).astype(BF)


def feed(place, mix, normed_one, cotangent, weights, parts, bias_own, bias_other, vectors, rows, columns):
    token_count, feature = normed_one.shape
    width = mix.shape[2]
    size = token_count // rows
    items = size // SPAN
    hidden_half = weights[1].shape[0]
    lines = 2 * hidden_half + columns + FEED_LINES
    slab = lambda columns: pl.BlockSpec((size, columns), lambda r, *_: (r, 0))
    whole = lambda shape: pl.BlockSpec(shape, lambda r, *_: (0,) * len(shape))
    flat = [*weights, *parts]
    fixed = [bias_own, bias_other, *vectors]
    return pl.pallas_call(
        feed_kernel,
        grid_spec=pltpu.PrefetchScalarGridSpec(
            num_scalar_prefetch=1,
            grid=(rows,),
            in_specs=[pl.BlockSpec((items, LANES, width), lambda r, *_: (r, 0, 0)), slab(feature), slab(feature)]
            + [whole_spec(one) for one in flat + fixed],
            out_specs=[
                slab(feature), slab(feature), pl.BlockSpec((items, width, LANES), lambda r, *_: (r, 0, 0)),
                whole((lines, feature)),
            ],
            scratch_shapes=[
                pltpu.VMEM((width, feature), BF),
                pltpu.VMEM((2, hidden_half, feature), BF),
                pltpu.VMEM((2, hidden_half, feature), BF),
                pltpu.VMEM((2, size, hidden_half), BF),
                pltpu.VMEM((2, size, hidden_half), F32),
                pltpu.VMEM((2, size, hidden_half), BF),
                pltpu.VMEM((size, width), BF),
                pltpu.VMEM((hidden_half, feature), F32),
                pltpu.VMEM((hidden_half, feature), F32),
                pltpu.VMEM((columns, feature), F32),
                pltpu.VMEM((1, hidden_half), F32),
                pltpu.VMEM((8, feature), F32),
            ],
        ),
        out_shape=[
            jax.ShapeDtypeStruct((token_count, feature), BF),
            jax.ShapeDtypeStruct((token_count, feature), F32),
            jax.ShapeDtypeStruct((rows * items, width, LANES), BF),
            jax.ShapeDtypeStruct((lines, feature), BF),
        ],
        compiler_params=pltpu.CompilerParams(vmem_limit_bytes=VMEM),
        name="feed",
    )(place, mix, normed_one, cotangent, *flat, *fixed)


def token_backward_kernel(
    place_ref, dq_in_ref, grad_two_ref, resid_ref, normed_ref, tokens_ref, embed_ref, q_ref, k_ref, v_ref, mix_ref,
    memory_sums_ref, memory_vec_ref,
    wq_own, wk_own, wv_own, cwq_own, wo_own, part_ref, rest_ref, gain_ref,
    grad_tokens_ref, sent_ref, kept_ref,
    wq, wk, wv, wo, cwq, cross_dq, low_q, low_k, low_v, cwq_acc, wq_acc, wk_acc, wv_acc, wo_acc, embed_acc, vec_acc, sums,
):
    row = pl.program_id(0)
    mine = place_ref[0]
    width = wq.shape[1]
    columns = wo_acc.shape[0]

    @pl.when(row == 0)
    def _():
        assemble_token(wq, wk, wv, cwq, wo, wq_own, wk_own, wv_own, cwq_own, wo_own, part_ref, rest_ref, place_ref)
        for acc in (cwq_acc, wq_acc, wk_acc, wv_acc, wo_acc, embed_acc, vec_acc):
            acc[...] = jnp.zeros_like(acc)

    if columns == width:
        own = slice(None)
    else:
        own = pl.ds(pl.multiple_of(mine * columns, columns), columns)
    tokens = tokens_ref[...]
    items = tokens.shape[0] // SPAN
    query_pos = jnp.concatenate([embed_ref[...]] * items, axis=0)
    shared_in = (tokens.astype(F32) + query_pos).astype(BF)
    cross_in = (normed_ref[...] + query_pos).astype(BF)
    cross_dq[...] = join_items([dq_in_ref[item].astype(F32) for item in range(items)]).astype(BF)
    cwq_acc[...] += mm_tn(cross_in, cross_dq[:, own])
    grad_cross_in = mm_nt(cross_dq[...], cwq[...])
    back = grad_two_ref[...] + grad_cross_in
    normed, spread = normalize(resid_ref[...])
    grad_one = normalize_back(back, normed, spread, gain_ref[...])
    low_one = grad_one.astype(BF)
    wo_acc[...] += mm_tn(mix_ref[:, own], low_one)
    g_items = cut_items(mm_nt(low_one, wo[...]).astype(BF).astype(F32))
    q_items = cut_items(q_ref[...].astype(F32) * SCALE)
    k_items, v_items = cut_items(k_ref[...].astype(F32)), cut_items(v_ref[...].astype(F32))
    all_dq, all_dk, all_dv = [], [], []
    for item in range(items):
        qt, gt = jnp.transpose(q_items[item]).astype(BF), jnp.transpose(g_items[item]).astype(BF)
        qn, gn, keys, values = (one[item].astype(BF) for one in (q_items, g_items, k_items, v_items))
        one_dq, one_dk, one_dv = [], [], []
        for at in range(0, width, PAIR):
            here = slice(at, at + PAIR)
            probs = self_probs(keys[:, here], block_rows(qt[here]))
            slopes = mm(values[:, here], block_rows(gt[here]))
            inner = jnp.sum(probs * slopes, axis=0, keepdims=True)
            low = (probs * (slopes - inner)).astype(BF)
            one_dv.append(mm(probs.astype(BF), block_columns(gn[:, here])))
            one_dk.append(mm(low, block_columns(qn[:, here])))
            one_dq.append(own_blocks(mm_tn(keys[:, here], low)))
        all_dq.append(jnp.transpose(jnp.concatenate(one_dq, axis=0) * SCALE))
        all_dk.append(jnp.concatenate(one_dk, axis=1))
        all_dv.append(jnp.concatenate(one_dv, axis=1))
    low_q[...] = join_items(all_dq).astype(BF)
    low_k[...] = join_items(all_dk).astype(BF)
    low_v[...] = join_items(all_dv).astype(BF)
    wq_acc[...] += mm_tn(shared_in, low_q[:, own])
    wk_acc[...] += mm_tn(shared_in, low_k[:, own])
    wv_acc[...] += mm_tn(tokens, low_v[:, own])
    grad_shared = mm_nt(low_q[...], wq[...]) + mm_nt(low_k[...], wk[...])
    grad_tokens_ref[...] = grad_one + grad_shared + mm_nt(low_v[...], wv[...])
    position = grad_shared + grad_cross_in
    embed_acc[...] += sum(position[at : at + SPAN] for at in range(0, position.shape[0], SPAN))
    vec_acc[...] += jnp.concatenate(
        [
            total_rows(back * normed), total_rows(back), total_rows(low_one.astype(F32)),
            total_rows(cross_dq[...].astype(F32)), total_rows(low_q[...].astype(F32)), total_rows(low_v[...].astype(F32)),
            jnp.zeros((2, width), F32),
        ],
        axis=0,
    )

    @pl.when(row == pl.num_programs(0) - 1)
    def _():
        feature = wq_acc.shape[0]
        for at, (one, two) in enumerate(((wq_acc, wk_acc), (wv_acc, cwq_acc))):
            sums[at * feature : (at + 1) * feature, :columns] = one[...].astype(BF)
            sums[at * feature : (at + 1) * feature, columns:] = two[...].astype(BF)
        sums[2 * feature : 3 * feature, :] = memory_sums_ref[...]
        sums[3 * feature : 3 * feature + columns, :] = wo_acc[...].astype(BF)
        at = 3 * feature + columns
        sums[at : at + LANES, :] = jnp.concatenate([embed_acc[...], jnp.zeros((LANES - SPAN, width), F32)], axis=0).astype(BF)
        vectors = jnp.concatenate([vec_acc[...], memory_vec_ref[...], jnp.zeros((7, width), F32)], axis=0)
        sums[at + LANES : at + LANES + 16, :] = vectors.astype(BF)
        sums[at + LANES + 16 :, :] = jnp.zeros((sums.shape[0] - at - LANES - 16, width), BF)
        give_halves(place_ref, sums, sent_ref, kept_ref)


def token_backward(place, dq, grad_two, resid, normed, tokens, embed, q, k, v, mix, memory_sums, memory_vec, weights, part, rest, gain, rows, columns, lines):
    token_count, feature = tokens.shape
    width = q.shape[1]
    size = token_count // rows
    items = size // SPAN
    slab = lambda columns: pl.BlockSpec((size, columns), lambda r, *_: (r, 0))
    whole = lambda shape: pl.BlockSpec(shape, lambda r, *_: (0,) * len(shape))
    flat = [memory_sums, memory_vec, *weights, part, rest]
    grads = [(feature, columns)] * 4 + [(columns, feature)]
    return pl.pallas_call(
        token_backward_kernel,
        grid_spec=pltpu.PrefetchScalarGridSpec(
            num_scalar_prefetch=1,
            grid=(rows,),
            in_specs=[pl.BlockSpec((items, LANES, width), lambda r, *_: (r, 0, 0))]
            + [slab(feature)] * 4 + [whole_spec(embed)] + [slab(width)] * 4
            + [whole_spec(one) for one in flat] + [whole_spec(gain)],
            out_specs=[slab(feature), whole((lines // 2, feature)), whole((lines // 2, feature))],
            scratch_shapes=[pltpu.VMEM((feature, width), BF)] * 3 + [pltpu.VMEM((width, feature), BF), pltpu.VMEM((feature, width), BF)]
            + [pltpu.VMEM((size, width), BF)] * 4
            + [pltpu.VMEM(one, F32) for one in grads] + [pltpu.VMEM((SPAN, feature), F32), pltpu.VMEM((8, feature), F32), pltpu.VMEM((lines, feature), BF)],
        ),
        out_shape=[jax.ShapeDtypeStruct((token_count, feature), F32)] + [jax.ShapeDtypeStruct((lines // 2, feature), BF)] * 2,
        compiler_params=pltpu.CompilerParams(vmem_limit_bytes=VMEM),
        name="token_backward",
    )(place, dq, grad_two, resid, normed, tokens, embed, q, k, v, mix, *flat, gain)


def pack_columns_kernel(place_ref, wk_ref, wv_ref, bias_ref, out_ref):
    half, columns = wk_ref.shape
    out_ref[:half, :columns] = wk_ref[...]
    out_ref[:half, columns:] = wv_ref[...]
    lines = [one.astype(F32) for one in split3(bias_ref[...])]
    lines = jnp.concatenate(lines + [jnp.zeros((BIAS_LINES - 3, columns), F32)], axis=0)
    out_ref[half:, :] = jnp.concatenate([lines, jnp.zeros_like(lines)], axis=1).astype(BF)


def pack_token_kernel(place_ref, wq_ref, wk_ref, wv_ref, cwq_ref, wo_ref, cwo_ref, out_ref):
    half, columns = wq_ref.shape
    out_ref[:half, :columns] = wq_ref[...]
    out_ref[:half, columns:] = wk_ref[...]
    out_ref[half : 2 * half, :columns] = wv_ref[...]
    out_ref[half : 2 * half, columns:] = cwq_ref[...]
    lines = wo_ref.shape[0]
    out_ref[2 * half : 2 * half + lines, :] = wo_ref[...]
    out_ref[2 * half + lines :, :] = cwo_ref[...]


def pack_lines_kernel(place_ref, w1_ref, w2_ref, out_ref):
    lines = w1_ref.shape[0]
    out_ref[:lines, :] = w1_ref[...]
    out_ref[lines:, :] = w2_ref[...]


def pack_half(kernel, bit, arrays, lines, columns):
    return pl.pallas_call(
        kernel,
        grid_spec=pltpu.PrefetchScalarGridSpec(
            num_scalar_prefetch=1, grid=(1,),
            in_specs=[
                whole_spec(one) if one.shape[0] == 1 else pl.BlockSpec((one.shape[0] // 2, one.shape[1]), lambda _, place: (place[0], 0))
                for one in arrays
            ],
            out_specs=pl.BlockSpec((lines, columns), lambda *_: (0, 0)),
        ),
        out_shape=jax.ShapeDtypeStruct((lines, columns), BF),
        compiler_params=pltpu.CompilerParams(vmem_limit_bytes=VMEM),
        name=kernel.__name__.replace("_kernel", ""),
    )(bit[None], *arrays)


def pack_bias_kernel(sbq_ref, sbv_ref, cbq_ref, cbv_ref, b1_ref, out_ref):
    columns = out_ref.shape[1]
    out_ref[...] = jnp.zeros_like(out_ref)
    size = sbq_ref.shape[1]
    out_ref[0:1, :size], out_ref[0:1, size : 2 * size] = sbq_ref[...], sbv_ref[...]
    out_ref[1:2, :size], out_ref[1:2, size : 2 * size] = cbq_ref[...], cbv_ref[...]
    for line, at in enumerate(range(0, b1_ref.shape[1], columns)):
        part = b1_ref[:, at : min(at + columns, b1_ref.shape[1])]
        out_ref[2 + line : 3 + line, : part.shape[1]] = part


def pack_bias(biases, columns):
    lines = -(-(2 + -(-biases[-1].shape[1] // columns)) // 8) * 8
    return pl.pallas_call(pack_bias_kernel, out_shape=jax.ShapeDtypeStruct((lines, columns), F32), name="pack_bias")(*biases)


def feed_unpack_kernel(hidden_half, columns, sums_ref, w1_ref, w2_ref, wo_ref, b1_ref, *vec_refs):
    w1_ref[...] = sums_ref[:hidden_half, :].astype(F32)
    w2_ref[...] = sums_ref[hidden_half : 2 * hidden_half, :].astype(F32)
    wo_ref[...] = sums_ref[2 * hidden_half : 2 * hidden_half + columns, :].astype(F32)
    vectors = sums_ref[2 * hidden_half + columns :, :].astype(F32)
    for line, one in enumerate(vec_refs):
        one[...] = vectors[line : line + 1]
    lines = -(-hidden_half // vectors.shape[1])
    b1_ref[...] = jnp.concatenate([vectors[8 + one : 9 + one] for one in range(lines)], axis=1)[:, :hidden_half]


def feed_unpack(sums, hidden_half, columns):
    feature = sums.shape[1]
    shapes = [(hidden_half, feature), (hidden_half, feature), (columns, feature), (1, hidden_half)] + [(1, feature)] * 6
    return pl.pallas_call(
        functools.partial(feed_unpack_kernel, hidden_half, columns),
        out_shape=[jax.ShapeDtypeStruct(one, F32) for one in shapes],
        compiler_params=pltpu.CompilerParams(vmem_limit_bytes=VMEM),
        name="feed_unpack",
    )(sums)


def token_unpack_kernel(
    place_ref, kept_ref, other_ref, wq_ref, wk_ref, wv_ref, cwq_ref, cwk_ref, cwv_ref, wo_ref, embed_ref,
    gain_ref, shift_ref, so_ref, cq_ref, sq_ref, sv_ref, cv_ref, sums, vectors,
):
    half = kept_ref.shape[0]
    sums[pl.ds(pl.multiple_of(place_ref[1] * half, half), half), :] = kept_ref[...]
    sums[pl.ds(pl.multiple_of((1 - place_ref[1]) * half, half), half), :] = other_ref[...]
    feature, columns = wq_ref.shape
    for at, (one, two) in enumerate(((wq_ref, wk_ref), (wv_ref, cwq_ref), (cwk_ref, cwv_ref))):
        one[...] = sums[at * feature : (at + 1) * feature, :columns].astype(F32)
        two[...] = sums[at * feature : (at + 1) * feature, columns:].astype(F32)
    wo_ref[...] = sums[3 * feature : 3 * feature + columns, :].astype(F32)
    at = 3 * feature + columns
    embed_ref[...] = sums[at : at + LANES, :].astype(F32)[:SPAN]
    vectors[...] = sums[at + LANES : at + LANES + 16, :].astype(F32)
    gain_ref[...], shift_ref[...], so_ref[...] = vectors[0:1, :], vectors[1:2, :], vectors[2:3, :]
    own = pl.ds(pl.multiple_of(place_ref[0] * columns, columns), columns)
    cq_ref[...], sq_ref[...], sv_ref[...] = vectors[3:4, own], vectors[4:5, own], vectors[5:6, own]
    cv_ref[...] = vectors[8:9, :columns]


def token_unpack(place, kept, other, feature, columns):
    half, width = kept.shape
    shapes = [(feature, columns)] * 6 + [(columns, feature), (SPAN, feature)] + [(1, feature)] * 3 + [(1, columns)] * 4
    whole = lambda shape: pl.BlockSpec(shape, lambda *_: (0, 0))
    return pl.pallas_call(
        token_unpack_kernel,
        grid_spec=pltpu.PrefetchScalarGridSpec(
            num_scalar_prefetch=1, grid=(1,),
            in_specs=[whole((half, width))] * 2,
            out_specs=[whole(one) for one in shapes],
            scratch_shapes=[pltpu.VMEM((2 * half, width), BF), pltpu.VMEM((16, width), F32)],
        ),
        out_shape=[jax.ShapeDtypeStruct(one, F32) for one in shapes],
        compiler_params=pltpu.CompilerParams(vmem_limit_bytes=VMEM),
        name="token_unpack",
    )(place, kept, other)


def after(value, *others):
    return lax.optimization_barrier((value, *others))[0]


class SumOverDp:
    def __init__(self, at, count):
        self.at, self.count = at, count
        hops = [1 << one for one in range(1, count.bit_length() - 1)]
        self.hops = list(zip(hops, hops[1:] + hops[:1]))

    def swap(self, array, by):
        return lax.ppermute(array, "dp", [(one, one ^ by) for one in range(self.count)])

    def bit(self, by):
        return (self.at // by) % 2

    def give(self, array, by):
        half = array.shape[0] // 2
        bit = self.bit(by)
        return lax.dynamic_slice_in_dim(array, (1 - bit) * half, half), lax.dynamic_slice_in_dim(array, bit * half, half)

    def add(self, kept, got):
        return (kept.astype(F32) + got.astype(F32)).astype(BF)

    def join(self, array, got, by):
        first = self.bit(by) == 0
        return jnp.concatenate([jnp.where(first, array, got), jnp.where(first, got, array)])

    def exchange(self, sent, bys, work):
        got = [self.swap(one, by) for one, by in zip(sent, bys)]
        done = work(sent)
        return got if done is None else list(lax.optimization_barrier((*got, done)))[: len(got)]

    def start(self, sent, kept, work):
        held = self.add(kept, self.swap(sent, 1))
        middle = held.shape[0] // 2
        two = [held[:middle], held[middle:]]
        for bys in self.hops:
            given = [self.give(one, by) for one, by in zip(two, bys)]
            got = self.exchange([one for one, _ in given], bys, work)
            two = [self.add(one, other) for (_, one), other in zip(given, got)]
        for bys in self.hops[:0:-1]:
            got = self.exchange(two, bys, work)
            two = [self.join(one, other, by) for one, other, by in zip(two, got, bys)]
        return tuple(two)

    def finish(self, two, work):
        bys = self.hops[0]
        got = self.exchange(two, bys, work)
        mine = jnp.concatenate([self.join(one, other, by) for one, other, by in zip(two, got, bys)])
        return mine, self.swap(mine, 1)


def solution(mesh):
    tensor, count = mesh.shape["tensor"], mesh.shape["dp"]

    def body(
        tokens, memory, mem_lengths, key_pad, query_embed,
        self_wq, self_bq, self_wk, self_wv, self_bv, self_wo, self_bo, norm1_gain, norm1_bias,
        cross_wq, cross_bq, cross_wk, cross_wv, cross_bv, cross_wo, cross_bo, norm2_gain, norm2_bias,
        ffn_w1, ffn_b1, ffn_w2, ffn_b2, norm3_gain, norm3_bias, cotangent,
    ):
        rank, at = lax.axis_index("tensor"), lax.axis_index("dp")
        side = (rank * 2 // tensor).astype(jnp.int32)
        bit = (at % 2).astype(jnp.int32)
        place = jnp.stack([side, bit])
        own_columns, own_hidden = self_wq.shape[1], ffn_w1.shape[1]
        feature = tokens.shape[1]
        columns, hidden_half = own_columns * tensor // 2, own_hidden * tensor // 2
        rows = mem_lengths.shape[0]
        direct = tensor == 2 and count > 1
        as_row = lambda one: one.reshape(1, -1)

        def two_halves(part, dim):
            if direct:
                return part, part
            full = lax.all_gather(part, "tensor", axis=dim, tiled=True)
            size = full.shape[dim] // 2
            cut = lambda which: lax.dynamic_slice_in_dim(full, which * size, size, axis=dim)
            return cut(side), cut(1 - side)

        def crossing(kernel, others, lines, sent, then):
            crossed = lax.ppermute(sent, "tensor", [(0, 1), (1, 0)]) if direct else sent
            return passing_on(kernel, others, lines, crossed, then)

        def passing_on(kernel, others, lines, crossed, then):
            if not direct:
                return crossed, pack_half(kernel, 1 - bit, others, lines, feature)
            return crossed, lax.ppermute(after(crossed, then), "dp", [(one, one ^ 1) for one in range(count)])

        cwk, cwv = two_halves(cross_wk, 1), two_halves(cross_wv, 1)
        swq, swk, swv, cwq = (two_halves(one, 1) for one in (self_wq, self_wk, self_wv, cross_wq))
        swo, cwo = two_halves(self_wo, 0), two_halves(cross_wo, 0)
        w1, w2 = two_halves(jnp.transpose(ffn_w1), 0), two_halves(ffn_w2, 0)
        biases = [two_halves(one, 0) for one in (self_bq, self_bv, cross_bq, cross_bv, ffn_b1)]
        memory_others = [cwk[1], cwv[1], as_row(biases[3][1])]
        memory_sent = pack_half(pack_columns_kernel, bit, memory_others, feature // 2 + BIAS_LINES, feature)
        bias_own = pack_bias([after(as_row(biases[0][0]), memory_sent)] + [as_row(own) for own, _ in biases[1:]], feature)
        if direct:
            bias_other = lax.ppermute(bias_own, "tensor", [(0, 1), (1, 0)])
        else:
            bias_other = pack_bias([as_row(other) for _, other in biases], feature)
        token_sent = pack_half(
            pack_token_kernel, bit, [after(swq[1], bias_own)] + [one[1] for one in (swk, swv, cwq, swo, cwo)], feature + columns, feature
        )
        memory_part, memory_rest = crossing(pack_columns_kernel, memory_others, feature // 2 + BIAS_LINES, memory_sent, token_sent)
        token_sent = after(token_sent, memory_part, bias_other)
        token_crossed = lax.ppermute(token_sent, "tensor", [(0, 1), (1, 0)]) if direct else token_sent
        outputs, feed_sent = None, None
        for row in range(rows):
            outputs = keys_values(
                mem_lengths, place, memory if feed_sent is None else after(memory, feed_sent), key_pad,
                cwk[0], cwv[0], memory_part, memory_rest, as_row(biases[3][0]), row, outputs,
            )
            if feed_sent is None:
                feed_sent = pack_half(pack_lines_kernel, bit, [after(w1[1], outputs[1], token_crossed), w2[1]], hidden_half, feature)
        memory_in, gate, cross_keys, cross_values, cwk_full, cwv_full = outputs
        token_part, token_rest = passing_on(
            pack_token_kernel, [one[1] for one in (swq, swk, swv, cwq, swo, cwo)], feature + columns, token_crossed, gate
        )
        token_weights = [one[0] for one in (swq, swk, swv, cwq, swo)]
        q, k, v, self_mix, resid_one, normed_one, qt = token_forward(
            place, tokens, query_embed, token_weights, token_part, token_rest, bias_own, bias_other,
            as_row(self_bo), as_row(norm1_gain), as_row(norm1_bias), 1,
        )
        mix, mixt, lse = cross_forward(mem_lengths, cross_keys, cross_values, gate, qt)
        feed_part, feed_rest = crossing(pack_lines_kernel, [w1[1], w2[1]], hidden_half, feed_sent, lse)
        layer_out, grad_two, gt, feed_sums = feed(
            place, mix, normed_one, cotangent, [cwo[0], w1[0], w2[0]], [token_part, token_rest, feed_part, feed_rest],
            bias_own, bias_other,
            [as_row(one) for one in (cross_bo, norm2_gain, norm2_bias, ffn_b2, norm3_gain, norm3_bias)], rows, columns,
        )
        multiple = 32 * count
        lines = -(-(3 * feature + columns + LANES + 16) // multiple) * multiple

        def backward():
            dk, dv, dq = cross_backward(mem_lengths, cross_keys, cross_values, gate, qt, gt, mixt, lse)
            memory_sums, memory_vec = memory_weights(place, dk, dv, memory, memory_in, columns)
            grad_tokens, sent, kept = token_backward(
                place, dq, grad_two, resid_one, normed_one, tokens, query_embed, q, k, v, self_mix, memory_sums, memory_vec,
                token_weights, token_part, token_rest, as_row(norm1_gain), 1, columns, lines,
            )
            pieces, given = 2, []

            def piece(sent):
                if len(given) == pieces:
                    return None
                held = given[-1] if given else None
                given.append(memory_gradient(after(dk, *sent), dv, cwk_full, cwv_full, len(given), pieces, held))
                return given[-1]

            state = token_sum.start(sent, kept, piece) if summed else (sent, kept)
            while len(given) < pieces:
                piece([])
            return grad_tokens, given[-1], *state

        summed = count > 2
        token_sum = SumOverDp(at, count)
        feed_total = lax.psum(feed_sums, "dp")
        shapes = jax.eval_shape(backward)
        grad_tokens, grad_memory, *state = lax.cond(
            at < count * rows, backward, lambda: tuple(jnp.zeros(one.shape, one.dtype) for one in shapes)
        )
        feed_grads = []

        def unpack_feed(sent):
            feed_grads.extend(feed_unpack(after(feed_total, *sent), hidden_half, columns))
            return feed_grads[0]

        if summed:
            kept, other = token_sum.finish(state, unpack_feed)
        else:
            other, kept = state
            unpack_feed([])
        g_sq, g_sk, g_sv, g_cq, g_ck, g_cv, g_so, g_embed, g_n1g, g_n1b, g_sbo, g_cbq, g_sbq, g_sbv, g_cbv = token_unpack(
            place, kept, other, feature, columns
        )
        g_w1t, g_w2, g_co, g_b1, g_n3g, g_n3b, g_b2, g_n2g, g_n2b, g_cbo = feed_grads

        def share(array, dim, size):
            if array.shape[dim] == size:
                return array
            return lax.dynamic_slice_in_dim(array, rank % (tensor // 2) * size, size, axis=dim)

        lanes = lambda array: share(array, 1, own_columns)
        bias = lambda array: share(array, 1, own_columns).reshape(-1)
        vector = lambda array: array.reshape(-1)
        return (
            layer_out, grad_tokens, grad_memory, g_embed,
            lanes(g_sq), bias(g_sbq), lanes(g_sk), lanes(g_sv), bias(g_sbv), share(g_so, 0, own_columns),
            vector(g_sbo), vector(g_n1g), vector(g_n1b),
            lanes(g_cq), bias(g_cbq), lanes(g_ck), lanes(g_cv), bias(g_cbv), share(g_co, 0, own_columns),
            vector(g_cbo), vector(g_n2g), vector(g_n2b),
            jnp.transpose(share(g_w1t, 0, own_hidden)), share(g_b1, 1, own_hidden).reshape(-1), share(g_w2, 0, own_hidden),
            vector(g_b2), vector(g_n3g), vector(g_n3b),
        )

    rep, by_row, by_col, by_first = P(), P("dp", None), P(None, "tensor"), P("tensor", None)
    one_dim = P("tensor")
    return jax.shard_map(
        body,
        mesh=mesh,
        in_specs=(
            by_row, by_row, by_row, by_row, rep,
            by_col, one_dim, by_col, by_col, one_dim, by_first, rep, rep, rep,
            by_col, one_dim, by_col, by_col, one_dim, by_first, rep, rep, rep,
            by_col, one_dim, by_first, rep, rep, rep, by_row,
        ),
        out_specs=(
            by_row, by_row, by_row, rep,
            by_col, one_dim, by_col, by_col, one_dim, by_first, rep, rep, rep,
            by_col, one_dim, by_col, by_col, one_dim, by_first, rep, rep, rep,
            by_col, one_dim, by_first, rep, rep, rep,
        ),
        check_vma=False,
    )
```

```python
import functools
import math

import jax
import jax.numpy as jnp
import numpy as np
from jax import lax
from jax.experimental import pallas as pl
from jax.experimental.pallas import tpu as pltpu
from jax.sharding import PartitionSpec as P

HEAD = 64
SPAN = 100
MEM_MOST = 1200
LANES = 128
PAIR = 2 * HEAD
TILE = 256
BLOCK = 1024
SUMS_BLOCK = 2048
SHARES = (3, 2, 1, 1, 1)
WINDOW = -(-(MEM_MOST + 15) // 32) * 32
FAR = -1.0e9
CHUNKS = 4
LUMP = 256
BIAS_LINES = 16
FEED_LINES = 16
SCALE = 1.0 / math.sqrt(HEAD)
VMEM = 60 << 20
BF = jnp.bfloat16
F32 = jnp.float32


def mm(left, right):
    return jnp.dot(left, right, preferred_element_type=F32)


def mm_tn(left, right):
    return lax.dot_general(left, right, (((0,), (0,)), ((), ())), preferred_element_type=F32)


def mm_nt(left, right):
    return lax.dot_general(left, right, (((1,), (1,)), ((), ())), preferred_element_type=F32)


def split3(value):
    top = value.astype(BF)
    rest = value - top.astype(F32)
    middle = rest.astype(BF)
    return top, middle, (rest - middle.astype(F32)).astype(BF)


def iota(shape, dim):
    return lax.broadcasted_iota(jnp.int32, shape, dim)


def whole_spec(array):
    return pl.BlockSpec(array.shape, lambda *_: (0,) * array.ndim)


def rates_of(feature):
    lane = np.arange(feature)
    rates = np.exp((lane // 2).astype(np.float32) * np.float32(-2.0 * math.log(10000.0) / feature)).astype(np.float32)
    return rates, np.where(lane % 2 == 1, 0.5 * math.pi, 0.0).astype(np.float32)


def bounds_of(lengths_ref, row):
    starts, ends, at = [], [], jnp.int32(0)
    for item in range(lengths_ref.shape[1]):
        starts.append(at)
        at = at + lengths_ref[row, item]
        ends.append(at)
    return starts, ends


def keys_values_kernel(
    first_block, row_blocks, lengths_ref, place_ref,
    memory_ref, pad_ref, angles_ref, local_sin_ref, local_cos_ref, wk_own, wv_own, part_ref, rest_ref, bias_ref, *refs,
):
    memory_in_ref, gate_ref, keys_ref, values_ref, wk_ref, wv_ref = refs[-6:]
    block = pl.program_id(0) + first_block
    row, block = block // row_blocks, lax.rem(block, row_blocks)
    parts = memory_ref.shape[0] // TILE
    items = lengths_ref.shape[1]
    columns = wk_own.shape[1]

    @pl.when(pl.program_id(0) == 0)
    def _():
        assemble(wk_ref, wk_own, part_ref, rest_ref, (0, 0), place_ref, 1)
        assemble(wv_ref, wv_own, part_ref, rest_ref, (0, columns), place_ref, 1)

    starts, ends = bounds_of(lengths_ref, row)
    lane = iota((TILE, LANES), 1)
    lane_starts, lane_ends = (
        sum(jnp.where(iota((1, LANES), 1) == item, one, 0) for item, one in enumerate(ones)) for ones in (starts, ends)
    )
    tiles, crowded = [], jnp.bool_(False)
    for part in range(parts):
        base = (block * parts + part) * TILE
        here = slice(part * TILE, (part + 1) * TILE)
        first = sum((one <= base).astype(jnp.int32) for one in ends)
        last = sum((one < base + TILE).astype(jnp.int32) for one in starts) - 1

        def start_of(item):
            return sum(jnp.where(item == index, one, 0) for index, one in enumerate(starts))

        def place(item, base=base):
            shift = (base - start_of(item)).astype(F32)
            angle = shift * angles_ref[0:1, :] + angles_ref[1:2, :]
            return jnp.sin(angle) * local_cos_ref[...] + jnp.cos(angle) * local_sin_ref[...]

        def later(item, held, base=base, place=place):
            return jnp.where(iota((TILE, 1), 0) + base >= start_of(item), place(item), held)

        position = later(jnp.minimum(first + 1, items - 1), place(first))
        memory_in_ref[here, :] = (memory_ref[here, :].astype(F32) + position).astype(BF)
        tiles.append((here, base, first, last, place, start_of))
        crowded = crowded | (last > first + 1)
    own_bias, line = bias_ref[...], part_ref.shape[0] - BIAS_LINES
    lines = part_ref[line : line + BIAS_LINES, :columns].astype(F32)
    other_bias = lines[0:1] + lines[1:2] + lines[2:3]
    low = place_ref[0] == 0
    biases = jnp.where(low, own_bias, other_bias), jnp.where(low, other_bias, own_bias)
    for half in range(2):
        here = slice(half * columns, (half + 1) * columns)
        values_ref[half] = (mm(memory_ref[...], wv_ref[:, here]) + biases[half]).astype(BF)
    for half in range(2):
        here = slice(half * columns, (half + 1) * columns)
        keys_ref[half] = mm(memory_in_ref[...], wk_ref[:, here]).astype(BF)
    for here, base, *_ in tiles:
        pad = jnp.transpose(jnp.broadcast_to(pad_ref[pl.ds(row, 1), here].astype(F32), (LANES, TILE)))
        slot_grid = iota((TILE, LANES), 0) + base
        mine = (slot_grid >= lane_starts) & (slot_grid < lane_ends)
        is_open = mine & ((pad > 0.0) | (slot_grid == lane_starts))
        gate = jnp.where(lane < items, jnp.where(is_open, 0.0, 1.0), jnp.where(lane < items + 3, 1.0, 0.0))
        gate_ref[here, :] = gate.astype(BF)

    @pl.when(crowded)
    def _():
        for here, base, first, last, place, start_of in tiles:

            def patch(item, carry, here=here, base=base, place=place, start_of=start_of):
                with_place = (memory_ref[here, :].astype(F32) + place(item)).astype(BF)
                slots = iota((TILE, 1), 0) + base
                memory_in_ref[here, :] = jnp.where(slots >= start_of(item), with_place, memory_in_ref[here, :])
                return carry

            lax.fori_loop(first + 2, last + 1, patch, 0)
        for half in range(2):
            keys_ref[half] = mm(memory_in_ref[...], wk_ref[:, half * columns : (half + 1) * columns]).astype(BF)


def keys_values(lengths, place, memory, key_pad, wk_own, wv_own, part, rest, bias, first, blocks, held):
    rows, slots = key_pad.shape
    total, feature = memory.shape
    columns = wk_own.shape[1]
    steps = slots // BLOCK
    rates, turn = rates_of(feature)
    local = np.arange(TILE)[:, None] * rates.astype(np.float64)
    fixed = [jnp.asarray(np.stack([rates, turn])), jnp.asarray(np.sin(local).astype(np.float32)), jnp.asarray(np.cos(local).astype(np.float32))]
    fixed += [wk_own, wv_own, part, rest, bias]
    slab = lambda columns: pl.BlockSpec((BLOCK, columns), lambda t, *_: (first + t, 0))
    halves = pl.BlockSpec((2, BLOCK, columns), lambda t, *_: (0, first + t, 0))
    full = pl.BlockSpec((feature, 2 * columns), lambda *_: (0, 0))
    held = [] if held is None else list(held)
    return pl.pallas_call(
        functools.partial(keys_values_kernel, first, steps),
        grid_spec=pltpu.PrefetchScalarGridSpec(
            num_scalar_prefetch=2,
            grid=(blocks,),
            in_specs=[slab(feature), pl.BlockSpec((rows, BLOCK), lambda t, *_: (0, lax.rem(first + t, steps)))] + [whole_spec(one) for one in fixed]
            + [pl.BlockSpec(memory_space=pl.ANY)] * len(held),
            out_specs=[slab(feature), slab(LANES), halves, halves, full, full],
        ),
        out_shape=[
            jax.ShapeDtypeStruct((total, feature), BF),
            jax.ShapeDtypeStruct((total, LANES), BF),
            jax.ShapeDtypeStruct((2, total, columns), BF),
            jax.ShapeDtypeStruct((2, total, columns), BF),
            jax.ShapeDtypeStruct((feature, 2 * columns), BF),
            jax.ShapeDtypeStruct((feature, 2 * columns), BF),
        ],
        input_output_aliases={4 + len(fixed) + one: one for one in range(len(held))},
        compiler_params=pltpu.CompilerParams(vmem_limit_bytes=VMEM),
        name="keys_values",
    )(lengths, place, memory, key_pad, *fixed, *held)


def block_rows(pair_transposed):
    blank = jnp.zeros((HEAD, pair_transposed.shape[1]), BF)
    upper = jnp.concatenate([pair_transposed[:HEAD], blank], axis=1)
    lower = jnp.concatenate([blank, pair_transposed[HEAD:]], axis=1)
    return jnp.concatenate([upper, lower], axis=0)


def block_columns(pair):
    twice = jnp.concatenate([pair, pair], axis=0)
    same = (iota(twice.shape, 0) < pair.shape[0]) == (iota(twice.shape, 1) < HEAD)
    return jnp.where(same, twice, jnp.zeros_like(twice))


def gate_rows(item, items, closed, added):
    row = iota((LANES, 2 * LANES), 0)
    value = jnp.where(row == item, closed, 0.0)
    if added is not None:
        for place, part in enumerate(split3(added)):
            value = jnp.where(row == items + place, part.astype(F32), value)
    return value.astype(BF)


def window_of(start, slots):
    return pl.multiple_of(jnp.minimum((start // 16) * 16, slots - WINDOW), 16)


def cross_forward_kernel(lengths_ref, keys_ref, values_ref, gate_ref, qt_ref, mix_ref, mixt_ref, lse_ref, scores_a, scores_b, probs_a, probs_b):
    row = pl.program_id(0)
    slots = keys_ref.shape[0]
    items = lengths_ref.shape[1]
    starts, ends = bounds_of(lengths_ref, row)
    works = [(item, pair) for pair in range(keys_ref.shape[1] // PAIR) for item in range(items)]
    scores_of, probs_of = (scores_a, scores_b), (probs_a, probs_b)
    largest, total = {}, {}
    size = WINDOW // CHUNKS

    def lanes(pair):
        return slice(pair * PAIR, (pair + 1) * PAIR)

    def prepare(work):
        item, pair = works[work]
        return jnp.concatenate([block_rows(qt_ref[item, lanes(pair), :]), gate_rows(item, items, FAR, None)], axis=0)

    def score(work, right, chunk):
        item, pair = works[work]
        rows = pl.ds(pl.multiple_of(window_of(starts[item], slots) + chunk * size, 16), size)
        part = mm(jnp.concatenate([keys_ref[rows, lanes(pair)], gate_ref[rows, :]], axis=1), right)
        scores_of[work % 2][chunk * size : (chunk + 1) * size, :] = part
        top = jnp.max(part.reshape(size // 8, 8, 2 * LANES), axis=0)
        largest[work] = top if chunk == 0 else jnp.maximum(largest[work], top)

    def soften(work, chunk):
        if chunk == 0:
            largest[work] = jnp.max(largest[work], axis=0, keepdims=True)
        here = slice(chunk * size, (chunk + 1) * size)
        expo = jnp.exp(scores_of[work % 2][here, :] - largest[work])
        probs_of[work % 2][here, :] = expo.astype(BF)
        add = jnp.sum(expo.reshape(size // 8, 8, 2 * LANES), axis=0)
        total[work] = add if chunk == 0 else total[work] + add

    def finish(work):
        item, pair = works[work]
        rows = pl.ds(window_of(starts[item], slots), WINDOW)
        sums = jnp.sum(total[work], axis=0, keepdims=True)
        both = mm_tn(values_ref[rows, lanes(pair)], probs_of[work % 2][...]) / sums
        mixed = own_blocks(both)
        mixt_ref[item, lanes(pair), :] = mixed
        mix_ref[item, :, lanes(pair)] = jnp.transpose(mixed).astype(BF)
        lse_ref[pair, item : item + 1, :] = largest[work] + jnp.log(sums)

    for step in range(len(works) + 2):
        right = prepare(step) if step < len(works) else None
        if step >= 2:
            finish(step - 2)
        for chunk in range(CHUNKS):
            if step < len(works):
                score(step, right, chunk)
            if 1 <= step <= len(works):
                soften(step - 1, chunk)


def cross_forward(lengths, keys, values, gate, qt):
    rows, items = lengths.shape
    slots, columns = keys.shape[1] // rows, keys.shape[2]
    width = 2 * columns
    pairs = width // PAIR
    by_half = pl.BlockSpec((None, slots, columns), lambda r, p, *_: (p, r, 0))
    turned = pl.BlockSpec((items, columns, LANES), lambda r, p, *_: (r, p, 0))
    return pl.pallas_call(
        cross_forward_kernel,
        grid_spec=pltpu.PrefetchScalarGridSpec(
            num_scalar_prefetch=1,
            grid=(rows, 2),
            in_specs=[by_half, by_half, pl.BlockSpec((slots, LANES), lambda r, p, *_: (r, 0)), turned],
            out_specs=[
                pl.BlockSpec((items, LANES, columns), lambda r, p, *_: (r, 0, p)),
                turned,
                pl.BlockSpec((pairs // 2, items, 2 * LANES), lambda r, p, *_: (r * 2 + p, 0, 0)),
            ],
            scratch_shapes=[pltpu.VMEM((WINDOW, 2 * LANES), F32)] * 2 + [pltpu.VMEM((WINDOW, 2 * LANES), BF)] * 2,
        ),
        out_shape=[
            jax.ShapeDtypeStruct((rows * items, LANES, width), BF),
            jax.ShapeDtypeStruct((rows * items, width, LANES), F32),
            jax.ShapeDtypeStruct((rows * pairs, items, 2 * LANES), F32),
        ],
        compiler_params=pltpu.CompilerParams(vmem_limit_bytes=VMEM),
        name="cross_forward",
    )(lengths, keys, values, gate, qt)


def cross_backward_kernel(lengths_ref, keys_ref, values_ref, gate_ref, qt_ref, gt_ref, mixt_ref, lse_ref, dk_ref, dv_ref, dq_ref):
    row = pl.program_id(0)
    slots = keys_ref.shape[0]
    items = lengths_ref.shape[1]
    starts, ends = bounds_of(lengths_ref, row)

    def one_item(item):
        at = window_of(starts[item], slots)
        rows = pl.ds(at, WINDOW)
        qt, gt = qt_ref[item], gt_ref[item]
        products = gt.astype(F32) * mixt_ref[item]
        inner = jnp.concatenate([jnp.sum(products[:HEAD], axis=0, keepdims=True), jnp.sum(products[HEAD:], axis=0, keepdims=True)], axis=1)
        score_right = jnp.concatenate([block_rows(qt), gate_rows(item, items, FAR, -lse_ref[0, item : item + 1, :])], axis=0)
        slope_right = jnp.concatenate([block_rows(gt), gate_rows(item, items, 0.0, -inner)], axis=0)
        keys, gate = keys_ref[rows, :], gate_ref[rows, :]
        probs = jnp.exp(mm(jnp.concatenate([keys, gate], axis=1), score_right))
        slopes = mm(jnp.concatenate([values_ref[rows, :], gate], axis=1), slope_right)
        low_scores = (probs * slopes).astype(BF)
        slot = iota((WINDOW, 1), 0) + at
        mine = (slot >= starts[item]) & (slot < ends[item])
        grad_values = mm(probs.astype(BF), block_columns(jnp.transpose(gt))).astype(BF)
        dv_ref[rows, :] = jnp.where(mine, grad_values, dv_ref[rows, :])
        grad_keys = mm(low_scores, block_columns(jnp.transpose(qt))).astype(BF)
        dk_ref[rows, :] = jnp.where(mine, grad_keys, dk_ref[rows, :])
        both = mm_tn(keys, low_scores)
        dq_ref[item] = jnp.transpose(jnp.concatenate([both[:HEAD, :LANES], both[HEAD:, LANES:]], axis=0) * SCALE).astype(BF)

    for item in range(items):
        one_item(item)


def cross_backward(lengths, keys, values, gate, qt, gt, mixt, lse):
    rows, items = lengths.shape
    _, total, columns = keys.shape
    slots, width = total // rows, 2 * columns
    pairs, inside = width // PAIR, columns // PAIR
    by_pair = pl.BlockSpec((None, slots, PAIR), lambda r, p, *_: (p // inside, r, p % inside))
    turned = pl.BlockSpec((items, PAIR, LANES), lambda r, p, *_: (r, p, 0))
    return pl.pallas_call(
        cross_backward_kernel,
        grid_spec=pltpu.PrefetchScalarGridSpec(
            num_scalar_prefetch=1,
            grid=(rows, pairs),
            in_specs=[
                by_pair, by_pair,
                pl.BlockSpec((slots, LANES), lambda r, p, *_: (r, 0)),
                turned, turned, turned,
                pl.BlockSpec((1, items, 2 * LANES), lambda r, p, *_: (r * pairs + p, 0, 0)),
            ],
            out_specs=[by_pair, by_pair, pl.BlockSpec((items, LANES, PAIR), lambda r, p, *_: (r, 0, p))],
        ),
        out_shape=[
            jax.ShapeDtypeStruct((2, total, columns), BF),
            jax.ShapeDtypeStruct((2, total, columns), BF),
            jax.ShapeDtypeStruct((rows * items, LANES, width), BF),
        ],
        compiler_params=pltpu.CompilerParams(vmem_limit_bytes=VMEM),
        name="cross_backward",
    )(lengths, keys, values, gate, qt, gt, mixt, lse)


def memory_weights_kernel(mine_ref, dk_ref, dv_ref, memory_ref, memory_in_ref, out_ref, vec_ref, wk_acc, wv_acc, bv_acc):
    step = pl.program_id(0)
    block, columns = dk_ref.shape

    @pl.when(step == 0)
    def _():
        wk_acc[...] = jnp.zeros_like(wk_acc)
        wv_acc[...] = jnp.zeros_like(wv_acc)
        bv_acc[...] = jnp.zeros_like(bv_acc)

    wk_acc[...] += mm_tn(dk_ref[...], memory_in_ref[...])
    wv_acc[...] += mm_tn(dv_ref[...], memory_ref[...])
    bv_acc[...] += jnp.sum(dv_ref[...].astype(F32).reshape(block // 8, 8, columns), axis=0)

    @pl.when(step == pl.num_programs(0) - 1)
    def _():
        out_ref[...] = jnp.concatenate([jnp.transpose(wk_acc[...]), jnp.transpose(wv_acc[...])], axis=1).astype(BF)
        vec_ref[...] = jnp.concatenate([jnp.sum(bv_acc[...], axis=0, keepdims=True), jnp.zeros((1, columns), F32)], axis=1)


def memory_weights(place, dk, dv, memory, memory_in, columns):
    total, feature = memory.shape
    own = pl.BlockSpec((None, SUMS_BLOCK, columns), lambda t, place: (place[0], t, 0))
    slab = pl.BlockSpec((SUMS_BLOCK, feature), lambda t, *_: (t, 0))
    whole = lambda shape: pl.BlockSpec(shape, lambda t, *_: (0,) * len(shape))
    return pl.pallas_call(
        memory_weights_kernel,
        grid_spec=pltpu.PrefetchScalarGridSpec(
            num_scalar_prefetch=1,
            grid=(total // SUMS_BLOCK,),
            in_specs=[own, own, slab, slab],
            out_specs=[whole((feature, 2 * columns)), whole((1, 2 * columns))],
            scratch_shapes=[pltpu.VMEM((columns, feature), F32), pltpu.VMEM((columns, feature), F32), pltpu.VMEM((8, columns), F32)],
        ),
        out_shape=[jax.ShapeDtypeStruct((feature, 2 * columns), BF), jax.ShapeDtypeStruct((1, 2 * columns), F32)],
        compiler_params=pltpu.CompilerParams(vmem_limit_bytes=VMEM),
        name="memory_weights",
    )(place, dk, dv, memory, memory_in)


def memory_gradient_kernel(dk_low, dk_high, dv_low, dv_high, wk_ref, wv_ref, *rest):
    dk = jnp.concatenate([dk_low[...], dk_high[...]], axis=1)
    dv = jnp.concatenate([dv_low[...], dv_high[...]], axis=1)
    rest[-1][...] = mm_nt(dk, wk_ref[...]) + mm_nt(dv, wv_ref[...])


def memory_gradient(dk, dv, wk, wv, first, blocks, held):
    _, total, columns = dk.shape
    feature = wk.shape[0]
    half = lambda which: pl.BlockSpec((None, BLOCK, columns), lambda t: (which, first + t, 0))
    operands, specs = [dk, dk, dv, dv, wk, wv], [half(0), half(1), half(0), half(1), whole_spec(wk), whole_spec(wv)]
    if held is not None:
        operands, specs = operands + [held], specs + [pl.BlockSpec(memory_space=pl.ANY)]
    return pl.pallas_call(
        memory_gradient_kernel,
        grid=(blocks,),
        in_specs=specs,
        out_specs=pl.BlockSpec((BLOCK, feature), lambda t: (first + t, 0)),
        out_shape=jax.ShapeDtypeStruct((total, feature), F32),
        input_output_aliases={} if held is None else {6: 0},
        compiler_params=pltpu.CompilerParams(vmem_limit_bytes=VMEM),
        name="memory_gradient",
    )(*operands)


def assemble(full_ref, own_ref, part_ref, rest_ref, corner, place_ref, dim):
    mine, bit = place_ref[0], place_ref[1]
    rows, columns = own_ref.shape
    half = rows // 2
    line, lane = corner
    for source, offset in ((part_ref, bit * half), (rest_ref, (1 - bit) * half)):
        if dim == 1:
            at = (pl.ds(pl.multiple_of(offset, half), half), pl.ds(pl.multiple_of((1 - mine) * columns, columns), columns))
        elif dim == 0:
            at = (pl.ds(pl.multiple_of((1 - mine) * rows + offset, half), half), slice(None))
        else:
            at = (1 - mine, pl.ds(pl.multiple_of(offset, half), half), slice(None))
        full_ref[at] = source[line : line + half, lane : lane + columns]
    if dim == 1:
        full_ref[:, pl.ds(pl.multiple_of(mine * columns, columns), columns)] = own_ref[...]
    elif dim == 0:
        full_ref[pl.ds(pl.multiple_of(mine * rows, rows), rows), :] = own_ref[...]
    else:
        full_ref[mine] = own_ref[...]


def bias_of(place_ref, own_ref, other_ref, line, lane, size):
    if size <= own_ref.shape[1] - lane:
        own, other = own_ref[line : line + 1, lane : lane + size], other_ref[line : line + 1, lane : lane + size]
    else:
        lines = -(-size // own_ref.shape[1])
        own, other = (jnp.concatenate([ref[line + one : line + one + 1, :] for one in range(lines)], axis=1)[:, :size] for ref in (own_ref, other_ref))
    first = place_ref[0] == 0
    return jnp.where(first, own, other), jnp.where(first, other, own)


def assemble_token(wq, wk, wv, cwq, wo, wq_own, wk_own, wv_own, cwq_own, wo_own, part_ref, rest_ref, place_ref):
    rows, columns = wq_own.shape
    assemble(wq, wq_own, part_ref, rest_ref, (0, 0), place_ref, 1)
    assemble(wk, wk_own, part_ref, rest_ref, (0, columns), place_ref, 1)
    assemble(wv, wv_own, part_ref, rest_ref, (rows // 2, 0), place_ref, 1)
    assemble(cwq, cwq_own, part_ref, rest_ref, (rows // 2, columns), place_ref, 1)
    assemble(wo, wo_own, part_ref, rest_ref, (rows, 0), place_ref, 0)


def give_halves(place_ref, sums, sent_ref, kept_ref):
    half = sent_ref.shape[0]
    sent_ref[...] = sums[pl.ds(pl.multiple_of((1 - place_ref[1]) * half, half), half), :]
    kept_ref[...] = sums[pl.ds(pl.multiple_of(place_ref[1] * half, half), half), :]


def normalize(value):
    center = value - jnp.mean(value, axis=-1, keepdims=True)
    spread = lax.rsqrt(jnp.mean(center * center, axis=-1, keepdims=True) + 1e-05)
    return center * spread, spread


def normalize_back(grad, normed, spread, gain):
    scaled = grad * gain
    inner = jnp.mean(scaled * normed, axis=-1, keepdims=True)
    return (scaled - jnp.mean(scaled, axis=-1, keepdims=True) - normed * inner) * spread


def total_rows(value):
    return jnp.sum(value, axis=0, keepdims=True)


def cut_items(value):
    blank = jnp.zeros((LANES - SPAN, value.shape[1]), value.dtype)
    return [jnp.concatenate([value[at : at + SPAN], blank], axis=0) for at in range(0, value.shape[0], SPAN)]


def join_items(pieces):
    return jnp.concatenate([one[:SPAN] for one in pieces], axis=0)


def self_probs(keys, qt_block):
    scores = mm(keys, qt_block)
    scores = jnp.where(iota(scores.shape, 0) < SPAN, scores, FAR)
    expo = jnp.exp(scores - jnp.max(scores, axis=0, keepdims=True))
    return expo / jnp.sum(expo, axis=0, keepdims=True)


def own_blocks(both):
    return jnp.concatenate([both[:HEAD, :LANES], both[HEAD:, LANES:]], axis=0)


def token_forward_kernel(
    place_ref, tokens_ref, embed_ref,
    wq_own, wk_own, wv_own, cwq_own, wo_own, part_ref, rest_ref, bias_own, bias_other, so_bias, gain_ref, shift_ref,
    q_ref, k_ref, v_ref, mix_ref, resid_ref, normed_ref, qt_ref,
    wq, wk, wv, wo, cwq,
):
    @pl.when(pl.program_id(0) == 0)
    def _():
        assemble_token(wq, wk, wv, cwq, wo, wq_own, wk_own, wv_own, cwq_own, wo_own, part_ref, rest_ref, place_ref)

    width = wq.shape[1]
    half = width // 2
    bias = lambda line, lane: jnp.concatenate(bias_of(place_ref, bias_own, bias_other, line, lane, half), axis=1)
    tokens = tokens_ref[...]
    items = tokens.shape[0] // SPAN
    query_pos = jnp.concatenate([embed_ref[...]] * items, axis=0)
    tokens_wide = tokens.astype(F32)
    shared_in = (tokens_wide + query_pos).astype(BF)
    q = (mm(shared_in, wq[...]) + bias(0, 0)).astype(BF)
    k = mm(shared_in, wk[...]).astype(BF)
    v = (mm(tokens, wv[...]) + bias(0, half)).astype(BF)
    q_ref[...], k_ref[...], v_ref[...] = q, k, v
    q_items, k_items, v_items = (cut_items(one.astype(F32)) for one in (q, k, v))
    mixes = []
    for item in range(items):
        qt = jnp.transpose(q_items[item] * SCALE).astype(BF)
        keys, values = k_items[item].astype(BF), v_items[item].astype(BF)
        mixed = []
        for at in range(0, width, PAIR):
            probs = self_probs(keys[:, at : at + PAIR], block_rows(qt[at : at + PAIR]))
            mixed.append(own_blocks(mm_tn(values[:, at : at + PAIR], probs.astype(BF))))
        mixes.append(jnp.transpose(jnp.concatenate(mixed, axis=0)))
    mix = join_items(mixes).astype(BF)
    mix_ref[...] = mix
    resid = tokens_wide + (mm(mix, wo[...]) + so_bias[...])
    resid_ref[...] = resid
    normed, _ = normalize(resid)
    normed = normed * gain_ref[...] + shift_ref[...]
    normed_ref[...] = normed
    cross_in = (normed + query_pos).astype(BF)
    cross_q = (mm(cross_in, cwq[...]) + bias(1, 0)).astype(BF).astype(F32) * SCALE
    for item, one in enumerate(cut_items(cross_q)):
        qt_ref[item] = jnp.transpose(one).astype(BF)


def token_forward(place, tokens, embed, weights, part, rest, bias_own, bias_other, so_bias, gain, shift, rows):
    token_count, feature = tokens.shape
    width = 2 * weights[0].shape[1]
    size = token_count // rows
    items = size // SPAN
    slab = lambda columns: pl.BlockSpec((size, columns), lambda r, *_: (r, 0))
    flat = [*weights, part, rest]
    fixed = [bias_own, bias_other, so_bias, gain, shift]
    return pl.pallas_call(
        token_forward_kernel,
        grid_spec=pltpu.PrefetchScalarGridSpec(
            num_scalar_prefetch=1,
            grid=(rows,),
            in_specs=[slab(feature), whole_spec(embed)] + [whole_spec(one) for one in flat + fixed],
            out_specs=[slab(width)] * 4 + [slab(feature)] * 2 + [pl.BlockSpec((items, width, LANES), lambda r, *_: (r, 0, 0))],
            scratch_shapes=[pltpu.VMEM((feature, width), BF)] * 3 + [pltpu.VMEM((width, feature), BF), pltpu.VMEM((feature, width), BF)],
        ),
        out_shape=[jax.ShapeDtypeStruct((token_count, width), BF)] * 4
        + [jax.ShapeDtypeStruct((token_count, feature), F32)] * 2
        + [jax.ShapeDtypeStruct((rows * items, width, LANES), BF)],
        compiler_params=pltpu.CompilerParams(vmem_limit_bytes=VMEM),
        name="token_forward",
    )(place, tokens, embed, *flat, *fixed)


def gelu_both(pre):
    inner = math.sqrt(2.0 / math.pi)
    square = pre * pre
    bend = jnp.tanh(pre * (inner + (inner * 0.044715) * square))
    lift = 0.5 + 0.5 * bend
    slope = lift + (0.5 * pre) * (1.0 - bend * bend) * (inner + (3.0 * inner * 0.044715) * square)
    return pre * lift, slope


def feed_kernel(
    place_ref, mix_in_ref, normed_one_ref, cotangent_ref,
    wo_own, w1_own, w2_own, token_part, token_rest, part_ref, rest_ref, bias_own, bias_other,
    co_bias, gain2_ref, shift2_ref, f_bias, gain3_ref, shift3_ref,
    out_ref, grad_two_ref, gt_ref, sums_ref,
    wo, w1, w2, hidden, slope, low_pre, mix_scr, w1_acc, w2_acc, wo_acc, b1_acc, vec_acc, semaphores,
):
    row = pl.program_id(0)
    mine = place_ref[0]
    columns = wo_acc.shape[0]
    width = wo.shape[0]
    size = out_ref.shape[0]
    hidden_half = w1.shape[1]

    half, bit = hidden_half // 2, place_ref[1]

    def fetch(weight, own_ref, line, at):
        pieces = [(own_ref, weight.at[mine])]
        for source, offset in ((part_ref, bit * half), (rest_ref, (1 - bit) * half)):
            pieces.append((source.at[line : line + half, :], weight.at[1 - mine, pl.ds(pl.multiple_of(offset, half), half), :]))
        return [pltpu.make_async_copy(*one, semaphores.at[at + index]) for index, one in enumerate(pieces)]

    fetch_one, fetch_two = fetch(w1, w1_own, 0, 0), fetch(w2, w2_own, half, 3)

    @pl.when(row == 0)
    def _():
        for one in (*fetch_one, *fetch_two):
            one.start()
        assemble(wo, wo_own, token_part, token_rest, (wo.shape[1] + columns // 2, 0), place_ref, 0)
        for acc in (w1_acc, w2_acc, wo_acc, b1_acc, vec_acc):
            acc[...] = jnp.zeros_like(acc)

    mix = join_items([mix_in_ref[item].astype(F32) for item in range(mix_in_ref.shape[0])]).astype(BF)
    mix_scr[...] = mix
    normed2, spread2 = normalize(normed_one_ref[...] + (mm(mix, wo[...]) + co_bias[...]))
    normed_two = normed2 * gain2_ref[...] + shift2_ref[...]
    feed_in = normed_two.astype(BF)
    b1 = bias_of(place_ref, bias_own, bias_other, 2, 0, hidden_half)
    total = normed_two + f_bias[...]

    @pl.when(row == 0)
    def _():
        for one in fetch_one:
            one.wait()

    for part in range(2):
        one, rise = gelu_both(mm_nt(feed_in, w1[part]) + b1[part])
        hidden[part] = one.astype(BF)
        slope[part] = rise

    @pl.when(row == 0)
    def _():
        for one in fetch_two:
            one.wait()

    for part in range(2):
        total = total + mm(hidden[part], w2[part])
    normed3, spread3 = normalize(total)
    out_ref[...] = (normed3 * gain3_ref[...] + shift3_ref[...]).astype(BF)
    cotangent = cotangent_ref[...].astype(F32)
    grad_three = normalize_back(cotangent, normed3, spread3, gain3_ref[...])
    low_three = grad_three.astype(BF)
    back = grad_three
    for part in range(2):
        low = (mm_nt(low_three, w2[part]) * slope[part]).astype(BF)
        low_pre[part] = low
        back = back + mm(low, w1[part])
    grad_two = normalize_back(back, normed2, spread2, gain2_ref[...])
    grad_two_ref[...] = grad_two
    low_two = grad_two.astype(BF)
    own_pre = low_pre[mine]
    w2_acc[...] += mm_tn(hidden[mine], low_three)
    w1_acc[...] += mm_tn(own_pre, feed_in)
    b1_acc[...] += total_rows(own_pre.astype(F32))
    if columns == width:
        own = slice(None)
    else:
        own = pl.ds(pl.multiple_of(mine * columns, columns), columns)
    wo_acc[...] += mm_tn(mix_scr[:, own], low_two)
    vec_acc[...] += jnp.concatenate(
        [
            total_rows(cotangent * normed3), total_rows(cotangent), total_rows(low_three.astype(F32)),
            total_rows(back * normed2), total_rows(back), total_rows(low_two.astype(F32)),
            jnp.zeros((2, vec_acc.shape[1]), F32),
        ],
        axis=0,
    )
    grad_mix = mm_nt(low_two, wo[...]).astype(BF).astype(F32)
    for item, one in enumerate(cut_items(grad_mix)):
        gt_ref[item] = jnp.transpose(one).astype(BF)

    @pl.when(row == pl.num_programs(0) - 1)
    def _():
        sums_ref[:hidden_half, :] = w1_acc[...].astype(BF)
        sums_ref[hidden_half : 2 * hidden_half, :] = w2_acc[...].astype(BF)
        sums_ref[2 * hidden_half : 2 * hidden_half + columns, :] = wo_acc[...].astype(BF)
        feature = vec_acc.shape[1]
        lines = [b1_acc[:, at : at + feature] for at in range(0, hidden_half, feature)]
        lines[-1] = jnp.concatenate([lines[-1], jnp.zeros((1, feature - lines[-1].shape[1]), F32)], axis=1)
        lines.append(jnp.zeros((FEED_LINES - 8 - len(lines), feature), F32))
        sums_ref[2 * hidden_half + columns :, :] = jnp.concatenate([vec_acc[...], *lines], axis=0).astype(BF)


def feed(place, mix, normed_one, cotangent, weights, parts, bias_own, bias_other, vectors, rows, columns):
    token_count, feature = normed_one.shape
    width = mix.shape[2]
    size = token_count // rows
    items = size // SPAN
    hidden_half = weights[1].shape[0]
    lines = 2 * hidden_half + columns + FEED_LINES
    slab = lambda columns: pl.BlockSpec((size, columns), lambda r, *_: (r, 0))
    whole = lambda shape: pl.BlockSpec(shape, lambda r, *_: (0,) * len(shape))
    flat = [*weights, *parts]
    fixed = [bias_own, bias_other, *vectors]
    far = pl.BlockSpec(memory_space=pl.ANY)
    return pl.pallas_call(
        feed_kernel,
        grid_spec=pltpu.PrefetchScalarGridSpec(
            num_scalar_prefetch=1,
            grid=(rows,),
            in_specs=[pl.BlockSpec((items, LANES, width), lambda r, *_: (r, 0, 0)), slab(feature), slab(feature)]
            + [far if index in (1, 2, 5, 6) else whole_spec(one) for index, one in enumerate(flat + fixed)],
            out_specs=[
                slab(feature), slab(feature), pl.BlockSpec((items, width, LANES), lambda r, *_: (r, 0, 0)),
                whole((lines, feature)),
            ],
            scratch_shapes=[
                pltpu.VMEM((width, feature), BF),
                pltpu.VMEM((2, hidden_half, feature), BF),
                pltpu.VMEM((2, hidden_half, feature), BF),
                pltpu.VMEM((2, size, hidden_half), BF),
                pltpu.VMEM((2, size, hidden_half), F32),
                pltpu.VMEM((2, size, hidden_half), BF),
                pltpu.VMEM((size, width), BF),
                pltpu.VMEM((hidden_half, feature), F32),
                pltpu.VMEM((hidden_half, feature), F32),
                pltpu.VMEM((columns, feature), F32),
                pltpu.VMEM((1, hidden_half), F32),
                pltpu.VMEM((8, feature), F32),
                pltpu.SemaphoreType.DMA((6,)),
            ],
        ),
        out_shape=[
            jax.ShapeDtypeStruct((token_count, feature), BF),
            jax.ShapeDtypeStruct((token_count, feature), F32),
            jax.ShapeDtypeStruct((rows * items, width, LANES), BF),
            jax.ShapeDtypeStruct((lines, feature), BF),
        ],
        compiler_params=pltpu.CompilerParams(vmem_limit_bytes=VMEM),
        name="feed",
    )(place, mix, normed_one, cotangent, *flat, *fixed)


def token_backward_kernel(
    place_ref, dq_in_ref, grad_two_ref, resid_ref, normed_ref, tokens_ref, embed_ref, q_ref, k_ref, v_ref, mix_ref,
    memory_sums_ref, memory_vec_ref,
    wq_own, wk_own, wv_own, cwq_own, wo_own, part_ref, rest_ref, gain_ref,
    grad_tokens_ref, sent_ref, kept_ref,
    wq, wk, wv, wo, cwq, cross_dq, low_q, low_k, low_v, cwq_acc, wq_acc, wk_acc, wv_acc, wo_acc, embed_acc, vec_acc, sums,
):
    row = pl.program_id(0)
    mine = place_ref[0]
    width = wq.shape[1]
    columns = wo_acc.shape[0]

    @pl.when(row == 0)
    def _():
        assemble_token(wq, wk, wv, cwq, wo, wq_own, wk_own, wv_own, cwq_own, wo_own, part_ref, rest_ref, place_ref)
        for acc in (cwq_acc, wq_acc, wk_acc, wv_acc, wo_acc, embed_acc, vec_acc):
            acc[...] = jnp.zeros_like(acc)

    if columns == width:
        own = slice(None)
    else:
        own = pl.ds(pl.multiple_of(mine * columns, columns), columns)
    tokens = tokens_ref[...]
    items = tokens.shape[0] // SPAN
    query_pos = jnp.concatenate([embed_ref[...]] * items, axis=0)
    shared_in = (tokens.astype(F32) + query_pos).astype(BF)
    cross_in = (normed_ref[...] + query_pos).astype(BF)
    cross_dq[...] = join_items([dq_in_ref[item].astype(F32) for item in range(items)]).astype(BF)
    cwq_acc[...] += mm_tn(cross_in, cross_dq[:, own])
    grad_cross_in = mm_nt(cross_dq[...], cwq[...])
    back = grad_two_ref[...] + grad_cross_in
    normed, spread = normalize(resid_ref[...])
    grad_one = normalize_back(back, normed, spread, gain_ref[...])
    low_one = grad_one.astype(BF)
    wo_acc[...] += mm_tn(mix_ref[:, own], low_one)
    g_items = cut_items(mm_nt(low_one, wo[...]).astype(BF).astype(F32))
    q_items = cut_items(q_ref[...].astype(F32) * SCALE)
    k_items, v_items = cut_items(k_ref[...].astype(F32)), cut_items(v_ref[...].astype(F32))
    all_dq, all_dk, all_dv = [], [], []
    for item in range(items):
        qt, gt = jnp.transpose(q_items[item]).astype(BF), jnp.transpose(g_items[item]).astype(BF)
        qn, gn, keys, values = (one[item].astype(BF) for one in (q_items, g_items, k_items, v_items))
        one_dq, one_dk, one_dv = [], [], []
        for at in range(0, width, PAIR):
            here = slice(at, at + PAIR)
            probs = self_probs(keys[:, here], block_rows(qt[here]))
            slopes = mm(values[:, here], block_rows(gt[here]))
            inner = jnp.sum(probs * slopes, axis=0, keepdims=True)
            low = (probs * (slopes - inner)).astype(BF)
            one_dv.append(mm(probs.astype(BF), block_columns(gn[:, here])))
            one_dk.append(mm(low, block_columns(qn[:, here])))
            one_dq.append(own_blocks(mm_tn(keys[:, here], low)))
        all_dq.append(jnp.transpose(jnp.concatenate(one_dq, axis=0) * SCALE))
        all_dk.append(jnp.concatenate(one_dk, axis=1))
        all_dv.append(jnp.concatenate(one_dv, axis=1))
    low_q[...] = join_items(all_dq).astype(BF)
    low_k[...] = join_items(all_dk).astype(BF)
    low_v[...] = join_items(all_dv).astype(BF)
    wq_acc[...] += mm_tn(shared_in, low_q[:, own])
    wk_acc[...] += mm_tn(shared_in, low_k[:, own])
    wv_acc[...] += mm_tn(tokens, low_v[:, own])
    grad_shared = mm_nt(low_q[...], wq[...]) + mm_nt(low_k[...], wk[...])
    grad_tokens_ref[...] = grad_one + grad_shared + mm_nt(low_v[...], wv[...])
    position = grad_shared + grad_cross_in
    embed_acc[...] += sum(position[at : at + SPAN] for at in range(0, position.shape[0], SPAN))
    vec_acc[...] += jnp.concatenate(
        [
            total_rows(back * normed), total_rows(back), total_rows(low_one.astype(F32)),
            total_rows(cross_dq[...].astype(F32)), total_rows(low_q[...].astype(F32)), total_rows(low_v[...].astype(F32)),
            jnp.zeros((2, width), F32),
        ],
        axis=0,
    )

    @pl.when(row == pl.num_programs(0) - 1)
    def _():
        feature = wq_acc.shape[0]
        for at, (one, two) in enumerate(((wq_acc, wk_acc), (wv_acc, cwq_acc))):
            sums[at * feature : (at + 1) * feature, :columns] = one[...].astype(BF)
            sums[at * feature : (at + 1) * feature, columns:] = two[...].astype(BF)
        sums[2 * feature : 3 * feature, :] = memory_sums_ref[...]
        sums[3 * feature : 3 * feature + columns, :] = wo_acc[...].astype(BF)
        at = 3 * feature + columns
        sums[at : at + LANES, :] = jnp.concatenate([embed_acc[...], jnp.zeros((LANES - SPAN, width), F32)], axis=0).astype(BF)
        vectors = jnp.concatenate([vec_acc[...], memory_vec_ref[...], jnp.zeros((7, width), F32)], axis=0)
        sums[at + LANES : at + LANES + 16, :] = vectors.astype(BF)
        sums[at + LANES + 16 :, :] = jnp.zeros((sums.shape[0] - at - LANES - 16, width), BF)
        give_halves(place_ref, sums, sent_ref, kept_ref)


def token_backward(place, dq, grad_two, resid, normed, tokens, embed, q, k, v, mix, memory_sums, memory_vec, weights, part, rest, gain, rows, columns, lines):
    token_count, feature = tokens.shape
    width = q.shape[1]
    size = token_count // rows
    items = size // SPAN
    slab = lambda columns: pl.BlockSpec((size, columns), lambda r, *_: (r, 0))
    whole = lambda shape: pl.BlockSpec(shape, lambda r, *_: (0,) * len(shape))
    flat = [memory_sums, memory_vec, *weights, part, rest]
    grads = [(feature, columns)] * 4 + [(columns, feature)]
    return pl.pallas_call(
        token_backward_kernel,
        grid_spec=pltpu.PrefetchScalarGridSpec(
            num_scalar_prefetch=1,
            grid=(rows,),
            in_specs=[pl.BlockSpec((items, LANES, width), lambda r, *_: (r, 0, 0))]
            + [slab(feature)] * 4 + [whole_spec(embed)] + [slab(width)] * 4
            + [whole_spec(one) for one in flat] + [whole_spec(gain)],
            out_specs=[slab(feature), whole((lines // 2, feature)), whole((lines // 2, feature))],
            scratch_shapes=[pltpu.VMEM((feature, width), BF)] * 3 + [pltpu.VMEM((width, feature), BF), pltpu.VMEM((feature, width), BF)]
            + [pltpu.VMEM((size, width), BF)] * 4
            + [pltpu.VMEM(one, F32) for one in grads] + [pltpu.VMEM((SPAN, feature), F32), pltpu.VMEM((8, feature), F32), pltpu.VMEM((lines, feature), BF)],
        ),
        out_shape=[jax.ShapeDtypeStruct((token_count, feature), F32)] + [jax.ShapeDtypeStruct((lines // 2, feature), BF)] * 2,
        compiler_params=pltpu.CompilerParams(vmem_limit_bytes=VMEM),
        name="token_backward",
    )(place, dq, grad_two, resid, normed, tokens, embed, q, k, v, mix, *flat, gain)


def pack_columns_kernel(place_ref, wk_ref, wv_ref, bias_ref, out_ref):
    half, columns = wk_ref.shape
    out_ref[:half, :columns] = wk_ref[...]
    out_ref[:half, columns:] = wv_ref[...]
    lines = [one.astype(F32) for one in split3(bias_ref[...])]
    lines = jnp.concatenate(lines + [jnp.zeros((BIAS_LINES - 3, columns), F32)], axis=0)
    out_ref[half:, :] = jnp.concatenate([lines, jnp.zeros_like(lines)], axis=1).astype(BF)


def pack_token_kernel(place_ref, wq_ref, wk_ref, wv_ref, cwq_ref, wo_ref, cwo_ref, out_ref):
    half, columns = wq_ref.shape
    out_ref[:half, :columns] = wq_ref[...]
    out_ref[:half, columns:] = wk_ref[...]
    out_ref[half : 2 * half, :columns] = wv_ref[...]
    out_ref[half : 2 * half, columns:] = cwq_ref[...]
    lines = wo_ref.shape[0]
    out_ref[2 * half : 2 * half + lines, :] = wo_ref[...]
    out_ref[2 * half + lines :, :] = cwo_ref[...]


def pack_lines_kernel(place_ref, w1_ref, w2_ref, out_ref):
    lines = w1_ref.shape[0]
    out_ref[:lines, :] = w1_ref[...]
    out_ref[lines:, :] = w2_ref[...]


def pack_half(kernel, bit, arrays, lines, columns):
    return pl.pallas_call(
        kernel,
        grid_spec=pltpu.PrefetchScalarGridSpec(
            num_scalar_prefetch=1, grid=(1,),
            in_specs=[
                whole_spec(one) if one.shape[0] == 1 else pl.BlockSpec((one.shape[0] // 2, one.shape[1]), lambda _, place: (place[0], 0))
                for one in arrays
            ],
            out_specs=pl.BlockSpec((lines, columns), lambda *_: (0, 0)),
        ),
        out_shape=jax.ShapeDtypeStruct((lines, columns), BF),
        compiler_params=pltpu.CompilerParams(vmem_limit_bytes=VMEM),
        name=kernel.__name__.replace("_kernel", ""),
    )(bit[None], *arrays)


def pack_bias_kernel(sbq_ref, sbv_ref, cbq_ref, cbv_ref, b1_ref, out_ref):
    columns = out_ref.shape[1]
    out_ref[...] = jnp.zeros_like(out_ref)
    size = sbq_ref.shape[1]
    out_ref[0:1, :size], out_ref[0:1, size : 2 * size] = sbq_ref[...], sbv_ref[...]
    out_ref[1:2, :size], out_ref[1:2, size : 2 * size] = cbq_ref[...], cbv_ref[...]
    for line, at in enumerate(range(0, b1_ref.shape[1], columns)):
        part = b1_ref[:, at : min(at + columns, b1_ref.shape[1])]
        out_ref[2 + line : 3 + line, : part.shape[1]] = part


def pack_bias(biases, columns):
    lines = -(-(2 + -(-biases[-1].shape[1] // columns)) // 8) * 8
    return pl.pallas_call(pack_bias_kernel, out_shape=jax.ShapeDtypeStruct((lines, columns), F32), name="pack_bias")(*biases)


def feed_unpack_kernel(hidden_half, columns, sums_ref, w1_ref, w2_ref, wo_ref, b1_ref, *vec_refs):
    w1_ref[...] = sums_ref[:hidden_half, :].astype(F32)
    w2_ref[...] = sums_ref[hidden_half : 2 * hidden_half, :].astype(F32)
    wo_ref[...] = sums_ref[2 * hidden_half : 2 * hidden_half + columns, :].astype(F32)
    vectors = sums_ref[2 * hidden_half + columns :, :].astype(F32)
    for line, one in enumerate(vec_refs):
        one[...] = vectors[line : line + 1]
    lines = -(-hidden_half // vectors.shape[1])
    b1_ref[...] = jnp.concatenate([vectors[8 + one : 9 + one] for one in range(lines)], axis=1)[:, :hidden_half]


def feed_unpack(sums, hidden_half, columns):
    feature = sums.shape[1]
    shapes = [(hidden_half, feature), (hidden_half, feature), (columns, feature), (1, hidden_half)] + [(1, feature)] * 6
    return pl.pallas_call(
        functools.partial(feed_unpack_kernel, hidden_half, columns),
        out_shape=[jax.ShapeDtypeStruct(one, F32) for one in shapes],
        compiler_params=pltpu.CompilerParams(vmem_limit_bytes=VMEM),
        name="feed_unpack",
    )(sums)


def token_unpack_kernel(
    place_ref, kept_ref, other_ref, wq_ref, wk_ref, wv_ref, cwq_ref, cwk_ref, cwv_ref, wo_ref, embed_ref,
    gain_ref, shift_ref, so_ref, cq_ref, sq_ref, sv_ref, cv_ref, sums, vectors,
):
    half = kept_ref.shape[0]
    sums[pl.ds(pl.multiple_of(place_ref[1] * half, half), half), :] = kept_ref[...]
    sums[pl.ds(pl.multiple_of((1 - place_ref[1]) * half, half), half), :] = other_ref[...]
    feature, columns = wq_ref.shape
    for at, (one, two) in enumerate(((wq_ref, wk_ref), (wv_ref, cwq_ref), (cwk_ref, cwv_ref))):
        one[...] = sums[at * feature : (at + 1) * feature, :columns].astype(F32)
        two[...] = sums[at * feature : (at + 1) * feature, columns:].astype(F32)
    wo_ref[...] = sums[3 * feature : 3 * feature + columns, :].astype(F32)
    at = 3 * feature + columns
    embed_ref[...] = sums[at : at + LANES, :].astype(F32)[:SPAN]
    vectors[...] = sums[at + LANES : at + LANES + 16, :].astype(F32)
    gain_ref[...], shift_ref[...], so_ref[...] = vectors[0:1, :], vectors[1:2, :], vectors[2:3, :]
    own = pl.ds(pl.multiple_of(place_ref[0] * columns, columns), columns)
    cq_ref[...], sq_ref[...], sv_ref[...] = vectors[3:4, own], vectors[4:5, own], vectors[5:6, own]
    cv_ref[...] = vectors[8:9, :columns]


def token_unpack(place, kept, other, feature, columns):
    half, width = kept.shape
    shapes = [(feature, columns)] * 6 + [(columns, feature), (SPAN, feature)] + [(1, feature)] * 3 + [(1, columns)] * 4
    whole = lambda shape: pl.BlockSpec(shape, lambda *_: (0, 0))
    return pl.pallas_call(
        token_unpack_kernel,
        grid_spec=pltpu.PrefetchScalarGridSpec(
            num_scalar_prefetch=1, grid=(1,),
            in_specs=[whole((half, width))] * 2,
            out_specs=[whole(one) for one in shapes],
            scratch_shapes=[pltpu.VMEM((2 * half, width), BF), pltpu.VMEM((16, width), F32)],
        ),
        out_shape=[jax.ShapeDtypeStruct(one, F32) for one in shapes],
        compiler_params=pltpu.CompilerParams(vmem_limit_bytes=VMEM),
        name="token_unpack",
    )(place, kept, other)


def after(value, *others):
    return lax.optimization_barrier((value, *others))[0]


class SumOverDp:
    def __init__(self, at, count):
        self.at, self.count = at, count
        hops = [1 << one for one in range(1, count.bit_length() - 1)]
        self.hops = list(zip(hops, hops[1:] + hops[:1]))

    def swap(self, array, by):
        return lax.ppermute(array, "dp", [(one, one ^ by) for one in range(self.count)])

    def bit(self, by):
        return (self.at // by) % 2

    def give(self, array, by):
        half = array.shape[0] // 2
        bit = self.bit(by)
        return lax.dynamic_slice_in_dim(array, (1 - bit) * half, half), lax.dynamic_slice_in_dim(array, bit * half, half)

    def add(self, kept, got):
        return (kept.astype(F32) + got.astype(F32)).astype(BF)

    def join(self, array, got, by):
        first = self.bit(by) == 0
        return jnp.concatenate([jnp.where(first, array, got), jnp.where(first, got, array)])

    def exchange(self, sent, bys, work):
        got = [self.swap(one, by) for one, by in zip(sent, bys)]
        done = work(sent)
        return got if done is None else list(lax.optimization_barrier((*got, done)))[: len(got)]

    def start(self, sent, kept, work):
        held = self.add(kept, self.swap(sent, 1))
        middle = held.shape[0] // 2
        two = [held[:middle], held[middle:]]
        for bys in self.hops:
            given = [self.give(one, by) for one, by in zip(two, bys)]
            got = self.exchange([one for one, _ in given], bys, work)
            two = [self.add(one, other) for (_, one), other in zip(given, got)]
        for bys in self.hops[:0:-1]:
            got = self.exchange(two, bys, work)
            two = [self.join(one, other, by) for one, other, by in zip(two, got, bys)]
        return tuple(two)

    def finish(self, two, work):
        bys = self.hops[0]
        got = self.exchange(two, bys, work)
        mine = jnp.concatenate([self.join(one, other, by) for one, other, by in zip(two, got, bys)])
        return mine, self.swap(mine, 1)


def solution(mesh):
    tensor, count = mesh.shape["tensor"], mesh.shape["dp"]

    def body(
        tokens, memory, mem_lengths, key_pad, query_embed,
        self_wq, self_bq, self_wk, self_wv, self_bv, self_wo, self_bo, norm1_gain, norm1_bias,
        cross_wq, cross_bq, cross_wk, cross_wv, cross_bv, cross_wo, cross_bo, norm2_gain, norm2_bias,
        ffn_w1, ffn_b1, ffn_w2, ffn_b2, norm3_gain, norm3_bias, cotangent,
    ):
        rank, at = lax.axis_index("tensor"), lax.axis_index("dp")
        side = (rank * 2 // tensor).astype(jnp.int32)
        bit = (at % 2).astype(jnp.int32)
        place = jnp.stack([side, bit])
        own_columns, own_hidden = self_wq.shape[1], ffn_w1.shape[1]
        feature = tokens.shape[1]
        columns, hidden_half = own_columns * tensor // 2, own_hidden * tensor // 2
        rows = mem_lengths.shape[0]
        direct = tensor == 2 and count > 1
        as_row = lambda one: one.reshape(1, -1)

        def two_halves(part, dim):
            if direct:
                return part, part
            full = lax.all_gather(part, "tensor", axis=dim, tiled=True)
            size = full.shape[dim] // 2
            cut = lambda which: lax.dynamic_slice_in_dim(full, which * size, size, axis=dim)
            return cut(side), cut(1 - side)

        def crossing(kernel, others, lines, sent, then):
            crossed = lax.ppermute(sent, "tensor", [(0, 1), (1, 0)]) if direct else sent
            return passing_on(kernel, others, lines, crossed, then)

        def passing_on(kernel, others, lines, crossed, then):
            if not direct:
                return crossed, pack_half(kernel, 1 - bit, others, lines, feature)
            return crossed, lax.ppermute(after(crossed, then), "dp", [(one, one ^ 1) for one in range(count)])

        cwk, cwv = two_halves(cross_wk, 1), two_halves(cross_wv, 1)
        swq, swk, swv, cwq = (two_halves(one, 1) for one in (self_wq, self_wk, self_wv, cross_wq))
        swo, cwo = two_halves(self_wo, 0), two_halves(cross_wo, 0)
        w1, w2 = two_halves(jnp.transpose(ffn_w1), 0), two_halves(ffn_w2, 0)
        biases = [two_halves(one, 0) for one in (self_bq, self_bv, cross_bq, cross_bv, ffn_b1)]
        memory_others = [cwk[1], cwv[1], as_row(biases[3][1])]
        memory_sent = pack_half(pack_columns_kernel, bit, memory_others, feature // 2 + BIAS_LINES, feature)
        bias_own = pack_bias([after(as_row(biases[0][0]), memory_sent)] + [as_row(own) for own, _ in biases[1:]], feature)
        if direct:
            bias_other = lax.ppermute(bias_own, "tensor", [(0, 1), (1, 0)])
        else:
            bias_other = pack_bias([as_row(other) for _, other in biases], feature)
        token_sent = pack_half(
            pack_token_kernel, bit, [after(swq[1], bias_own)] + [one[1] for one in (swk, swv, cwq, swo, cwo)], feature + columns, feature
        )
        feed_sent = pack_half(pack_lines_kernel, bit, [after(w1[1], token_sent), w2[1]], hidden_half, feature)
        memory_part, memory_rest = crossing(pack_columns_kernel, memory_others, feature // 2 + BIAS_LINES, memory_sent, feed_sent)
        token_sent = after(token_sent, memory_part, bias_other)
        token_crossed = lax.ppermute(token_sent, "tensor", [(0, 1), (1, 0)]) if direct else token_sent
        operands = cwk[0], cwv[0], memory_part, memory_rest, as_row(biases[3][0])
        blocks = memory.shape[0] // BLOCK
        early = blocks * 5 // 8
        outputs = keys_values(mem_lengths, place, memory, key_pad, *operands, 0, early, None)
        feed_sent = after(feed_sent, outputs[1], token_crossed)
        token_part, token_rest = passing_on(
            pack_token_kernel, [one[1] for one in (swq, swk, swv, cwq, swo, cwo)], feature + columns, token_crossed, outputs[1]
        )
        outputs = keys_values(mem_lengths, place, after(memory, feed_sent, token_part), key_pad, *operands, early, blocks - early, outputs)
        memory_in, gate, cross_keys, cross_values, cwk_full, cwv_full = outputs
        token_weights = [one[0] for one in (swq, swk, swv, cwq, swo)]
        q, k, v, self_mix, resid_one, normed_one, qt = token_forward(
            place, tokens, query_embed, token_weights, token_part, token_rest, bias_own, bias_other,
            as_row(self_bo), as_row(norm1_gain), as_row(norm1_bias), 1,
        )
        mix, mixt, lse = cross_forward(mem_lengths, cross_keys, cross_values, gate, qt)
        feed_part, feed_rest = crossing(pack_lines_kernel, [w1[1], w2[1]], hidden_half, feed_sent, lse)
        layer_out, grad_two, gt, feed_sums = feed(
            place, mix, normed_one, cotangent, [cwo[0], w1[0], w2[0]], [token_part, token_rest, feed_part, feed_rest],
            bias_own, bias_other,
            [as_row(one) for one in (cross_bo, norm2_gain, norm2_bias, ffn_b2, norm3_gain, norm3_bias)], rows, columns,
        )
        multiple = 32 * count
        lines = -(-(3 * feature + columns + LANES + 16) // multiple) * multiple

        def backward():
            dk, dv, dq = cross_backward(mem_lengths, cross_keys, cross_values, gate, qt, gt, mixt, lse)
            memory_sums, memory_vec = memory_weights(place, dk, dv, memory, memory_in, columns)
            grad_tokens, sent, kept = token_backward(
                place, dq, grad_two, resid_one, normed_one, tokens, query_embed, q, k, v, self_mix, memory_sums, memory_vec,
                token_weights, token_part, token_rest, as_row(norm1_gain), 1, columns, lines,
            )
            blocks, given = memory.shape[0] // BLOCK, []

            def piece(sent, share=None):
                step, first = len(given), sum(SHARES[: len(given)])
                share = min(SHARES[step] if share is None and step < len(SHARES) else blocks, blocks - first)
                if share <= 0:
                    return None
                held = given[-1] if given else None
                given.append(memory_gradient(after(dk, *sent), dv, cwk_full, cwv_full, first, share, held))
                return given[-1]

            state = token_sum.start(sent, kept, piece) if summed else (sent, kept)
            piece([], blocks)
            return grad_tokens, given[-1], *state

        summed = count > 2
        token_sum = SumOverDp(at, count)
        feed_total = lax.psum(feed_sums, "dp")
        shapes = jax.eval_shape(backward)
        grad_tokens, grad_memory, *state = lax.cond(
            at < count * rows, backward, lambda: tuple(jnp.zeros(one.shape, one.dtype) for one in shapes)
        )
        feed_grads = []

        def unpack_feed(sent):
            feed_grads.extend(feed_unpack(after(feed_total, *sent), hidden_half, columns))
            return feed_grads[0]

        if summed:
            kept, other = token_sum.finish(state, unpack_feed)
        else:
            other, kept = state
            unpack_feed([])
        g_sq, g_sk, g_sv, g_cq, g_ck, g_cv, g_so, g_embed, g_n1g, g_n1b, g_sbo, g_cbq, g_sbq, g_sbv, g_cbv = token_unpack(
            place, kept, other, feature, columns
        )
        g_w1t, g_w2, g_co, g_b1, g_n3g, g_n3b, g_b2, g_n2g, g_n2b, g_cbo = feed_grads

        def share(array, dim, size):
            if array.shape[dim] == size:
                return array
            return lax.dynamic_slice_in_dim(array, rank % (tensor // 2) * size, size, axis=dim)

        lanes = lambda array: share(array, 1, own_columns)
        bias = lambda array: share(array, 1, own_columns).reshape(-1)
        vector = lambda array: array.reshape(-1)
        return (
            layer_out, grad_tokens, grad_memory, g_embed,
            lanes(g_sq), bias(g_sbq), lanes(g_sk), lanes(g_sv), bias(g_sbv), share(g_so, 0, own_columns),
            vector(g_sbo), vector(g_n1g), vector(g_n1b),
            lanes(g_cq), bias(g_cbq), lanes(g_ck), lanes(g_cv), bias(g_cbv), share(g_co, 0, own_columns),
            vector(g_cbo), vector(g_n2g), vector(g_n2b),
            jnp.transpose(share(g_w1t, 0, own_hidden)), share(g_b1, 1, own_hidden).reshape(-1), share(g_w2, 0, own_hidden),
            vector(g_b2), vector(g_n3g), vector(g_n3b),
        )

    rep, by_row, by_col, by_first = P(), P("dp", None), P(None, "tensor"), P("tensor", None)
    one_dim = P("tensor")
    return jax.shard_map(
        body,
        mesh=mesh,
        in_specs=(
            by_row, by_row, by_row, by_row, rep,
            by_col, one_dim, by_col, by_col, one_dim, by_first, rep, rep, rep,
            by_col, one_dim, by_col, by_col, one_dim, by_first, rep, rep, rep,
            by_col, one_dim, by_first, rep, rep, rep, by_row,
        ),
        out_specs=(
            by_row, by_row, by_row, rep,
            by_col, one_dim, by_col, by_col, one_dim, by_first, rep, rep, rep,
            by_col, one_dim, by_col, by_col, one_dim, by_first, rep, rep, rep,
            by_col, one_dim, by_first, rep, rep, rep,
        ),
        check_vma=False,
    )
```

```python
import functools
import math

import jax
import jax.numpy as jnp
import numpy as np
from jax import lax
from jax.experimental import pallas as pl
from jax.experimental.pallas import tpu as pltpu
from jax.sharding import PartitionSpec as P

HEAD = 64
SPAN = 100
MEM_MOST = 1200
LANES = 128
PAIR = 2 * HEAD
TILE = 256
BLOCK = 1024
SUMS_BLOCK = 2048
SHARES = (3, 2, 1, 1, 1)
WINDOW = -(-(MEM_MOST + 15) // 32) * 32
FAR = -1.0e9
CHUNKS = 4
LUMP = 256
BIAS_LINES = 16
FEED_LINES = 16
SCALE = 1.0 / math.sqrt(HEAD)
VMEM = 60 << 20
BF = jnp.bfloat16
F32 = jnp.float32


def mm(left, right):
    return jnp.dot(left, right, preferred_element_type=F32)


def mm_tn(left, right):
    return lax.dot_general(left, right, (((0,), (0,)), ((), ())), preferred_element_type=F32)


def mm_nt(left, right):
    return lax.dot_general(left, right, (((1,), (1,)), ((), ())), preferred_element_type=F32)


def split3(value):
    top = value.astype(BF)
    rest = value - top.astype(F32)
    middle = rest.astype(BF)
    return top, middle, (rest - middle.astype(F32)).astype(BF)


def iota(shape, dim):
    return lax.broadcasted_iota(jnp.int32, shape, dim)


def whole_spec(array):
    return pl.BlockSpec(array.shape, lambda *_: (0,) * array.ndim)


def rates_of(feature):
    lane = np.arange(feature)
    rates = np.exp((lane // 2).astype(np.float32) * np.float32(-2.0 * math.log(10000.0) / feature)).astype(np.float32)
    return rates, np.where(lane % 2 == 1, 0.5 * math.pi, 0.0).astype(np.float32)


def bounds_of(lengths_ref, row):
    starts, ends, at = [], [], jnp.int32(0)
    for item in range(lengths_ref.shape[1]):
        starts.append(at)
        at = at + lengths_ref[row, item]
        ends.append(at)
    return starts, ends


def keys_values_kernel(
    first_block, row_blocks, lengths_ref, place_ref,
    memory_ref, pad_ref, angles_ref, local_sin_ref, local_cos_ref, wk_own, wv_own, part_ref, rest_ref, bias_ref, *refs,
):
    memory_in_ref, gate_ref, keys_ref, values_ref, wk_ref, wv_ref = refs[-6:]
    block = pl.program_id(0) + first_block
    row, block = block // row_blocks, lax.rem(block, row_blocks)
    parts = memory_ref.shape[0] // TILE
    items = lengths_ref.shape[1]
    columns = wk_own.shape[1]

    @pl.when(pl.program_id(0) == 0)
    def _():
        assemble(wk_ref, wk_own, part_ref, rest_ref, (0, 0), place_ref, 1)
        assemble(wv_ref, wv_own, part_ref, rest_ref, (0, columns), place_ref, 1)

    starts, ends = bounds_of(lengths_ref, row)
    lane = iota((TILE, LANES), 1)
    lane_starts, lane_ends = (
        sum(jnp.where(iota((1, LANES), 1) == item, one, 0) for item, one in enumerate(ones)) for ones in (starts, ends)
    )
    tiles, crowded = [], jnp.bool_(False)
    for part in range(parts):
        base = (block * parts + part) * TILE
        here = slice(part * TILE, (part + 1) * TILE)
        first = sum((one <= base).astype(jnp.int32) for one in ends)
        last = sum((one < base + TILE).astype(jnp.int32) for one in starts) - 1

        def start_of(item):
            return sum(jnp.where(item == index, one, 0) for index, one in enumerate(starts))

        def place(item, base=base):
            shift = (base - start_of(item)).astype(F32)
            angle = shift * angles_ref[0:1, :] + angles_ref[1:2, :]
            return jnp.sin(angle) * local_cos_ref[...] + jnp.cos(angle) * local_sin_ref[...]

        def later(item, held, base=base, place=place):
            return jnp.where(iota((TILE, 1), 0) + base >= start_of(item), place(item), held)

        position = later(jnp.minimum(first + 1, items - 1), place(first))
        memory_in_ref[here, :] = (memory_ref[here, :].astype(F32) + position).astype(BF)
        tiles.append((here, base, first, last, place, start_of))
        crowded = crowded | (last > first + 1)
    own_bias, line = bias_ref[...], part_ref.shape[0] - BIAS_LINES
    lines = part_ref[line : line + BIAS_LINES, :columns].astype(F32)
    other_bias = lines[0:1] + lines[1:2] + lines[2:3]
    low = place_ref[0] == 0
    biases = jnp.where(low, own_bias, other_bias), jnp.where(low, other_bias, own_bias)
    for half in range(2):
        here = slice(half * columns, (half + 1) * columns)
        values_ref[half] = (mm(memory_ref[...], wv_ref[:, here]) + biases[half]).astype(BF)
    for half in range(2):
        here = slice(half * columns, (half + 1) * columns)
        keys_ref[half] = mm(memory_in_ref[...], wk_ref[:, here]).astype(BF)
    for here, base, *_ in tiles:
        pad = jnp.transpose(jnp.broadcast_to(pad_ref[pl.ds(row, 1), here].astype(F32), (LANES, TILE)))
        slot_grid = iota((TILE, LANES), 0) + base
        mine = (slot_grid >= lane_starts) & (slot_grid < lane_ends)
        is_open = mine & ((pad > 0.0) | (slot_grid == lane_starts))
        gate = jnp.where(lane < items, jnp.where(is_open, 0.0, 1.0), jnp.where(lane < items + 3, 1.0, 0.0))
        gate_ref[here, :] = gate.astype(BF)

    @pl.when(crowded)
    def _():
        for here, base, first, last, place, start_of in tiles:

            def patch(item, carry, here=here, base=base, place=place, start_of=start_of):
                with_place = (memory_ref[here, :].astype(F32) + place(item)).astype(BF)
                slots = iota((TILE, 1), 0) + base
                memory_in_ref[here, :] = jnp.where(slots >= start_of(item), with_place, memory_in_ref[here, :])
                return carry

            lax.fori_loop(first + 2, last + 1, patch, 0)
        for half in range(2):
            keys_ref[half] = mm(memory_in_ref[...], wk_ref[:, half * columns : (half + 1) * columns]).astype(BF)


def keys_values(lengths, place, memory, key_pad, wk_own, wv_own, part, rest, bias, first, blocks, held):
    rows, slots = key_pad.shape
    total, feature = memory.shape
    columns = wk_own.shape[1]
    steps = slots // BLOCK
    rates, turn = rates_of(feature)
    local = np.arange(TILE)[:, None] * rates.astype(np.float64)
    fixed = [jnp.asarray(np.stack([rates, turn])), jnp.asarray(np.sin(local).astype(np.float32)), jnp.asarray(np.cos(local).astype(np.float32))]
    fixed += [wk_own, wv_own, part, rest, bias]
    slab = lambda columns: pl.BlockSpec((BLOCK, columns), lambda t, *_: (first + t, 0))
    halves = pl.BlockSpec((2, BLOCK, columns), lambda t, *_: (0, first + t, 0))
    full = pl.BlockSpec((feature, 2 * columns), lambda *_: (0, 0))
    held = [] if held is None else list(held)
    return pl.pallas_call(
        functools.partial(keys_values_kernel, first, steps),
        grid_spec=pltpu.PrefetchScalarGridSpec(
            num_scalar_prefetch=2,
            grid=(blocks,),
            in_specs=[slab(feature), pl.BlockSpec((rows, BLOCK), lambda t, *_: (0, lax.rem(first + t, steps)))] + [whole_spec(one) for one in fixed]
            + [pl.BlockSpec(memory_space=pl.ANY)] * len(held),
            out_specs=[slab(feature), slab(LANES), halves, halves, full, full],
        ),
        out_shape=[
            jax.ShapeDtypeStruct((total, feature), BF),
            jax.ShapeDtypeStruct((total, LANES), BF),
            jax.ShapeDtypeStruct((2, total, columns), BF),
            jax.ShapeDtypeStruct((2, total, columns), BF),
            jax.ShapeDtypeStruct((feature, 2 * columns), BF),
            jax.ShapeDtypeStruct((feature, 2 * columns), BF),
        ],
        input_output_aliases={4 + len(fixed) + one: one for one in range(len(held))},
        compiler_params=pltpu.CompilerParams(vmem_limit_bytes=VMEM),
        name="keys_values",
    )(lengths, place, memory, key_pad, *fixed, *held)


def block_rows(pair_transposed):
    blank = jnp.zeros((HEAD, pair_transposed.shape[1]), BF)
    upper = jnp.concatenate([pair_transposed[:HEAD], blank], axis=1)
    lower = jnp.concatenate([blank, pair_transposed[HEAD:]], axis=1)
    return jnp.concatenate([upper, lower], axis=0)


def block_columns(pair):
    twice = jnp.concatenate([pair, pair], axis=0)
    same = (iota(twice.shape, 0) < pair.shape[0]) == (iota(twice.shape, 1) < HEAD)
    return jnp.where(same, twice, jnp.zeros_like(twice))


def gate_rows(item, items, closed, added):
    row = iota((LANES, 2 * LANES), 0)
    value = jnp.where(row == item, closed, 0.0)
    if added is not None:
        for place, part in enumerate(split3(added)):
            value = jnp.where(row == items + place, part.astype(F32), value)
    return value.astype(BF)


def window_of(start, slots):
    return pl.multiple_of(jnp.minimum((start // 16) * 16, slots - WINDOW), 16)


def cross_forward_kernel(lengths_ref, keys_ref, values_ref, gate_ref, qt_ref, mix_ref, mixt_ref, lse_ref, scores_a, scores_b, probs_a, probs_b):
    row = pl.program_id(0)
    slots = keys_ref.shape[0]
    items = lengths_ref.shape[1]
    starts, ends = bounds_of(lengths_ref, row)
    works = [(item, pair) for pair in range(keys_ref.shape[1] // PAIR) for item in range(items)]
    scores_of, probs_of = (scores_a, scores_b), (probs_a, probs_b)
    largest, total = {}, {}
    size = WINDOW // CHUNKS

    def lanes(pair):
        return slice(pair * PAIR, (pair + 1) * PAIR)

    def prepare(work):
        item, pair = works[work]
        return jnp.concatenate([block_rows(qt_ref[item, lanes(pair), :]), gate_rows(item, items, FAR, None)], axis=0)

    def score(work, right, chunk):
        item, pair = works[work]
        rows = pl.ds(pl.multiple_of(window_of(starts[item], slots) + chunk * size, 16), size)
        part = mm(jnp.concatenate([keys_ref[rows, lanes(pair)], gate_ref[rows, :]], axis=1), right)
        scores_of[work % 2][chunk * size : (chunk + 1) * size, :] = part
        top = jnp.max(part.reshape(size // 8, 8, 2 * LANES), axis=0)
        largest[work] = top if chunk == 0 else jnp.maximum(largest[work], top)

    def soften(work, chunk):
        if chunk == 0:
            largest[work] = jnp.max(largest[work], axis=0, keepdims=True)
        here = slice(chunk * size, (chunk + 1) * size)
        expo = jnp.exp(scores_of[work % 2][here, :] - largest[work])
        probs_of[work % 2][here, :] = expo.astype(BF)
        add = jnp.sum(expo.reshape(size // 8, 8, 2 * LANES), axis=0)
        total[work] = add if chunk == 0 else total[work] + add

    def finish(work):
        item, pair = works[work]
        rows = pl.ds(window_of(starts[item], slots), WINDOW)
        sums = jnp.sum(total[work], axis=0, keepdims=True)
        both = mm_tn(values_ref[rows, lanes(pair)], probs_of[work % 2][...]) / sums
        mixed = own_blocks(both)
        mixt_ref[item, lanes(pair), :] = mixed
        mix_ref[item, :, lanes(pair)] = jnp.transpose(mixed).astype(BF)
        lse_ref[pair, item : item + 1, :] = largest[work] + jnp.log(sums)

    for step in range(len(works) + 2):
        right = prepare(step) if step < len(works) else None
        if step >= 2:
            finish(step - 2)
        for chunk in range(CHUNKS):
            if step < len(works):
                score(step, right, chunk)
            if 1 <= step <= len(works):
                soften(step - 1, chunk)


def cross_forward(lengths, keys, values, gate, qt):
    rows, items = lengths.shape
    slots, columns = keys.shape[1] // rows, keys.shape[2]
    width = 2 * columns
    pairs = width // PAIR
    by_half = pl.BlockSpec((None, slots, columns), lambda r, p, *_: (p, r, 0))
    turned = pl.BlockSpec((items, columns, LANES), lambda r, p, *_: (r, p, 0))
    return pl.pallas_call(
        cross_forward_kernel,
        grid_spec=pltpu.PrefetchScalarGridSpec(
            num_scalar_prefetch=1,
            grid=(rows, 2),
            in_specs=[by_half, by_half, pl.BlockSpec((slots, LANES), lambda r, p, *_: (r, 0)), turned],
            out_specs=[
                pl.BlockSpec((items, LANES, columns), lambda r, p, *_: (r, 0, p)),
                turned,
                pl.BlockSpec((pairs // 2, items, 2 * LANES), lambda r, p, *_: (r * 2 + p, 0, 0)),
            ],
            scratch_shapes=[pltpu.VMEM((WINDOW, 2 * LANES), F32)] * 2 + [pltpu.VMEM((WINDOW, 2 * LANES), BF)] * 2,
        ),
        out_shape=[
            jax.ShapeDtypeStruct((rows * items, LANES, width), BF),
            jax.ShapeDtypeStruct((rows * items, width, LANES), F32),
            jax.ShapeDtypeStruct((rows * pairs, items, 2 * LANES), F32),
        ],
        compiler_params=pltpu.CompilerParams(vmem_limit_bytes=VMEM),
        name="cross_forward",
    )(lengths, keys, values, gate, qt)


def cross_backward_kernel(lengths_ref, keys_ref, values_ref, gate_ref, qt_ref, gt_ref, mixt_ref, lse_ref, dk_ref, dv_ref, dq_ref):
    row = pl.program_id(0)
    slots = keys_ref.shape[0]
    items = lengths_ref.shape[1]
    starts, ends = bounds_of(lengths_ref, row)

    def one_item(item):
        at = window_of(starts[item], slots)
        rows = pl.ds(at, WINDOW)
        qt, gt = qt_ref[item], gt_ref[item]
        products = gt.astype(F32) * mixt_ref[item]
        inner = jnp.concatenate([jnp.sum(products[:HEAD], axis=0, keepdims=True), jnp.sum(products[HEAD:], axis=0, keepdims=True)], axis=1)
        score_right = jnp.concatenate([block_rows(qt), gate_rows(item, items, FAR, -lse_ref[0, item : item + 1, :])], axis=0)
        slope_right = jnp.concatenate([block_rows(gt), gate_rows(item, items, 0.0, -inner)], axis=0)
        keys, gate = keys_ref[rows, :], gate_ref[rows, :]
        probs = jnp.exp(mm(jnp.concatenate([keys, gate], axis=1), score_right))
        slopes = mm(jnp.concatenate([values_ref[rows, :], gate], axis=1), slope_right)
        low_scores = (probs * slopes).astype(BF)
        slot = iota((WINDOW, 1), 0) + at
        mine = (slot >= starts[item]) & (slot < ends[item])
        grad_values = mm(probs.astype(BF), block_columns(jnp.transpose(gt))).astype(BF)
        dv_ref[rows, :] = jnp.where(mine, grad_values, dv_ref[rows, :])
        grad_keys = mm(low_scores, block_columns(jnp.transpose(qt))).astype(BF)
        dk_ref[rows, :] = jnp.where(mine, grad_keys, dk_ref[rows, :])
        both = mm_tn(keys, low_scores)
        dq_ref[item] = jnp.transpose(jnp.concatenate([both[:HEAD, :LANES], both[HEAD:, LANES:]], axis=0) * SCALE).astype(BF)

    for item in range(items):
        one_item(item)


def cross_backward(lengths, keys, values, gate, qt, gt, mixt, lse):
    rows, items = lengths.shape
    _, total, columns = keys.shape
    slots, width = total // rows, 2 * columns
    pairs, inside = width // PAIR, columns // PAIR
    by_pair = pl.BlockSpec((None, slots, PAIR), lambda r, p, *_: (p // inside, r, p % inside))
    turned = pl.BlockSpec((items, PAIR, LANES), lambda r, p, *_: (r, p, 0))
    return pl.pallas_call(
        cross_backward_kernel,
        grid_spec=pltpu.PrefetchScalarGridSpec(
            num_scalar_prefetch=1,
            grid=(rows, pairs),
            in_specs=[
                by_pair, by_pair,
                pl.BlockSpec((slots, LANES), lambda r, p, *_: (r, 0)),
                turned, turned, turned,
                pl.BlockSpec((1, items, 2 * LANES), lambda r, p, *_: (r * pairs + p, 0, 0)),
            ],
            out_specs=[by_pair, by_pair, pl.BlockSpec((items, LANES, PAIR), lambda r, p, *_: (r, 0, p))],
        ),
        out_shape=[
            jax.ShapeDtypeStruct((2, total, columns), BF),
            jax.ShapeDtypeStruct((2, total, columns), BF),
            jax.ShapeDtypeStruct((rows * items, LANES, width), BF),
        ],
        compiler_params=pltpu.CompilerParams(vmem_limit_bytes=VMEM),
        name="cross_backward",
    )(lengths, keys, values, gate, qt, gt, mixt, lse)


def memory_weights_kernel(mine_ref, dk_ref, dv_ref, memory_ref, memory_in_ref, out_ref, vec_ref, wk_acc, wv_acc, bv_acc):
    step = pl.program_id(0)
    block, columns = dk_ref.shape

    @pl.when(step == 0)
    def _():
        wk_acc[...] = jnp.zeros_like(wk_acc)
        wv_acc[...] = jnp.zeros_like(wv_acc)
        bv_acc[...] = jnp.zeros_like(bv_acc)

    wk_acc[...] += mm_tn(dk_ref[...], memory_in_ref[...])
    wv_acc[...] += mm_tn(dv_ref[...], memory_ref[...])
    bv_acc[...] += jnp.sum(dv_ref[...].astype(F32).reshape(block // 8, 8, columns), axis=0)

    @pl.when(step == pl.num_programs(0) - 1)
    def _():
        out_ref[...] = jnp.concatenate([jnp.transpose(wk_acc[...]), jnp.transpose(wv_acc[...])], axis=1).astype(BF)
        vec_ref[...] = jnp.concatenate([jnp.sum(bv_acc[...], axis=0, keepdims=True), jnp.zeros((1, columns), F32)], axis=1)


def memory_weights(place, dk, dv, memory, memory_in, columns):
    total, feature = memory.shape
    own = pl.BlockSpec((None, SUMS_BLOCK, columns), lambda t, place: (place[0], t, 0))
    slab = pl.BlockSpec((SUMS_BLOCK, feature), lambda t, *_: (t, 0))
    whole = lambda shape: pl.BlockSpec(shape, lambda t, *_: (0,) * len(shape))
    return pl.pallas_call(
        memory_weights_kernel,
        grid_spec=pltpu.PrefetchScalarGridSpec(
            num_scalar_prefetch=1,
            grid=(total // SUMS_BLOCK,),
            in_specs=[own, own, slab, slab],
            out_specs=[whole((feature, 2 * columns)), whole((1, 2 * columns))],
            scratch_shapes=[pltpu.VMEM((columns, feature), F32), pltpu.VMEM((columns, feature), F32), pltpu.VMEM((8, columns), F32)],
        ),
        out_shape=[jax.ShapeDtypeStruct((feature, 2 * columns), BF), jax.ShapeDtypeStruct((1, 2 * columns), F32)],
        compiler_params=pltpu.CompilerParams(vmem_limit_bytes=VMEM),
        name="memory_weights",
    )(place, dk, dv, memory, memory_in)


def memory_gradient_kernel(dk_low, dk_high, dv_low, dv_high, wk_ref, wv_ref, *rest):
    dk = jnp.concatenate([dk_low[...], dk_high[...]], axis=1)
    dv = jnp.concatenate([dv_low[...], dv_high[...]], axis=1)
    rest[-1][...] = mm_nt(dk, wk_ref[...]) + mm_nt(dv, wv_ref[...])


def memory_gradient(dk, dv, wk, wv, first, blocks, held):
    _, total, columns = dk.shape
    feature = wk.shape[0]
    half = lambda which: pl.BlockSpec((None, BLOCK, columns), lambda t: (which, first + t, 0))
    operands, specs = [dk, dk, dv, dv, wk, wv], [half(0), half(1), half(0), half(1), whole_spec(wk), whole_spec(wv)]
    if held is not None:
        operands, specs = operands + [held], specs + [pl.BlockSpec(memory_space=pl.ANY)]
    return pl.pallas_call(
        memory_gradient_kernel,
        grid=(blocks,),
        in_specs=specs,
        out_specs=pl.BlockSpec((BLOCK, feature), lambda t: (first + t, 0)),
        out_shape=jax.ShapeDtypeStruct((total, feature), F32),
        input_output_aliases={} if held is None else {6: 0},
        compiler_params=pltpu.CompilerParams(vmem_limit_bytes=VMEM),
        name="memory_gradient",
    )(*operands)


def assemble(full_ref, own_ref, part_ref, rest_ref, corner, place_ref, dim):
    mine, bit = place_ref[0], place_ref[1]
    rows, columns = own_ref.shape
    half = rows // 2
    line, lane = corner
    for source, offset in ((part_ref, bit * half), (rest_ref, (1 - bit) * half)):
        if dim == 1:
            at = (pl.ds(pl.multiple_of(offset, half), half), pl.ds(pl.multiple_of((1 - mine) * columns, columns), columns))
        elif dim == 0:
            at = (pl.ds(pl.multiple_of((1 - mine) * rows + offset, half), half), slice(None))
        else:
            at = (1 - mine, pl.ds(pl.multiple_of(offset, half), half), slice(None))
        full_ref[at] = source[line : line + half, lane : lane + columns]
    if dim == 1:
        full_ref[:, pl.ds(pl.multiple_of(mine * columns, columns), columns)] = own_ref[...]
    elif dim == 0:
        full_ref[pl.ds(pl.multiple_of(mine * rows, rows), rows), :] = own_ref[...]
    else:
        full_ref[mine] = own_ref[...]


def bias_of(place_ref, own_ref, other_ref, line, lane, size):
    if size <= own_ref.shape[1] - lane:
        own, other = own_ref[line : line + 1, lane : lane + size], other_ref[line : line + 1, lane : lane + size]
    else:
        lines = -(-size // own_ref.shape[1])
        own, other = (jnp.concatenate([ref[line + one : line + one + 1, :] for one in range(lines)], axis=1)[:, :size] for ref in (own_ref, other_ref))
    first = place_ref[0] == 0
    return jnp.where(first, own, other), jnp.where(first, other, own)


def assemble_token(wq, wk, wv, cwq, wo, wq_own, wk_own, wv_own, cwq_own, wo_own, part_ref, rest_ref, place_ref):
    rows, columns = wq_own.shape
    assemble(wq, wq_own, part_ref, rest_ref, (0, 0), place_ref, 1)
    assemble(wk, wk_own, part_ref, rest_ref, (0, columns), place_ref, 1)
    assemble(wv, wv_own, part_ref, rest_ref, (rows // 2, 0), place_ref, 1)
    assemble(cwq, cwq_own, part_ref, rest_ref, (rows // 2, columns), place_ref, 1)
    assemble(wo, wo_own, part_ref, rest_ref, (rows, 0), place_ref, 0)


def give_halves(place_ref, sums, sent_ref, kept_ref):
    half = sent_ref.shape[0]
    sent_ref[...] = sums[pl.ds(pl.multiple_of((1 - place_ref[1]) * half, half), half), :]
    kept_ref[...] = sums[pl.ds(pl.multiple_of(place_ref[1] * half, half), half), :]


def normalize(value):
    center = value - jnp.mean(value, axis=-1, keepdims=True)
    spread = lax.rsqrt(jnp.mean(center * center, axis=-1, keepdims=True) + 1e-05)
    return center * spread, spread


def normalize_back(grad, normed, spread, gain):
    scaled = grad * gain
    inner = jnp.mean(scaled * normed, axis=-1, keepdims=True)
    return (scaled - jnp.mean(scaled, axis=-1, keepdims=True) - normed * inner) * spread


def total_rows(value):
    return jnp.sum(value, axis=0, keepdims=True)


def cut_items(value):
    blank = jnp.zeros((LANES - SPAN, value.shape[1]), value.dtype)
    return [jnp.concatenate([value[at : at + SPAN], blank], axis=0) for at in range(0, value.shape[0], SPAN)]


def join_items(pieces):
    return jnp.concatenate([one[:SPAN] for one in pieces], axis=0)


def self_probs(keys, qt_block):
    scores = mm(keys, qt_block)
    scores = jnp.where(iota(scores.shape, 0) < SPAN, scores, FAR)
    expo = jnp.exp(scores - jnp.max(scores, axis=0, keepdims=True))
    return expo / jnp.sum(expo, axis=0, keepdims=True)


def own_blocks(both):
    return jnp.concatenate([both[:HEAD, :LANES], both[HEAD:, LANES:]], axis=0)


def token_forward_kernel(
    place_ref, tokens_ref, embed_ref,
    wq_own, wk_own, wv_own, cwq_own, wo_own, part_ref, rest_ref, bias_own, bias_other, so_bias, gain_ref, shift_ref,
    q_ref, k_ref, v_ref, mix_ref, resid_ref, normed_ref, qt_ref,
    wq, wk, wv, wo, cwq,
):
    @pl.when(pl.program_id(0) == 0)
    def _():
        assemble_token(wq, wk, wv, cwq, wo, wq_own, wk_own, wv_own, cwq_own, wo_own, part_ref, rest_ref, place_ref)

    width = wq.shape[1]
    half = width // 2
    bias = lambda line, lane: jnp.concatenate(bias_of(place_ref, bias_own, bias_other, line, lane, half), axis=1)
    tokens = tokens_ref[...]
    items = tokens.shape[0] // SPAN
    query_pos = jnp.concatenate([embed_ref[...]] * items, axis=0)
    tokens_wide = tokens.astype(F32)
    shared_in = (tokens_wide + query_pos).astype(BF)
    q = (mm(shared_in, wq[...]) + bias(0, 0)).astype(BF)
    k = mm(shared_in, wk[...]).astype(BF)
    v = (mm(tokens, wv[...]) + bias(0, half)).astype(BF)
    q_ref[...], k_ref[...], v_ref[...] = q, k, v
    q_items, k_items, v_items = (cut_items(one.astype(F32)) for one in (q, k, v))
    mixes = []
    for item in range(items):
        qt = jnp.transpose(q_items[item] * SCALE).astype(BF)
        keys, values = k_items[item].astype(BF), v_items[item].astype(BF)
        mixed = []
        for at in range(0, width, PAIR):
            probs = self_probs(keys[:, at : at + PAIR], block_rows(qt[at : at + PAIR]))
            mixed.append(own_blocks(mm_tn(values[:, at : at + PAIR], probs.astype(BF))))
        mixes.append(jnp.transpose(jnp.concatenate(mixed, axis=0)))
    mix = join_items(mixes).astype(BF)
    mix_ref[...] = mix
    resid = tokens_wide + (mm(mix, wo[...]) + so_bias[...])
    resid_ref[...] = resid
    normed, _ = normalize(resid)
    normed = normed * gain_ref[...] + shift_ref[...]
    normed_ref[...] = normed
    cross_in = (normed + query_pos).astype(BF)
    cross_q = (mm(cross_in, cwq[...]) + bias(1, 0)).astype(BF).astype(F32) * SCALE
    for item, one in enumerate(cut_items(cross_q)):
        qt_ref[item] = jnp.transpose(one).astype(BF)


def token_forward(place, tokens, embed, weights, part, rest, bias_own, bias_other, so_bias, gain, shift, rows):
    token_count, feature = tokens.shape
    width = 2 * weights[0].shape[1]
    size = token_count // rows
    items = size // SPAN
    slab = lambda columns: pl.BlockSpec((size, columns), lambda r, *_: (r, 0))
    flat = [*weights, part, rest]
    fixed = [bias_own, bias_other, so_bias, gain, shift]
    return pl.pallas_call(
        token_forward_kernel,
        grid_spec=pltpu.PrefetchScalarGridSpec(
            num_scalar_prefetch=1,
            grid=(rows,),
            in_specs=[slab(feature), whole_spec(embed)] + [whole_spec(one) for one in flat + fixed],
            out_specs=[slab(width)] * 4 + [slab(feature)] * 2 + [pl.BlockSpec((items, width, LANES), lambda r, *_: (r, 0, 0))],
            scratch_shapes=[pltpu.VMEM((feature, width), BF)] * 3 + [pltpu.VMEM((width, feature), BF), pltpu.VMEM((feature, width), BF)],
        ),
        out_shape=[jax.ShapeDtypeStruct((token_count, width), BF)] * 4
        + [jax.ShapeDtypeStruct((token_count, feature), F32)] * 2
        + [jax.ShapeDtypeStruct((rows * items, width, LANES), BF)],
        compiler_params=pltpu.CompilerParams(vmem_limit_bytes=VMEM),
        name="token_forward",
    )(place, tokens, embed, *flat, *fixed)


def gelu_both(pre):
    inner = math.sqrt(2.0 / math.pi)
    square = pre * pre
    bend = jnp.tanh(pre * (inner + (inner * 0.044715) * square))
    lift = 0.5 + 0.5 * bend
    slope = lift + (0.5 * pre) * (1.0 - bend * bend) * (inner + (3.0 * inner * 0.044715) * square)
    return pre * lift, slope


def feed_kernel(
    place_ref, mix_in_ref, normed_one_ref, cotangent_ref,
    wo_own, w1_own, w2_own, token_part, token_rest, part_ref, rest_ref, bias_own, bias_other,
    co_bias, gain2_ref, shift2_ref, f_bias, gain3_ref, shift3_ref,
    out_ref, grad_two_ref, gt_ref, sums_ref,
    wo, w1, w2, hidden, slope, low_pre, mix_scr, w1_acc, w2_acc, wo_acc, b1_acc, vec_acc, semaphores,
):
    row = pl.program_id(0)
    mine = place_ref[0]
    columns = wo_acc.shape[0]
    width = wo.shape[0]
    size = out_ref.shape[0]
    hidden_half = w1.shape[1]

    half, bit = hidden_half // 2, place_ref[1]

    def fetch(weight, own_ref, line, at):
        pieces = [(own_ref, weight.at[mine])]
        for source, offset in ((part_ref, bit * half), (rest_ref, (1 - bit) * half)):
            pieces.append((source.at[line : line + half, :], weight.at[1 - mine, pl.ds(pl.multiple_of(offset, half), half), :]))
        return [pltpu.make_async_copy(*one, semaphores.at[at + index]) for index, one in enumerate(pieces)]

    fetch_one, fetch_two = fetch(w1, w1_own, 0, 0), fetch(w2, w2_own, half, 3)

    @pl.when(row == 0)
    def _():
        for one in (*fetch_one, *fetch_two):
            one.start()
        assemble(wo, wo_own, token_part, token_rest, (wo.shape[1] + columns // 2, 0), place_ref, 0)
        for acc in (w1_acc, w2_acc, wo_acc, b1_acc, vec_acc):
            acc[...] = jnp.zeros_like(acc)

    mix = join_items([mix_in_ref[item].astype(F32) for item in range(mix_in_ref.shape[0])]).astype(BF)
    mix_scr[...] = mix
    normed2, spread2 = normalize(normed_one_ref[...] + (mm(mix, wo[...]) + co_bias[...]))
    normed_two = normed2 * gain2_ref[...] + shift2_ref[...]
    feed_in = normed_two.astype(BF)
    b1 = bias_of(place_ref, bias_own, bias_other, 2, 0, hidden_half)
    total = normed_two + f_bias[...]

    @pl.when(row == 0)
    def _():
        for one in fetch_one:
            one.wait()

    for part in range(2):
        one, rise = gelu_both(mm_nt(feed_in, w1[part]) + b1[part])
        hidden[part] = one.astype(BF)
        slope[part] = rise

    @pl.when(row == 0)
    def _():
        for one in fetch_two:
            one.wait()

    for part in range(2):
        total = total + mm(hidden[part], w2[part])
    normed3, spread3 = normalize(total)
    out_ref[...] = (normed3 * gain3_ref[...] + shift3_ref[...]).astype(BF)
    cotangent = cotangent_ref[...].astype(F32)
    grad_three = normalize_back(cotangent, normed3, spread3, gain3_ref[...])
    low_three = grad_three.astype(BF)
    back = grad_three
    for part in range(2):
        low = (mm_nt(low_three, w2[part]) * slope[part]).astype(BF)
        low_pre[part] = low
        back = back + mm(low, w1[part])
    grad_two = normalize_back(back, normed2, spread2, gain2_ref[...])
    grad_two_ref[...] = grad_two
    low_two = grad_two.astype(BF)
    own_pre = low_pre[mine]
    w2_acc[...] += mm_tn(hidden[mine], low_three)
    w1_acc[...] += mm_tn(own_pre, feed_in)
    b1_acc[...] += total_rows(own_pre.astype(F32))
    if columns == width:
        own = slice(None)
    else:
        own = pl.ds(pl.multiple_of(mine * columns, columns), columns)
    wo_acc[...] += mm_tn(mix_scr[:, own], low_two)
    vec_acc[...] += jnp.concatenate(
        [
            total_rows(cotangent * normed3), total_rows(cotangent), total_rows(low_three.astype(F32)),
            total_rows(back * normed2), total_rows(back), total_rows(low_two.astype(F32)),
            jnp.zeros((2, vec_acc.shape[1]), F32),
        ],
        axis=0,
    )
    grad_mix = mm_nt(low_two, wo[...]).astype(BF).astype(F32)
    for item, one in enumerate(cut_items(grad_mix)):
        gt_ref[item] = jnp.transpose(one).astype(BF)

    @pl.when(row == pl.num_programs(0) - 1)
    def _():
        sums_ref[:hidden_half, :] = w1_acc[...].astype(BF)
        sums_ref[hidden_half : 2 * hidden_half, :] = w2_acc[...].astype(BF)
        sums_ref[2 * hidden_half : 2 * hidden_half + columns, :] = wo_acc[...].astype(BF)
        feature = vec_acc.shape[1]
        lines = [b1_acc[:, at : at + feature] for at in range(0, hidden_half, feature)]
        lines[-1] = jnp.concatenate([lines[-1], jnp.zeros((1, feature - lines[-1].shape[1]), F32)], axis=1)
        lines.append(jnp.zeros((FEED_LINES - 8 - len(lines), feature), F32))
        sums_ref[2 * hidden_half + columns :, :] = jnp.concatenate([vec_acc[...], *lines], axis=0).astype(BF)


def feed(place, mix, normed_one, cotangent, weights, parts, bias_own, bias_other, vectors, rows, columns):
    token_count, feature = normed_one.shape
    width = mix.shape[2]
    size = token_count // rows
    items = size // SPAN
    hidden_half = weights[1].shape[0]
    lines = 2 * hidden_half + columns + FEED_LINES
    slab = lambda columns: pl.BlockSpec((size, columns), lambda r, *_: (r, 0))
    whole = lambda shape: pl.BlockSpec(shape, lambda r, *_: (0,) * len(shape))
    flat = [*weights, *parts]
    fixed = [bias_own, bias_other, *vectors]
    far = pl.BlockSpec(memory_space=pl.ANY)
    return pl.pallas_call(
        feed_kernel,
        grid_spec=pltpu.PrefetchScalarGridSpec(
            num_scalar_prefetch=1,
            grid=(rows,),
            in_specs=[pl.BlockSpec((items, LANES, width), lambda r, *_: (r, 0, 0)), slab(feature), slab(feature)]
            + [far if index in (1, 2, 5, 6) else whole_spec(one) for index, one in enumerate(flat + fixed)],
            out_specs=[
                slab(feature), slab(feature), pl.BlockSpec((items, width, LANES), lambda r, *_: (r, 0, 0)),
                whole((lines, feature)),
            ],
            scratch_shapes=[
                pltpu.VMEM((width, feature), BF),
                pltpu.VMEM((2, hidden_half, feature), BF),
                pltpu.VMEM((2, hidden_half, feature), BF),
                pltpu.VMEM((2, size, hidden_half), BF),
                pltpu.VMEM((2, size, hidden_half), F32),
                pltpu.VMEM((2, size, hidden_half), BF),
                pltpu.VMEM((size, width), BF),
                pltpu.VMEM((hidden_half, feature), F32),
                pltpu.VMEM((hidden_half, feature), F32),
                pltpu.VMEM((columns, feature), F32),
                pltpu.VMEM((1, hidden_half), F32),
                pltpu.VMEM((8, feature), F32),
                pltpu.SemaphoreType.DMA((6,)),
            ],
        ),
        out_shape=[
            jax.ShapeDtypeStruct((token_count, feature), BF),
            jax.ShapeDtypeStruct((token_count, feature), F32),
            jax.ShapeDtypeStruct((rows * items, width, LANES), BF),
            jax.ShapeDtypeStruct((lines, feature), BF),
        ],
        compiler_params=pltpu.CompilerParams(vmem_limit_bytes=VMEM),
        name="feed",
    )(place, mix, normed_one, cotangent, *flat, *fixed)


def token_backward_kernel(
    place_ref, dq_in_ref, grad_two_ref, resid_ref, normed_ref, tokens_ref, embed_ref, q_ref, k_ref, v_ref, mix_ref,
    memory_sums_ref, memory_vec_ref,
    wq_own, wk_own, wv_own, cwq_own, wo_own, part_ref, rest_ref, gain_ref,
    grad_tokens_ref, sent_ref, kept_ref,
    wq, wk, wv, wo, cwq, cross_dq, low_q, low_k, low_v, cwq_acc, wq_acc, wk_acc, wv_acc, wo_acc, embed_acc, vec_acc, sums,
):
    row = pl.program_id(0)
    mine = place_ref[0]
    width = wq.shape[1]
    columns = wo_acc.shape[0]

    @pl.when(row == 0)
    def _():
        assemble_token(wq, wk, wv, cwq, wo, wq_own, wk_own, wv_own, cwq_own, wo_own, part_ref, rest_ref, place_ref)
        for acc in (cwq_acc, wq_acc, wk_acc, wv_acc, wo_acc, embed_acc, vec_acc):
            acc[...] = jnp.zeros_like(acc)

    if columns == width:
        own = slice(None)
    else:
        own = pl.ds(pl.multiple_of(mine * columns, columns), columns)
    tokens = tokens_ref[...]
    items = tokens.shape[0] // SPAN
    query_pos = jnp.concatenate([embed_ref[...]] * items, axis=0)
    shared_in = (tokens.astype(F32) + query_pos).astype(BF)
    cross_in = (normed_ref[...] + query_pos).astype(BF)
    cross_dq[...] = join_items([dq_in_ref[item].astype(F32) for item in range(items)]).astype(BF)
    cwq_acc[...] += mm_tn(cross_in, cross_dq[:, own])
    grad_cross_in = mm_nt(cross_dq[...], cwq[...])
    back = grad_two_ref[...] + grad_cross_in
    normed, spread = normalize(resid_ref[...])
    grad_one = normalize_back(back, normed, spread, gain_ref[...])
    low_one = grad_one.astype(BF)
    wo_acc[...] += mm_tn(mix_ref[:, own], low_one)
    g_items = cut_items(mm_nt(low_one, wo[...]).astype(BF).astype(F32))
    q_items = cut_items(q_ref[...].astype(F32) * SCALE)
    k_items, v_items = cut_items(k_ref[...].astype(F32)), cut_items(v_ref[...].astype(F32))
    all_dq, all_dk, all_dv = [], [], []
    for item in range(items):
        qt, gt = jnp.transpose(q_items[item]).astype(BF), jnp.transpose(g_items[item]).astype(BF)
        qn, gn, keys, values = (one[item].astype(BF) for one in (q_items, g_items, k_items, v_items))
        one_dq, one_dk, one_dv = [], [], []
        for at in range(0, width, PAIR):
            here = slice(at, at + PAIR)
            probs = self_probs(keys[:, here], block_rows(qt[here]))
            slopes = mm(values[:, here], block_rows(gt[here]))
            inner = jnp.sum(probs * slopes, axis=0, keepdims=True)
            low = (probs * (slopes - inner)).astype(BF)
            one_dv.append(mm(probs.astype(BF), block_columns(gn[:, here])))
            one_dk.append(mm(low, block_columns(qn[:, here])))
            one_dq.append(own_blocks(mm_tn(keys[:, here], low)))
        all_dq.append(jnp.transpose(jnp.concatenate(one_dq, axis=0) * SCALE))
        all_dk.append(jnp.concatenate(one_dk, axis=1))
        all_dv.append(jnp.concatenate(one_dv, axis=1))
    low_q[...] = join_items(all_dq).astype(BF)
    low_k[...] = join_items(all_dk).astype(BF)
    low_v[...] = join_items(all_dv).astype(BF)
    wq_acc[...] += mm_tn(shared_in, low_q[:, own])
    wk_acc[...] += mm_tn(shared_in, low_k[:, own])
    wv_acc[...] += mm_tn(tokens, low_v[:, own])
    grad_shared = mm_nt(low_q[...], wq[...]) + mm_nt(low_k[...], wk[...])
    grad_tokens_ref[...] = grad_one + grad_shared + mm_nt(low_v[...], wv[...])
    position = grad_shared + grad_cross_in
    embed_acc[...] += sum(position[at : at + SPAN] for at in range(0, position.shape[0], SPAN))
    vec_acc[...] += jnp.concatenate(
        [
            total_rows(back * normed), total_rows(back), total_rows(low_one.astype(F32)),
            total_rows(cross_dq[...].astype(F32)), total_rows(low_q[...].astype(F32)), total_rows(low_v[...].astype(F32)),
            jnp.zeros((2, width), F32),
        ],
        axis=0,
    )

    @pl.when(row == pl.num_programs(0) - 1)
    def _():
        feature = wq_acc.shape[0]
        for at, (one, two) in enumerate(((wq_acc, wk_acc), (wv_acc, cwq_acc))):
            sums[at * feature : (at + 1) * feature, :columns] = one[...].astype(BF)
            sums[at * feature : (at + 1) * feature, columns:] = two[...].astype(BF)
        sums[2 * feature : 3 * feature, :] = memory_sums_ref[...]
        sums[3 * feature : 3 * feature + columns, :] = wo_acc[...].astype(BF)
        at = 3 * feature + columns
        sums[at : at + LANES, :] = jnp.concatenate([embed_acc[...], jnp.zeros((LANES - SPAN, width), F32)], axis=0).astype(BF)
        vectors = jnp.concatenate([vec_acc[...], memory_vec_ref[...], jnp.zeros((7, width), F32)], axis=0)
        sums[at + LANES : at + LANES + 16, :] = vectors.astype(BF)
        sums[at + LANES + 16 :, :] = jnp.zeros((sums.shape[0] - at - LANES - 16, width), BF)
        give_halves(place_ref, sums, sent_ref, kept_ref)


def token_backward(place, dq, grad_two, resid, normed, tokens, embed, q, k, v, mix, memory_sums, memory_vec, weights, part, rest, gain, rows, columns, lines):
    token_count, feature = tokens.shape
    width = q.shape[1]
    size = token_count // rows
    items = size // SPAN
    slab = lambda columns: pl.BlockSpec((size, columns), lambda r, *_: (r, 0))
    whole = lambda shape: pl.BlockSpec(shape, lambda r, *_: (0,) * len(shape))
    flat = [memory_sums, memory_vec, *weights, part, rest]
    grads = [(feature, columns)] * 4 + [(columns, feature)]
    return pl.pallas_call(
        token_backward_kernel,
        grid_spec=pltpu.PrefetchScalarGridSpec(
            num_scalar_prefetch=1,
            grid=(rows,),
            in_specs=[pl.BlockSpec((items, LANES, width), lambda r, *_: (r, 0, 0))]
            + [slab(feature)] * 4 + [whole_spec(embed)] + [slab(width)] * 4
            + [whole_spec(one) for one in flat] + [whole_spec(gain)],
            out_specs=[slab(feature), whole((lines // 2, feature)), whole((lines // 2, feature))],
            scratch_shapes=[pltpu.VMEM((feature, width), BF)] * 3 + [pltpu.VMEM((width, feature), BF), pltpu.VMEM((feature, width), BF)]
            + [pltpu.VMEM((size, width), BF)] * 4
            + [pltpu.VMEM(one, F32) for one in grads] + [pltpu.VMEM((SPAN, feature), F32), pltpu.VMEM((8, feature), F32), pltpu.VMEM((lines, feature), BF)],
        ),
        out_shape=[jax.ShapeDtypeStruct((token_count, feature), F32)] + [jax.ShapeDtypeStruct((lines // 2, feature), BF)] * 2,
        compiler_params=pltpu.CompilerParams(vmem_limit_bytes=VMEM),
        name="token_backward",
    )(place, dq, grad_two, resid, normed, tokens, embed, q, k, v, mix, *flat, gain)


def pack_columns_kernel(place_ref, wk_ref, wv_ref, bias_ref, out_ref):
    half, columns = wk_ref.shape
    out_ref[:half, :columns] = wk_ref[...]
    out_ref[:half, columns:] = wv_ref[...]
    lines = [one.astype(F32) for one in split3(bias_ref[...])]
    lines = jnp.concatenate(lines + [jnp.zeros((BIAS_LINES - 3, columns), F32)], axis=0)
    out_ref[half:, :] = jnp.concatenate([lines, jnp.zeros_like(lines)], axis=1).astype(BF)


def pack_token_kernel(place_ref, wq_ref, wk_ref, wv_ref, cwq_ref, wo_ref, cwo_ref, out_ref):
    half, columns = wq_ref.shape
    out_ref[:half, :columns] = wq_ref[...]
    out_ref[:half, columns:] = wk_ref[...]
    out_ref[half : 2 * half, :columns] = wv_ref[...]
    out_ref[half : 2 * half, columns:] = cwq_ref[...]
    lines = wo_ref.shape[0]
    out_ref[2 * half : 2 * half + lines, :] = wo_ref[...]
    out_ref[2 * half + lines :, :] = cwo_ref[...]


def pack_lines_kernel(place_ref, w1_ref, w2_ref, out_ref):
    lines = w1_ref.shape[0]
    out_ref[:lines, :] = w1_ref[...]
    out_ref[lines:, :] = w2_ref[...]


def pack_half(kernel, bit, arrays, lines, columns):
    return pl.pallas_call(
        kernel,
        grid_spec=pltpu.PrefetchScalarGridSpec(
            num_scalar_prefetch=1, grid=(1,),
            in_specs=[
                whole_spec(one) if one.shape[0] == 1 else pl.BlockSpec((one.shape[0] // 2, one.shape[1]), lambda _, place: (place[0], 0))
                for one in arrays
            ],
            out_specs=pl.BlockSpec((lines, columns), lambda *_: (0, 0)),
        ),
        out_shape=jax.ShapeDtypeStruct((lines, columns), BF),
        compiler_params=pltpu.CompilerParams(vmem_limit_bytes=VMEM),
        name=kernel.__name__.replace("_kernel", ""),
    )(bit[None], *arrays)


def pack_bias_kernel(sbq_ref, sbv_ref, cbq_ref, cbv_ref, b1_ref, out_ref):
    columns = out_ref.shape[1]
    out_ref[...] = jnp.zeros_like(out_ref)
    size = sbq_ref.shape[1]
    out_ref[0:1, :size], out_ref[0:1, size : 2 * size] = sbq_ref[...], sbv_ref[...]
    out_ref[1:2, :size], out_ref[1:2, size : 2 * size] = cbq_ref[...], cbv_ref[...]
    for line, at in enumerate(range(0, b1_ref.shape[1], columns)):
        part = b1_ref[:, at : min(at + columns, b1_ref.shape[1])]
        out_ref[2 + line : 3 + line, : part.shape[1]] = part


def pack_bias(biases, columns):
    lines = -(-(2 + -(-biases[-1].shape[1] // columns)) // 8) * 8
    return pl.pallas_call(pack_bias_kernel, out_shape=jax.ShapeDtypeStruct((lines, columns), F32), name="pack_bias")(*biases)


def feed_unpack_kernel(hidden_half, columns, sums_ref, w1_ref, w2_ref, wo_ref, b1_ref, *vec_refs):
    w1_ref[...] = sums_ref[:hidden_half, :].astype(F32)
    w2_ref[...] = sums_ref[hidden_half : 2 * hidden_half, :].astype(F32)
    wo_ref[...] = sums_ref[2 * hidden_half : 2 * hidden_half + columns, :].astype(F32)
    vectors = sums_ref[2 * hidden_half + columns :, :].astype(F32)
    for line, one in enumerate(vec_refs):
        one[...] = vectors[line : line + 1]
    lines = -(-hidden_half // vectors.shape[1])
    b1_ref[...] = jnp.concatenate([vectors[8 + one : 9 + one] for one in range(lines)], axis=1)[:, :hidden_half]


def feed_unpack(sums, hidden_half, columns):
    feature = sums.shape[1]
    shapes = [(hidden_half, feature), (hidden_half, feature), (columns, feature), (1, hidden_half)] + [(1, feature)] * 6
    return pl.pallas_call(
        functools.partial(feed_unpack_kernel, hidden_half, columns),
        out_shape=[jax.ShapeDtypeStruct(one, F32) for one in shapes],
        compiler_params=pltpu.CompilerParams(vmem_limit_bytes=VMEM),
        name="feed_unpack",
    )(sums)


def token_unpack_kernel(
    place_ref, kept_ref, other_ref, wq_ref, wk_ref, wv_ref, cwq_ref, cwk_ref, cwv_ref, wo_ref, embed_ref,
    gain_ref, shift_ref, so_ref, cq_ref, sq_ref, sv_ref, cv_ref, sums, vectors,
):
    half = kept_ref.shape[0]
    sums[pl.ds(pl.multiple_of(place_ref[1] * half, half), half), :] = kept_ref[...]
    sums[pl.ds(pl.multiple_of((1 - place_ref[1]) * half, half), half), :] = other_ref[...]
    feature, columns = wq_ref.shape
    for at, (one, two) in enumerate(((wq_ref, wk_ref), (wv_ref, cwq_ref), (cwk_ref, cwv_ref))):
        one[...] = sums[at * feature : (at + 1) * feature, :columns].astype(F32)
        two[...] = sums[at * feature : (at + 1) * feature, columns:].astype(F32)
    wo_ref[...] = sums[3 * feature : 3 * feature + columns, :].astype(F32)
    at = 3 * feature + columns
    embed_ref[...] = sums[at : at + LANES, :].astype(F32)[:SPAN]
    vectors[...] = sums[at + LANES : at + LANES + 16, :].astype(F32)
    gain_ref[...], shift_ref[...], so_ref[...] = vectors[0:1, :], vectors[1:2, :], vectors[2:3, :]
    own = pl.ds(pl.multiple_of(place_ref[0] * columns, columns), columns)
    cq_ref[...], sq_ref[...], sv_ref[...] = vectors[3:4, own], vectors[4:5, own], vectors[5:6, own]
    cv_ref[...] = vectors[8:9, :columns]


def token_unpack(place, kept, other, feature, columns):
    half, width = kept.shape
    shapes = [(feature, columns)] * 6 + [(columns, feature), (SPAN, feature)] + [(1, feature)] * 3 + [(1, columns)] * 4
    whole = lambda shape: pl.BlockSpec(shape, lambda *_: (0, 0))
    return pl.pallas_call(
        token_unpack_kernel,
        grid_spec=pltpu.PrefetchScalarGridSpec(
            num_scalar_prefetch=1, grid=(1,),
            in_specs=[whole((half, width))] * 2,
            out_specs=[whole(one) for one in shapes],
            scratch_shapes=[pltpu.VMEM((2 * half, width), BF), pltpu.VMEM((16, width), F32)],
        ),
        out_shape=[jax.ShapeDtypeStruct(one, F32) for one in shapes],
        compiler_params=pltpu.CompilerParams(vmem_limit_bytes=VMEM),
        name="token_unpack",
    )(place, kept, other)


def after(value, *others):
    return lax.optimization_barrier((value, *others))[0]


class SumOverDp:
    def __init__(self, at, count):
        self.at, self.count = at, count
        hops = [1 << one for one in range(1, count.bit_length() - 1)]
        self.hops = list(zip(hops, hops[1:] + hops[:1]))

    def swap(self, array, by):
        return lax.ppermute(array, "dp", [(one, one ^ by) for one in range(self.count)])

    def bit(self, by):
        return (self.at // by) % 2

    def give(self, array, by):
        half = array.shape[0] // 2
        bit = self.bit(by)
        return lax.dynamic_slice_in_dim(array, (1 - bit) * half, half), lax.dynamic_slice_in_dim(array, bit * half, half)

    def add(self, kept, got):
        return (kept.astype(F32) + got.astype(F32)).astype(BF)

    def join(self, array, got, by):
        first = self.bit(by) == 0
        return jnp.concatenate([jnp.where(first, array, got), jnp.where(first, got, array)])

    def exchange(self, sent, bys, work):
        got = [self.swap(one, by) for one, by in zip(sent, bys)]
        done = work(sent)
        return got if done is None else list(lax.optimization_barrier((*got, done)))[: len(got)]

    def start(self, sent, kept, work):
        held = self.add(kept, self.swap(sent, 1))
        middle = held.shape[0] // 2
        two = [held[:middle], held[middle:]]
        for bys in self.hops:
            given = [self.give(one, by) for one, by in zip(two, bys)]
            got = self.exchange([one for one, _ in given], bys, work)
            two = [self.add(one, other) for (_, one), other in zip(given, got)]
        for bys in self.hops[:0:-1]:
            got = self.exchange(two, bys, work)
            two = [self.join(one, other, by) for one, other, by in zip(two, got, bys)]
        return tuple(two)

    def finish(self, two, work):
        bys = self.hops[0]
        got = self.exchange(two, bys, work)
        mine = jnp.concatenate([self.join(one, other, by) for one, other, by in zip(two, got, bys)])
        return mine, self.swap(mine, 1)


def solution(mesh):
    tensor, count = mesh.shape["tensor"], mesh.shape["dp"]

    def body(
        tokens, memory, mem_lengths, key_pad, query_embed,
        self_wq, self_bq, self_wk, self_wv, self_bv, self_wo, self_bo, norm1_gain, norm1_bias,
        cross_wq, cross_bq, cross_wk, cross_wv, cross_bv, cross_wo, cross_bo, norm2_gain, norm2_bias,
        ffn_w1, ffn_b1, ffn_w2, ffn_b2, norm3_gain, norm3_bias, cotangent,
    ):
        rank, at = lax.axis_index("tensor"), lax.axis_index("dp")
        side = (rank * 2 // tensor).astype(jnp.int32)
        bit = (at % 2).astype(jnp.int32)
        place = jnp.stack([side, bit])
        own_columns, own_hidden = self_wq.shape[1], ffn_w1.shape[1]
        feature = tokens.shape[1]
        columns, hidden_half = own_columns * tensor // 2, own_hidden * tensor // 2
        rows = mem_lengths.shape[0]
        direct = tensor == 2 and count > 1
        as_row = lambda one: one.reshape(1, -1)

        def two_halves(part, dim):
            if direct:
                return part, part
            full = lax.all_gather(part, "tensor", axis=dim, tiled=True)
            size = full.shape[dim] // 2
            cut = lambda which: lax.dynamic_slice_in_dim(full, which * size, size, axis=dim)
            return cut(side), cut(1 - side)

        def crossing(kernel, others, lines, sent, then):
            crossed = lax.ppermute(sent, "tensor", [(0, 1), (1, 0)]) if direct else sent
            return passing_on(kernel, others, lines, crossed, then)

        def passing_on(kernel, others, lines, crossed, then):
            if not direct:
                return crossed, pack_half(kernel, 1 - bit, others, lines, feature)
            return crossed, lax.ppermute(after(crossed, then), "dp", [(one, one ^ 1) for one in range(count)])

        cwk, cwv = two_halves(cross_wk, 1), two_halves(cross_wv, 1)
        swq, swk, swv, cwq = (two_halves(one, 1) for one in (self_wq, self_wk, self_wv, cross_wq))
        swo, cwo = two_halves(self_wo, 0), two_halves(cross_wo, 0)
        w1, w2 = two_halves(jnp.transpose(ffn_w1), 0), two_halves(ffn_w2, 0)
        biases = [two_halves(one, 0) for one in (self_bq, self_bv, cross_bq, cross_bv, ffn_b1)]
        memory_others = [cwk[1], cwv[1], as_row(biases[3][1])]
        memory_sent = pack_half(pack_columns_kernel, bit, memory_others, feature // 2 + BIAS_LINES, feature)
        bias_own = pack_bias([after(as_row(biases[0][0]), memory_sent)] + [as_row(own) for own, _ in biases[1:]], feature)
        if direct:
            bias_other = lax.ppermute(bias_own, "tensor", [(0, 1), (1, 0)])
        else:
            bias_other = pack_bias([as_row(other) for _, other in biases], feature)
        token_sent = pack_half(
            pack_token_kernel, bit, [after(swq[1], bias_own)] + [one[1] for one in (swk, swv, cwq, swo, cwo)], feature + columns, feature
        )
        feed_sent = pack_half(pack_lines_kernel, bit, [after(w1[1], token_sent), w2[1]], hidden_half, feature)
        memory_part, memory_rest = crossing(pack_columns_kernel, memory_others, feature // 2 + BIAS_LINES, memory_sent, feed_sent)
        token_sent = after(token_sent, memory_part, bias_other, feed_sent)
        token_crossed = lax.ppermute(token_sent, "tensor", [(0, 1), (1, 0)]) if direct else token_sent
        operands = cwk[0], cwv[0], memory_part, memory_rest, as_row(biases[3][0])
        blocks = memory.shape[0] // BLOCK
        early = blocks * 3 // 4
        outputs = keys_values(mem_lengths, place, memory, key_pad, *operands, 0, early, None)
        feed_sent = after(feed_sent, outputs[1], token_crossed)
        token_part, token_rest = passing_on(
            pack_token_kernel, [one[1] for one in (swq, swk, swv, cwq, swo, cwo)], feature + columns, token_crossed, outputs[1]
        )
        outputs = keys_values(mem_lengths, place, after(memory, feed_sent, token_part), key_pad, *operands, early, blocks - early, outputs)
        memory_in, gate, cross_keys, cross_values, cwk_full, cwv_full = outputs
        token_weights = [one[0] for one in (swq, swk, swv, cwq, swo)]
        q, k, v, self_mix, resid_one, normed_one, qt = token_forward(
            place, tokens, query_embed, token_weights, token_part, token_rest, bias_own, bias_other,
            as_row(self_bo), as_row(norm1_gain), as_row(norm1_bias), 1,
        )
        mix, mixt, lse = cross_forward(mem_lengths, cross_keys, cross_values, gate, qt)
        feed_part, feed_rest = crossing(pack_lines_kernel, [w1[1], w2[1]], hidden_half, feed_sent, lse)
        layer_out, grad_two, gt, feed_sums = feed(
            place, mix, normed_one, cotangent, [cwo[0], w1[0], w2[0]], [token_part, token_rest, feed_part, feed_rest],
            bias_own, bias_other,
            [as_row(one) for one in (cross_bo, norm2_gain, norm2_bias, ffn_b2, norm3_gain, norm3_bias)], rows, columns,
        )
        multiple = 32 * count
        lines = -(-(3 * feature + columns + LANES + 16) // multiple) * multiple

        def backward():
            dk, dv, dq = cross_backward(mem_lengths, cross_keys, cross_values, gate, qt, gt, mixt, lse)
            memory_sums, memory_vec = memory_weights(place, dk, dv, memory, memory_in, columns)
            grad_tokens, sent, kept = token_backward(
                place, dq, grad_two, resid_one, normed_one, tokens, query_embed, q, k, v, self_mix, memory_sums, memory_vec,
                token_weights, token_part, token_rest, as_row(norm1_gain), rows, columns, lines,
            )
            blocks, given = memory.shape[0] // BLOCK, []

            def piece(sent, share=None):
                step, first = len(given), sum(SHARES[: len(given)])
                share = min(SHARES[step] if share is None and step < len(SHARES) else blocks, blocks - first)
                if share <= 0:
                    return None
                held = given[-1] if given else None
                given.append(memory_gradient(after(dk, *sent), dv, cwk_full, cwv_full, first, share, held))
                return given[-1]

            state = token_sum.start(sent, kept, piece) if summed else (sent, kept)
            piece([], blocks)
            return grad_tokens, given[-1], *state

        summed = count > 2
        token_sum = SumOverDp(at, count)
        feed_total = lax.psum(feed_sums, "dp")
        shapes = jax.eval_shape(backward)
        grad_tokens, grad_memory, *state = lax.cond(
            at < count * rows, backward, lambda: tuple(jnp.zeros(one.shape, one.dtype) for one in shapes)
        )
        feed_grads = []

        def unpack_feed(sent):
            feed_grads.extend(feed_unpack(after(feed_total, *sent), hidden_half, columns))
            return feed_grads[0]

        if summed:
            kept, other = token_sum.finish(state, unpack_feed)
        else:
            other, kept = state
            unpack_feed([])
        g_sq, g_sk, g_sv, g_cq, g_ck, g_cv, g_so, g_embed, g_n1g, g_n1b, g_sbo, g_cbq, g_sbq, g_sbv, g_cbv = token_unpack(
            place, kept, other, feature, columns
        )
        g_w1t, g_w2, g_co, g_b1, g_n3g, g_n3b, g_b2, g_n2g, g_n2b, g_cbo = feed_grads

        def share(array, dim, size):
            if array.shape[dim] == size:
                return array
            return lax.dynamic_slice_in_dim(array, rank % (tensor // 2) * size, size, axis=dim)

        lanes = lambda array: share(array, 1, own_columns)
        bias = lambda array: share(array, 1, own_columns).reshape(-1)
        vector = lambda array: array.reshape(-1)
        return (
            layer_out, grad_tokens, grad_memory, g_embed,
            lanes(g_sq), bias(g_sbq), lanes(g_sk), lanes(g_sv), bias(g_sbv), share(g_so, 0, own_columns),
            vector(g_sbo), vector(g_n1g), vector(g_n1b),
            lanes(g_cq), bias(g_cbq), lanes(g_ck), lanes(g_cv), bias(g_cbv), share(g_co, 0, own_columns),
            vector(g_cbo), vector(g_n2g), vector(g_n2b),
            jnp.transpose(share(g_w1t, 0, own_hidden)), share(g_b1, 1, own_hidden).reshape(-1), share(g_w2, 0, own_hidden),
            vector(g_b2), vector(g_n3g), vector(g_n3b),
        )

    rep, by_row, by_col, by_first = P(), P("dp", None), P(None, "tensor"), P("tensor", None)
    one_dim = P("tensor")
    return jax.shard_map(
        body,
        mesh=mesh,
        in_specs=(
            by_row, by_row, by_row, by_row, rep,
            by_col, one_dim, by_col, by_col, one_dim, by_first, rep, rep, rep,
            by_col, one_dim, by_col, by_col, one_dim, by_first, rep, rep, rep,
            by_col, one_dim, by_first, rep, rep, rep, by_row,
        ),
        out_specs=(
            by_row, by_row, by_row, rep,
            by_col, one_dim, by_col, by_col, one_dim, by_first, rep, rep, rep,
            by_col, one_dim, by_col, by_col, one_dim, by_first, rep, rep, rep,
            by_col, one_dim, by_first, rep, rep, rep,
        ),
        check_vma=False,
    )
```
